32 devices in a mesh: groups: 2 (over y), shard: 4 (over z), section: 2 (over x), halo: 2 (over core).
Axes of the slice: x: 2, y: 2, z: 4, core: 2. Of those that a mesh axis runs over, the one named last changes fastest.
Arguments:
- features: bfloat16 [4, 4, 16, 64, 320], P(('groups', 'section'), 'shard', 'halo'), parts along dimension 0, may hold values from -6 to 6
- timesteps: int32 [4, 2], P(('groups', 'section')), parts along dimension 0, may hold values from 0 to 999
- conv_first: bfloat16 [2, 3, 3, 320, 320], P('section'), may hold values from -0.109375 to 0.109375
- conv_second: bfloat16 [2, 3, 3, 320, 320], P('section'), may hold values from -0.109375 to 0.109375
- time_weight: bfloat16 [2, 320, 320], P('section'), may hold values from -0.3125 to 0.3125
- qkv_weight: bfloat16 [2, 320, 960], P('section'), may hold values from -7 to 7
- attn_out: bfloat16 [2, 320, 320], P('section'), may hold values from -0.3125 to 0.3125
- geglu_in: bfloat16 [2, 320, 2560], P('section'), may hold values from -0.3125 to 0.3125
- geglu_out: bfloat16 [2, 1280, 320], P('section'), may hold values from -0.15625 to 0.15625
Outputs:
- result: bfloat16 [4, 4, 16, 64, 320], P(('groups', 'section'), 'shard', 'halo'), parts along dimension 0
The draws below stay inside these ranges and needn't reach their ends.
There are 2 independent parts, one for each index of `groups`. The reference program is written for one: setup_inputs(seed, part) draws one part's arguments, and reference() takes and returns one part's arrays. A program takes and returns all parts, laid end to end along the dimension named above; an argument that names none is the same for every part. Nothing has to cross between parts.
All inputs are finite; a program needn't handle non-finite values.
Results may differ from the reference program's by a relative error of at most 0.02.
Values may be sent and summed in bfloat16 or wider, within the bound.
No kernel may reach another device: no remote copies, remote signals or barrier semaphores. Data moves between devices by JAX's collectives and lax.ppermute only.
A program may use at most 64 MiB of HBM per device.

```python
import math
import jax
import jax.numpy as jnp
from jax import lax

C = 320
HEAD_DIM = 64
FF = 1280
GROUPS = 32
WIDTH = 64
STEPS = 2
SECTIONS = 2
FRAMES = 4
HEIGHT = 16


def draw_qkv_weight(key, part):
    first_key, second_key, third_key = jax.random.split(jax.random.fold_in(key, 7), 3)
    scaling = C ** (-0.5)
    key_weight = jax.random.truncated_normal(second_key, -4.0, 4.0, (SECTIONS, C, C), jnp.float32) * scaling
    value_weight = jax.random.truncated_normal(third_key, -4.0, 4.0, (SECTIONS, C, C), jnp.float32) * scaling
    noise_weight = jax.random.truncated_normal(first_key, -4.0, 4.0, (SECTIONS, C, C), jnp.float32) * scaling
    query_weight = noise_weight
    return jnp.concatenate([query_weight, key_weight, value_weight], axis=2).astype(jnp.bfloat16)


def set_ends(drawn, own_key, low, largest):
    extent = drawn.shape
    spot = [jax.random.randint(jax.random.fold_in(own_key, axis), (), 0, extent[axis]) for axis in range(len(extent))]
    drawn = drawn.at[tuple(spot)].set(low)
    longest = extent.index(max(extent))
    spot[longest] = (spot[longest] + 1) % extent[longest]
    return drawn.at[tuple(spot)].set(largest)


def level_of(stream_key, dims, cuts, low, top_value):
    def one(axis_at, parts):
        steps = jax.random.uniform(jax.random.fold_in(jax.random.fold_in(stream_key, 6), axis_at), (parts,), jnp.float32, low / len(cuts), top_value / len(cuts))
        return jnp.repeat(jnp.exp(steps), dims[axis_at] // parts).reshape((-1,) + (1,) * (len(dims) - axis_at - 1))

    loudness = one(*cuts[0])
    for cut in cuts[1:]:
        loudness = loudness * one(*cut)
    return loudness


def gaussian(own_key, shape, scale, bound, pieces=(), kind=jnp.bfloat16):
    factor_of = level_of(own_key, shape, pieces, -0.22, 0.18) if pieces else 1.0
    result = jax.random.normal(own_key, shape, jnp.float32) * scale * factor_of
    return jnp.minimum(jnp.maximum(result, -bound), bound).astype(kind)


def setup_inputs(seed: int = 0, part: int = 0) -> dict:
    splits = jax.random.split(jax.random.key(seed), 10)
    part_keys = jax.random.split(jax.random.fold_in(splits[9], part), 10)
    return {
        "features": gaussian(part_keys[0], (SECTIONS, FRAMES, HEIGHT, WIDTH, C), 1.0, 6.0, ((0, 2), (1, 4), (2, 2))),
        "timesteps": set_ends(jax.random.randint(part_keys[1], (SECTIONS, STEPS), 0, 1000), jax.random.fold_in(part_keys[1], 1), 0, 999).astype(jnp.int32),
        "conv_first": gaussian(splits[2], (SECTIONS, 3, 3, C, C), (9 * C) ** -0.5, 0.109375, ((0, 2),)),
        "conv_second": gaussian(splits[3], (SECTIONS, 3, 3, C, C), (9 * C) ** -0.5, 0.109375, ((0, 2),)),
        "time_weight": gaussian(splits[4], (SECTIONS, C, C), C ** -0.5, 0.3125, ((0, 2),)),
        "qkv_weight": draw_qkv_weight(jax.random.fold_in(splits[9], 71), part),
        "attn_out": gaussian(splits[6], (SECTIONS, C, C), C ** -0.5, 0.3125, ((0, 2),)),
        "geglu_in": gaussian(splits[7], (SECTIONS, C, 2 * FF), C ** -0.5, 0.3125, ((0, 2),)),
        "geglu_out": gaussian(splits[8], (SECTIONS, FF, C), FF ** -0.5, 0.15625, ((0, 2),)),
    }


def norm_silu(field):
    frames, height, column_count, channels = field.shape
    grouped = field.reshape(frames, height * column_count, GROUPS, channels // GROUPS)
    average = lax.optimization_barrier(jnp.mean(grouped, axis=(1, 3), keepdims=True))
    squares = lax.optimization_barrier(jnp.mean(grouped * grouped, axis=(1, 3), keepdims=True))
    normed = (grouped - average) * lax.rsqrt(squares - average * average + 1e-05)
    return jax.nn.silu(normed).reshape(field.shape).astype(jnp.bfloat16)

def conv_frames(active, kernel):
    frames, height, column_count, channels = active.shape
    padded = jnp.pad(active, ((0, 0), (1, 1), (1, 1), (0, 0)))
    outcome = jnp.zeros((frames * height * column_count, kernel.shape[3]), jnp.float32)
    for row_offset in range(3):
        for column_offset in range(3):
            window = padded[:, row_offset:row_offset + height, column_offset:column_offset + column_count, :]
            outcome = outcome + jnp.dot(window.reshape(-1, channels), kernel[row_offset, column_offset], preferred_element_type=jnp.float32)
    return outcome.reshape(frames, height, column_count, kernel.shape[3])

def embed_time(stamp, time_weight):
    half_width = time_weight.shape[0] // 2
    frequency = jnp.exp(-math.log(10000.0) * jnp.arange(half_width, dtype=jnp.float32) / half_width)
    angles = stamp.astype(jnp.float32) * frequency
    sinusoid = jnp.concatenate([jnp.cos(angles), jnp.sin(angles)])
    return jnp.dot(jax.nn.silu(sinusoid).astype(jnp.bfloat16)[None, :], time_weight, preferred_element_type=jnp.float32)[0]

def layer_norm(stream):
    values_f = stream.astype(jnp.float32)
    average = lax.optimization_barrier(jnp.mean(values_f, axis=-1, keepdims=True))
    centred = values_f - average
    spread = lax.optimization_barrier(jnp.mean(centred * centred, axis=-1, keepdims=True))
    return (centred * lax.rsqrt(spread + 1e-05)).astype(jnp.bfloat16)

def attend(query, key_block, value_block):
    query_frames, pixels, channels = query.shape
    head_count = channels // HEAD_DIM

    def split_heads(tensor):
        return tensor.reshape(tensor.shape[0], tensor.shape[1], head_count, HEAD_DIM).astype(jnp.float32)
    scores = jnp.einsum('fphd,gphd->phfg', split_heads(query), split_heads(key_block)) * HEAD_DIM ** (-0.5)
    weights = jax.nn.softmax(scores, axis=-1).astype(jnp.bfloat16)
    mixed = jnp.einsum('phfg,gphd->fphd', weights.astype(jnp.float32), split_heads(value_block))
    return mixed.reshape(query_frames, pixels, channels).astype(jnp.bfloat16)

def temporal(stream, qkv_weight, attn_out):
    frames, pixels, channels = stream.shape
    normed = layer_norm(stream).reshape(-1, channels)
    projected = jnp.dot(normed, qkv_weight, preferred_element_type=jnp.float32).astype(jnp.bfloat16)
    projected = projected.reshape(frames, pixels, 3 * channels)
    mixed = attend(projected[:, :, :channels], projected[:, :, channels:2 * channels], projected[:, :, 2 * channels:])
    update = jnp.dot(mixed.reshape(-1, channels), attn_out, preferred_element_type=jnp.float32).reshape(stream.shape)
    return (stream.astype(jnp.float32) + update).astype(jnp.bfloat16)

def feed(stream, geglu_in, geglu_out):
    channels = stream.shape[2]
    inner = geglu_out.shape[0]
    normed = layer_norm(stream).reshape(-1, channels)
    projected = jnp.dot(normed, geglu_in, preferred_element_type=jnp.float32)
    active = (projected[:, :inner] * jax.nn.gelu(projected[:, inner:], approximate=False)).astype(jnp.bfloat16)
    update = jnp.dot(active, geglu_out, preferred_element_type=jnp.float32).reshape(stream.shape)
    return (stream.astype(jnp.float32) + update).astype(jnp.bfloat16)

def section_block(field, stamp, conv_first, conv_second, time_weight, qkv_weight, attn_out, geglu_in, geglu_out):
    frames, height, column_count, channels = field.shape
    base = field.astype(jnp.float32)
    first = conv_frames(norm_silu(base), conv_first) + embed_time(stamp, time_weight)
    second = conv_frames(norm_silu(first), conv_second)
    stream = (base + second).astype(jnp.bfloat16).reshape(frames, height * column_count, channels)
    stream = temporal(stream, qkv_weight, attn_out)
    stream = feed(stream, geglu_in, geglu_out)
    return stream.reshape(field.shape)

def reference(features, timesteps, conv_first, conv_second, time_weight, qkv_weight, attn_out, geglu_in, geglu_out):
    current = features
    for denoise_step in range(STEPS):
        current = jnp.roll(current, 1, axis=0)
        outputs = []
        for section in range(SECTIONS):
            outputs.append(section_block(current[section], timesteps[section, denoise_step], conv_first[section], conv_second[section], time_weight[section], qkv_weight[section], attn_out[section], geglu_in[section], geglu_out[section]))
        current = jnp.stack(outputs)
    return current
```

```python
import functools
import math

import jax
import jax.numpy as jnp
from jax import lax
from jax.experimental import pallas as pl
from jax.experimental.pallas import tpu as pltpu
from jax.sharding import PartitionSpec as P

HEAD_DIM = 64
GROUPS = 32
STEPS = 2
LANES = 128
WIDE = 256
F32 = jnp.float32
BF16 = jnp.bfloat16


def round_up(value, unit):
    return -(-value // unit) * unit


def group_scale(total, square, entries, group_width, channels):
    lanes = total.shape[1]
    left = lax.broadcasted_iota(jnp.int32, (lanes, lanes), 0)
    right = lax.broadcasted_iota(jnp.int32, (lanes, lanes), 1)
    group = [
        sum((side >= g * group_width).astype(jnp.int32) for g in range(1, channels // group_width))
        for side in (left[:, :1], right[:1, :])
    ]
    same = (group[0] == group[1]) & (left < channels) & (right < channels)
    both = jnp.concatenate([total, square, jnp.zeros((6, lanes), F32)], axis=0)
    summed = jnp.dot(
        both, same.astype(F32), preferred_element_type=F32, precision=lax.Precision.HIGHEST
    ) / entries
    average = summed[0:1]
    scale = lax.rsqrt(summed[1:2] - average * average + 1e-05)
    inside = lax.broadcasted_iota(jnp.int32, (1, lanes), 1) < channels
    scale = jnp.where(inside, scale, 0.0)
    return scale, -average * scale


def spatial_kernel(rows, half, columns, channels, group_width, step, pieces, shards, *refs):
    own_refs, other_refs = refs[:pieces], refs[pieces : 2 * pieces]
    weights = refs[2 * pieces : 2 * pieces + 4]
    embeds = refs[2 * pieces + 4]
    outs = refs[2 * pieces + 5 : 2 * pieces + 5 + shards]
    field, active, hidden, tails, main1, tail1, main2, tail2, arrived_sems = refs[
        2 * pieces + 5 + shards :
    ]
    loads = [
        pltpu.make_async_copy(source, target, arrived_sems.at[i])
        for i, (source, target) in enumerate(zip(weights, (main1, tail1, main2, tail2)))
    ]
    for load in loads:
        load.start()
    embed = embeds[step : step + 1, :]
    lanes = field.shape[1]
    own_rows = rows // half
    part = own_rows * columns // shards
    size = own_rows * columns // pieces
    here = lax.axis_index("halo")
    spot = lax.axis_index("shard")
    own_base = here * (own_rows * columns)
    other_base = (1 - here) * (own_rows * columns)

    field[:, lanes - LANES :] = jnp.zeros((rows * columns, LANES), F32)
    for base, arrived in ((own_base, own_refs), (other_base, other_refs)):
        for d in range(pieces):
            place = pl.multiple_of(base + lax.rem(spot + d, pieces) * size, size)
            field[pl.ds(place, size), :channels] = arrived[d][...].astype(F32)

    column = lax.broadcasted_iota(jnp.int32, (columns, 1), 0)

    def sums(source):
        def body(i, carry):
            total, square = carry
            chunk = source[pl.ds(pl.multiple_of(i * columns, columns), columns), :]
            chunk = chunk.reshape(columns // 8, 8, lanes)
            return total + jnp.sum(chunk, axis=0), square + jnp.sum(chunk * chunk, axis=0)

        zero = jnp.zeros((8, lanes), F32)
        total, square = lax.fori_loop(0, rows, body, (zero, zero))
        return jnp.sum(total, axis=0, keepdims=True), jnp.sum(square, axis=0, keepdims=True)

    def activate(source, scale, shift, first, count):
        def body(i, _):
            row = first - 1 + i
            inside = (row >= 0) & (row < rows)
            at = pl.multiple_of(jnp.clip(row, 0, rows - 1) * columns, columns)
            u = source[pl.ds(at, columns), :] * scale + shift
            g = u * (0.5 + 0.5 * jnp.tanh(0.5 * u))
            g = g * inside.astype(F32)
            before = jnp.where(column == 0, 0.0, pltpu.roll(g, 1, 0))
            after = jnp.where(column == columns - 1, 0.0, pltpu.roll(g, columns - 1, 0))
            to = pl.ds(pl.multiple_of(i * columns, columns), columns)
            active[to, 0:WIDE] = before[:, :WIDE].astype(BF16)
            active[to, WIDE : 2 * WIDE] = g[:, :WIDE].astype(BF16)
            active[to, 2 * WIDE : 3 * WIDE] = after[:, :WIDE].astype(BF16)
            mixed = before[:, WIDE:] + pltpu.roll(g[:, WIDE:], LANES // 2, 1)
            active[to, 3 * WIDE : 3 * WIDE + LANES] = mixed.astype(BF16)
            active[to, 3 * WIDE + LANES :] = after[:, WIDE:].astype(BF16)
            return 0

        lax.fori_loop(0, count + 2, body, 0)

    def convolve(main, tail, count):
        tokens = count * columns
        tails[0 : tokens + 2 * columns, :] = jnp.dot(
            active[0 : tokens + 2 * columns, :], tail[...], preferred_element_type=F32
        )
        wide = sum(
            jnp.dot(
                active[r * columns : r * columns + tokens, :], main[r], preferred_element_type=F32
            )
            for r in range(3)
        )
        narrow = (
            tails[0:tokens, :LANES]
            + pltpu.roll(tails[columns : columns + tokens, :LANES], LANES // 2, 1)
            + tails[2 * columns : 2 * columns + tokens, LANES:]
        )
        return wide, narrow

    entries = float(rows * columns * group_width)
    low = lax.broadcasted_iota(jnp.int32, (1, LANES), 1) < channels - WIDE
    activate(field, *group_scale(*sums(field), entries, group_width, channels), 0, rows)
    loads[0].wait()
    loads[1].wait()
    wide, narrow = convolve(main1, tail1, rows)
    hidden[:, :WIDE] = wide + embed[:, :WIDE]
    hidden[:, WIDE:] = jnp.where(low, narrow + embed[:, WIDE:], 0.0)
    activate(
        hidden,
        *group_scale(*sums(hidden), entries, group_width, channels),
        here * own_rows,
        own_rows,
    )
    loads[2].wait()
    loads[3].wait()
    wide, narrow = convolve(main2, tail2, own_rows)
    mine = pl.ds(pl.multiple_of(own_base, columns), own_rows * columns)
    hidden[mine, :WIDE] = wide + field[mine, :WIDE]
    hidden[mine, WIDE:] = narrow + field[mine, WIDE:]
    for d in range(shards):
        place = pl.multiple_of(own_base + lax.rem(spot + d, shards) * part, part)
        outs[d][...] = hidden[pl.ds(place, part), :channels].astype(BF16)


def spatial(own, other, weights, embeds, step, rows, columns, half, shards):
    pieces = len(own)
    channels = own[0].shape[1]
    lanes = round_up(channels, LANES)
    tokens = rows * columns
    depth = weights[0].shape[1]
    kernel = functools.partial(
        spatial_kernel, rows, half, columns, channels, channels // GROUPS, step, pieces, shards
    )
    flops = 2 * tokens * depth * 4 * WIDE * 3 // 2
    vmem = pl.BlockSpec(memory_space=pltpu.VMEM)
    hbm = pl.BlockSpec(memory_space=pltpu.HBM)
    return pl.pallas_call(
        kernel,
        out_shape=[jax.ShapeDtypeStruct((tokens // half // shards, channels), BF16)] * shards,
        in_specs=[vmem] * (2 * pieces) + [hbm] * 4 + [vmem],
        out_specs=[vmem] * shards,
        scratch_shapes=[
            pltpu.VMEM((tokens, lanes), F32),
            pltpu.VMEM((tokens + 2 * columns, depth), BF16),
            pltpu.VMEM((tokens, lanes), F32),
            pltpu.VMEM((tokens + 2 * columns, WIDE), F32),
            *[pltpu.VMEM(w.shape, BF16) for w in weights],
            pltpu.SemaphoreType.DMA((4,)),
        ],
        compiler_params=pltpu.CompilerParams(vmem_limit_bytes=40 * 1024 * 1024),
        cost_estimate=pl.CostEstimate(
            flops=flops, bytes_accessed=6000000, transcendentals=tokens * lanes
        ),
        name="spatial",
    )(*own, *other, *weights, embeds)


def prepare_kernel(channels, kernel1, kernel2, qkv, main1, tail1, main2, tail2, padded):
    spare = channels - WIDE
    depth = main1.shape[1]
    for kernel, main, tail in ((kernel1, main1, tail1), (kernel2, main2, tail2)):
        main[:, 3 * channels :, :] = jnp.zeros((3, depth - 3 * channels, WIDE), BF16)
        tail[3 * channels :, :] = jnp.zeros((depth - 3 * channels, WIDE), BF16)
        for s in range(3):
            for source, target in (
                (slice(0, WIDE), slice(s * WIDE, (s + 1) * WIDE)),
                (slice(WIDE, channels), slice(3 * WIDE + s * spare, 3 * WIDE + (s + 1) * spare)),
            ):
                for r in range(3):
                    main[r, target, :] = kernel[r, s, source, :WIDE]
                first, second, third = [kernel[r, s, source, WIDE:] for r in range(3)]
                tail[target, :LANES] = jnp.concatenate([first, second], axis=1)
                tail[target, LANES:] = jnp.concatenate([third, jnp.zeros_like(third)], axis=1)
    lanes = padded.shape[1] // 3
    padded[...] = jnp.zeros(padded.shape, BF16)
    for i in range(3):
        padded[:, i * lanes : i * lanes + channels] = qkv[:, i * channels : (i + 1) * channels]


def prepare(conv_first, conv_second, qkv):
    channels = qkv.shape[0]
    depth = round_up(3 * channels, WIDE)
    lanes = round_up(channels, LANES)
    vmem = pl.BlockSpec(memory_space=pltpu.VMEM)
    main = jax.ShapeDtypeStruct((3, depth, WIDE), BF16)
    tail = jax.ShapeDtypeStruct((depth, WIDE), BF16)
    outs = [main, tail, main, tail, jax.ShapeDtypeStruct((channels, 3 * lanes), BF16)]
    *packed, padded = pl.pallas_call(
        functools.partial(prepare_kernel, channels),
        out_shape=outs,
        in_specs=[vmem] * 3,
        out_specs=[vmem] * 5,
        compiler_params=pltpu.CompilerParams(vmem_limit_bytes=40 * 1024 * 1024),
        cost_estimate=pl.CostEstimate(flops=0, bytes_accessed=10000000, transcendentals=0),
        name="prepare",
    )(conv_first, conv_second, qkv)
    return packed, padded


def norm_rows(values):
    average = jnp.mean(values, axis=-1, keepdims=True)
    centred = values - average
    spread = jnp.mean(centred * centred, axis=-1, keepdims=True)
    return (centred * lax.rsqrt(spread + 1e-05)).astype(BF16)


def temporal_kernel(frames, heads, *refs):
    parts = refs[:frames]
    weights = refs[frames : frames + 4]
    outs = refs[frames + 4 : 2 * frames + 4]
    stream, projected, products, mixed, active = refs[2 * frames + 4 : 2 * frames + 9]
    qkv, attn_out, geglu_in, geglu_out, arrived_sems = refs[2 * frames + 9 :]
    loads = [
        pltpu.make_async_copy(source, target, arrived_sems.at[i])
        for i, (source, target) in enumerate(zip(weights, (qkv, attn_out, geglu_in, geglu_out)))
    ]
    for load in loads:
        load.start()
    pixels, channels = parts[0].shape
    lanes = projected.shape[1] // 3
    inner = geglu_out.shape[1]

    for f in range(frames):
        stream[f * pixels : (f + 1) * pixels, :] = parts[f][...]
    normed = norm_rows(stream[...].astype(F32))
    loads[0].wait()
    projected[...] = jnp.dot(normed, qkv[...], preferred_element_type=F32).astype(BF16)

    lane = lax.broadcasted_iota(jnp.int32, (2 * lanes, LANES), 0)
    head = lax.broadcasted_iota(jnp.int32, (2 * lanes, LANES), 1)
    lane = jnp.where(lane >= lanes, lane - lanes, lane)
    gather = ((lane >= head * HEAD_DIM) & (lane < (head + 1) * HEAD_DIM) & (head < heads)).astype(BF16)
    lane = lax.broadcasted_iota(jnp.int32, (LANES, lanes), 1)
    head = lax.broadcasted_iota(jnp.int32, (LANES, lanes), 0)
    spread = ((lane >= head * HEAD_DIM) & (lane < (head + 1) * HEAD_DIM) & (head < heads)).astype(BF16)

    for f in range(frames):
        query = projected[f * pixels : (f + 1) * pixels, 0:lanes].astype(F32)
        for g in range(frames):
            key = projected[g * pixels : (g + 1) * pixels, lanes : 2 * lanes].astype(F32)
            product = query * key
            high = product.astype(BF16)
            at = slice(g * pixels, (g + 1) * pixels)
            products[at, 0:lanes] = high
            products[at, lanes:] = (product - high.astype(F32)).astype(BF16)
        scores = jnp.dot(products[...], gather, preferred_element_type=F32) * HEAD_DIM ** (-0.5)
        scores = [scores[g * pixels : (g + 1) * pixels] for g in range(frames)]
        top = functools.reduce(jnp.maximum, scores)
        scores = [jnp.exp(score - top) for score in scores]
        total = 1.0 / sum(scores)
        weights = jnp.concatenate([score * total for score in scores], axis=0).astype(BF16)
        weights = jnp.dot(weights, spread, preferred_element_type=F32)
        mix = sum(
            weights[g * pixels : (g + 1) * pixels]
            * projected[g * pixels : (g + 1) * pixels, 2 * lanes :].astype(F32)
            for g in range(frames)
        )
        mixed[f * pixels : (f + 1) * pixels, :] = mix.astype(BF16)

    loads[1].wait()
    update = jnp.dot(mixed[:, :channels], attn_out[...], preferred_element_type=F32)
    stream[...] = (stream[...].astype(F32) + update).astype(BF16)
    normed = norm_rows(stream[...].astype(F32))
    loads[2].wait()
    for at in range(0, inner, WIDE):
        value = jnp.dot(normed, geglu_in[:, at : at + WIDE], preferred_element_type=F32)
        gate = jnp.dot(normed, geglu_in[:, inner + at : inner + at + WIDE], preferred_element_type=F32)
        act = value * (0.5 * gate) * (1.0 + lax.erf(gate * math.sqrt(0.5)))
        active[:, at : at + WIDE] = act.astype(BF16)
    loads[3].wait()
    update = lax.dot_general(
        active[...], geglu_out[...], (((1,), (1,)), ((), ())), preferred_element_type=F32
    )
    update = (stream[...].astype(F32) + update).astype(BF16)
    for f in range(frames):
        outs[f][...] = update[f * pixels : (f + 1) * pixels, :]


def temporal(parts, weights):
    frames = len(parts)
    pixels, channels = parts[0].shape
    lanes = round_up(channels, LANES)
    tokens = frames * pixels
    inner = weights[3].shape[1]
    vmem = pl.BlockSpec(memory_space=pltpu.VMEM)
    hbm = pl.BlockSpec(memory_space=pltpu.HBM)
    flops = 2 * tokens * channels * (3 * lanes + channels + 3 * inner)
    return pl.pallas_call(
        functools.partial(temporal_kernel, frames, channels // HEAD_DIM),
        out_shape=[jax.ShapeDtypeStruct((pixels, channels), BF16)] * frames,
        in_specs=[vmem] * frames + [hbm] * 4,
        out_specs=[vmem] * frames,
        scratch_shapes=[
            pltpu.VMEM((tokens, channels), BF16),
            pltpu.VMEM((tokens, 3 * lanes), BF16),
            pltpu.VMEM((tokens, 2 * lanes), BF16),
            pltpu.VMEM((tokens, lanes), BF16),
            pltpu.VMEM((tokens, inner), BF16),
            *[pltpu.VMEM(w.shape, BF16) for w in weights],
            pltpu.SemaphoreType.DMA((4,)),
        ],
        compiler_params=pltpu.CompilerParams(vmem_limit_bytes=40 * 1024 * 1024),
        cost_estimate=pl.CostEstimate(
            flops=flops, bytes_accessed=4000000, transcendentals=tokens * inner
        ),
        name="temporal",
    )(*parts, *weights)


def send(block, hops):
    axes = tuple(axis for axis, _ in hops)
    sizes = [lax.axis_size(axis) for axis in axes]
    route = []
    for source in range(math.prod(sizes)):
        rest, target, stride = source, 0, 1
        for size, (_, distance) in zip(reversed(sizes), reversed(hops)):
            target += (rest % size + distance) % size * stride
            rest, stride = rest // size, stride * size
        route.append((source, target))
    if all(a == b for a, b in route):
        return block
    return lax.ppermute(block, axes if len(axes) > 1 else axes[0], route)


def embed_time(stamps, time_weight):
    half_width = time_weight.shape[0] // 2
    frequency = jnp.exp(-math.log(10000.0) * jnp.arange(half_width, dtype=F32) / half_width)
    angles = stamps.astype(F32)[:, None] * frequency[None, :]
    sinusoid = jnp.concatenate([jnp.cos(angles), jnp.sin(angles)], axis=1)
    out = jnp.dot(jax.nn.silu(sinusoid).astype(BF16), time_weight, preferred_element_type=F32)
    return jnp.pad(out, ((0, 0), (0, round_up(out.shape[1], LANES) - out.shape[1])))


def per_device(
    features,
    timesteps,
    conv_first,
    conv_second,
    time_weight,
    qkv_weight,
    attn_out,
    geglu_in,
    geglu_out,
):
    _, _, own_rows, columns, channels = features.shape
    half = lax.axis_size("halo")
    rows = own_rows * half
    shards = lax.axis_size("shard")
    spot = lax.axis_index("shard")
    part = own_rows * columns // shards

    moved = send(features.reshape(own_rows * columns, channels), (("section", 1),))
    embeds = embed_time(timesteps[0], time_weight[0])
    spatial_weights, padded = prepare(conv_first[0], conv_second[0], qkv_weight[0])
    temporal_weights = (padded, attn_out[0], geglu_in[0], geglu_out[0].T)

    own, other = [moved], [send(moved, (("halo", 1),))]
    for denoise_step in range(STEPS):
        parts = spatial(
            own, other, spatial_weights, embeds, denoise_step, rows, columns, half, shards
        )
        parts = [send(parts[d], (("shard", d),)) for d in range(shards)]
        parts = temporal(parts, temporal_weights)
        if denoise_step < STEPS - 1:
            own = [send(parts[d], (("shard", -d), ("section", 1))) for d in range(shards)]
            other = [send(block, (("halo", 1),)) for block in own]
        else:
            own = [send(parts[d], (("shard", -d),)) for d in range(shards)]
    result = jnp.zeros((own_rows * columns, channels), BF16)
    for d in range(shards):
        result = lax.dynamic_update_slice_in_dim(
            result, own[d], lax.rem(spot + d, shards) * part, axis=0
        )
    return result.reshape(features.shape)


def solution(mesh):
    return jax.shard_map(
        per_device,
        mesh=mesh,
        in_specs=(
            P(("groups", "section"), "shard", "halo", None, None),
            P(("groups", "section"), None),
            P("section", None, None, None, None),
            P("section", None, None, None, None),
            P("section", None, None),
            P("section", None, None),
            P("section", None, None),
            P("section", None, None),
            P("section", None, None),
        ),
        out_specs=P(("groups", "section"), "shard", "halo", None, None),
        check_vma=False,
    )
```

```python
import functools
import math

import jax
import jax.numpy as jnp
from jax import lax
from jax.experimental import pallas as pl
from jax.experimental.pallas import tpu as pltpu
from jax.sharding import PartitionSpec as P

HEAD_DIM = 64
GROUPS = 32
STEPS = 2
LANES = 128
WIDE = 256
F32 = jnp.float32
BF16 = jnp.bfloat16


def round_up(value, unit):
    return -(-value // unit) * unit


def window_sum(values, width, direction):
    lanes = values.shape[1]
    done, result, power, size = 0, None, values, 1
    while True:
        if width & size:
            moved = power
            if done:
                moved = pltpu.roll(power, done if direction > 0 else lanes - done, 1)
            result = moved if result is None else result + moved
            done += size
        if done == width:
            return result
        power = power + pltpu.roll(power, size if direction > 0 else lanes - size, 1)
        size *= 2


def group_scale(total, square, entries, group_width, channels):
    lanes = total.shape[1]
    lane = lax.broadcasted_iota(jnp.int32, (1, lanes), 1)
    last = (lane % group_width == group_width - 1) & (lane < channels)

    def mean(sums):
        sums = window_sum(jnp.broadcast_to(jnp.sum(sums, axis=0, keepdims=True), (8, lanes)), group_width, 1)
        return window_sum(jnp.where(last, sums, 0.0), group_width, -1)[0:1] / entries

    average = mean(total)
    scale = lax.rsqrt(mean(square) - average * average + 1e-05)
    scale = jnp.where(lane < channels, 0.5 * scale, 0.0)
    return scale, -average * scale


def spatial_kernel(rows, half, columns, channels, group_width, step, pieces, shards, *refs):
    own_refs, other_refs = refs[:pieces], refs[pieces : 2 * pieces]
    sources = refs[2 * pieces : 2 * pieces + 2]
    embeds = refs[2 * pieces + 2]
    outs = refs[2 * pieces + 3 : 2 * pieces + 3 + shards]
    field, hidden, middle, edge, pair, kernel1, kernel2, arrived_sems = refs[
        2 * pieces + 3 + shards :
    ]
    loads = [
        pltpu.make_async_copy(source, target, arrived_sems.at[i])
        for i, (source, target) in enumerate(zip(sources, (kernel1, kernel2)))
    ]
    for load in loads:
        load.start()
    embed = embeds[step : step + 1, :]
    lanes = field.shape[1]
    own_rows = rows // half
    part = own_rows * columns // shards
    size = own_rows * columns // pieces
    here = lax.axis_index("halo")
    spot = lax.axis_index("shard")
    own_base = here * (own_rows * columns)
    other_base = (1 - here) * (own_rows * columns)
    zero = jnp.zeros((8, lanes), F32)

    field[:, lanes - LANES :] = jnp.zeros((rows * columns, LANES), F32)
    for base, arrived in ((own_base, own_refs), (other_base, other_refs)):
        for d in range(pieces):
            place = pl.multiple_of(base + lax.rem(spot + d, pieces) * size, size)
            field[pl.ds(place, size), :channels] = arrived[d][...].astype(F32)

    def sum_row(i, carry):
        total, square = carry
        chunk = field[pl.ds(pl.multiple_of(i * columns, columns), columns), :]
        chunk = chunk.reshape(columns // 8, 8, lanes)
        return total + jnp.sum(chunk, axis=0), square + jnp.sum(chunk * chunk, axis=0)

    field_sums = lax.fori_loop(0, rows, sum_row, (zero, zero), unroll=4)

    def activate(source, scale, shift, first, start, stop):
        def body(i, before):
            row = first - 1 + i
            inside = ((row >= 0) & (row < rows)).astype(F32)
            at = pl.multiple_of(jnp.clip(row, 0, rows - 1) * columns, columns)
            u = source[pl.ds(at, columns), :] * (scale * inside) + shift * inside
            g = u + u * jnp.tanh(u)
            to = pl.ds(pl.multiple_of(i * columns, columns), columns)
            rest = g[:, WIDE:]
            middle[to, :] = g[:, :WIDE].astype(BF16)
            edge[to, :] = rest.astype(BF16)
            pair[to, :] = (before + pltpu.roll(rest, LANES // 2, 1)).astype(BF16)
            return rest

        lax.fori_loop(start, stop, body, jnp.zeros((columns, LANES), F32), unroll=4)

    step_rows = min(WIDE, own_rows * columns)
    column = lax.broadcasted_iota(jnp.int32, (step_rows, 1), 0) % columns
    low = lax.broadcasted_iota(jnp.int32, (1, LANES), 1) < channels - WIDE

    def convolve(kernel, start):
        top, mid, bottom = [slice(start + r * columns, start + r * columns + step_rows) for r in range(3)]
        window = jnp.concatenate(
            [middle[top, :], middle[mid, :], middle[bottom, :], pair[mid, :], edge[bottom, :]], axis=1
        )
        y = jnp.dot(window, kernel[...], preferred_element_type=F32)

        def from_left(values):
            return jnp.where(column == 0, 0.0, pltpu.roll(values, 1, 0))

        def from_right(values):
            return jnp.where(column == columns - 1, 0.0, pltpu.roll(values, step_rows - 1, 0))

        wide = y[:, WIDE : 2 * WIDE] + from_left(y[:, :WIDE]) + from_right(y[:, 2 * WIDE : 3 * WIDE])
        tail = y[:, 3 * WIDE : 3 * WIDE + LANES]
        narrow = from_left(tail) + pltpu.roll(tail, LANES // 2, 1) + from_right(y[:, 3 * WIDE + LANES :])
        return wide, narrow

    entries = float(rows * columns * group_width)
    for pad in (0, (rows + 1) * columns):
        middle[pad : pad + columns, :] = jnp.zeros((columns, WIDE), BF16)
        edge[pad : pad + columns, :] = jnp.zeros((columns, LANES), BF16)
    activate(field, *group_scale(*field_sums, entries, group_width, channels), 0, 1, rows + 1)
    loads[0].wait()
    total, square = zero, zero
    for start in range(0, rows * columns, step_rows):
        wide, narrow = convolve(kernel1, start)
        chunk = jnp.concatenate(
            [wide + embed[:, :WIDE], jnp.where(low, narrow + embed[:, WIDE:], 0.0)], axis=1
        )
        hidden[start : start + step_rows, :] = chunk
        chunk = chunk.reshape(step_rows // 8, 8, lanes)
        total = total + jnp.sum(chunk, axis=0)
        square = square + jnp.sum(chunk * chunk, axis=0)
    activate(
        hidden,
        *group_scale(total, square, entries, group_width, channels),
        here * own_rows,
        0,
        own_rows + 2,
    )
    loads[1].wait()
    for start in range(0, own_rows * columns, step_rows):
        wide, narrow = convolve(kernel2, start)
        mine = pl.ds(pl.multiple_of(own_base + start, step_rows), step_rows)
        hidden[mine, :WIDE] = wide + field[mine, :WIDE]
        hidden[mine, WIDE:] = narrow + field[mine, WIDE:]
    for d in range(shards):
        place = pl.multiple_of(own_base + lax.rem(spot + d, shards) * part, part)
        outs[d][...] = hidden[pl.ds(place, part), :channels].astype(BF16)


def spatial(own, other, weights, embeds, step, rows, columns, half, shards):
    pieces = len(own)
    channels = own[0].shape[1]
    lanes = round_up(channels, LANES)
    tokens = rows * columns
    padded = tokens + 2 * columns
    depth = weights[0].shape[0]
    kernel = functools.partial(
        spatial_kernel, rows, half, columns, channels, channels // GROUPS, step, pieces, shards
    )
    vmem = pl.BlockSpec(memory_space=pltpu.VMEM)
    hbm = pl.BlockSpec(memory_space=pltpu.HBM)
    return pl.pallas_call(
        kernel,
        out_shape=[jax.ShapeDtypeStruct((tokens // half // shards, channels), BF16)] * shards,
        in_specs=[vmem] * (2 * pieces) + [hbm] * 2 + [vmem],
        out_specs=[vmem] * shards,
        scratch_shapes=[
            pltpu.VMEM((tokens, lanes), F32),
            pltpu.VMEM((tokens, lanes), F32),
            pltpu.VMEM((padded, WIDE), BF16),
            pltpu.VMEM((padded, LANES), BF16),
            pltpu.VMEM((padded, LANES), BF16),
            *[pltpu.VMEM(w.shape, BF16) for w in weights],
            pltpu.SemaphoreType.DMA((2,)),
        ],
        compiler_params=pltpu.CompilerParams(vmem_limit_bytes=40 * 1024 * 1024),
        cost_estimate=pl.CostEstimate(
            flops=3 * tokens * depth * depth,
            bytes_accessed=6000000,
            transcendentals=tokens * lanes,
        ),
        name="spatial",
    )(*own, *other, *weights, embeds)


def prepare_kernel(channels, *refs):
    sources, targets, buffers = refs[:3], refs[3:6], refs[6:12]
    arrived_sems, left_sems = refs[12:]
    loads = [
        pltpu.make_async_copy(source, buffer, arrived_sems.at[i])
        for i, (source, buffer) in enumerate(zip(sources, buffers[:3]))
    ]
    stores = [
        pltpu.make_async_copy(buffer, target, left_sems.at[i])
        for i, (buffer, target) in enumerate(zip(buffers[3:], targets))
    ]
    for load in loads:
        load.start()
    spare = channels - WIDE
    for i in range(2):
        kernel, packed = buffers[i], buffers[3 + i]
        depth = packed.shape[0]
        packed[3 * channels :, :] = jnp.zeros((depth - 3 * channels, depth), BF16)
        loads[i].wait()
        for r in range(3):
            for source, target in (
                (slice(0, WIDE), slice(r * WIDE, (r + 1) * WIDE)),
                (slice(WIDE, channels), slice(3 * WIDE + r * spare, 3 * WIDE + (r + 1) * spare)),
            ):
                for s in range(3):
                    packed[target, s * WIDE : (s + 1) * WIDE] = kernel[r, s, source, :WIDE]
                first, second, third = [kernel[r, s, source, WIDE:] for s in range(3)]
                packed[target, 3 * WIDE : 3 * WIDE + LANES] = jnp.concatenate([first, second], axis=1)
                packed[target, 3 * WIDE + LANES :] = jnp.concatenate(
                    [third, jnp.zeros_like(third)], axis=1
                )
        stores[i].start()
    qkv, padded = buffers[2], buffers[5]
    lanes = padded.shape[1] // 3
    padded[...] = jnp.zeros(padded.shape, BF16)
    loads[2].wait()
    for i in range(3):
        padded[:, i * lanes : i * lanes + channels] = qkv[:, i * channels : (i + 1) * channels]
    stores[2].start()
    for store in stores:
        store.wait()


def prepare(conv_first, conv_second, qkv):
    channels = qkv.shape[0]
    depth = round_up(3 * channels, WIDE)
    lanes = round_up(channels, LANES)
    hbm = pl.BlockSpec(memory_space=pltpu.HBM)
    sources = (conv_first, conv_second, qkv)
    shapes = [(depth, depth), (depth, depth), (channels, 3 * lanes)]
    *packed, padded = pl.pallas_call(
        functools.partial(prepare_kernel, channels),
        out_shape=[jax.ShapeDtypeStruct(shape, BF16) for shape in shapes],
        in_specs=[hbm] * 3,
        out_specs=[hbm] * 3,
        scratch_shapes=[
            *[pltpu.VMEM(source.shape, BF16) for source in sources],
            *[pltpu.VMEM(shape, BF16) for shape in shapes],
            pltpu.SemaphoreType.DMA((3,)),
            pltpu.SemaphoreType.DMA((3,)),
        ],
        compiler_params=pltpu.CompilerParams(vmem_limit_bytes=40 * 1024 * 1024),
        cost_estimate=pl.CostEstimate(flops=0, bytes_accessed=10000000, transcendentals=0),
        name="prepare",
    )(*sources)
    return packed, padded


def norm_rows(values):
    average = jnp.mean(values, axis=-1, keepdims=True)
    centred = values - average
    spread = jnp.mean(centred * centred, axis=-1, keepdims=True)
    return (centred * lax.rsqrt(spread + 1e-05)).astype(BF16)


def temporal_kernel(frames, *refs):
    parts = refs[:frames]
    weights = refs[frames : frames + 4]
    outs = refs[frames + 4 : 2 * frames + 4]
    stream, projected, mixed, active = refs[2 * frames + 4 : 2 * frames + 8]
    qkv, attn_out, geglu_in, geglu_out, arrived_sems = refs[2 * frames + 8 :]
    loads = [
        pltpu.make_async_copy(source, target, arrived_sems.at[i])
        for i, (source, target) in enumerate(zip(weights, (qkv, attn_out, geglu_in, geglu_out)))
    ]
    loads[0].start()
    pixels, channels = parts[0].shape
    lanes = projected.shape[1] // 3
    inner = geglu_out.shape[1]

    for f in range(frames):
        stream[f * pixels : (f + 1) * pixels, :] = parts[f][...]
    normed = norm_rows(stream[...].astype(F32))
    loads[0].wait()
    for load in loads[1:]:
        load.start()
    projected[...] = jnp.dot(normed, qkv[...], preferred_element_type=F32).astype(BF16)

    pack = min(pixels, WIDE // frames)
    tile = frames * pack
    same = (
        lax.broadcasted_iota(jnp.int32, (tile, tile), 0) % pack
        == lax.broadcasted_iota(jnp.int32, (tile, tile), 1) % pack
    )
    lane = lax.broadcasted_iota(jnp.int32, (1, LANES), 1)
    sharing = LANES // HEAD_DIM
    for first in range(0, pixels, pack):
        places = [slice(f * pixels + first, f * pixels + first + pack) for f in range(frames)]
        for at in range(0, channels, LANES):
            query, key, value = [
                jnp.concatenate([projected[p, i * lanes + at : i * lanes + at + LANES] for p in places])
                for i in range(3)
            ]
            mix = None
            for j in range(min(sharing, (channels - at) // HEAD_DIM)):
                chosen = (lane >= j * HEAD_DIM) & (lane < (j + 1) * HEAD_DIM)
                scores = lax.dot_general(
                    query * chosen.astype(BF16),
                    key,
                    (((1,), (1,)), ((), ())),
                    preferred_element_type=F32,
                )
                scores = jnp.where(same, scores, float(jnp.finfo(F32).min))
                top = jnp.max(scores, axis=1, keepdims=True)
                powers = jnp.exp((scores - top) * HEAD_DIM ** (-0.5))
                total = jnp.sum(powers, axis=1, keepdims=True)
                weights = (powers * (1.0 / total)).astype(BF16)
                head = jnp.dot(weights, value, preferred_element_type=F32)
                mix = head if mix is None else jnp.where(chosen, head, mix)
            mix = mix.astype(BF16)
            for f, p in enumerate(places):
                mixed[p, at : at + LANES] = mix[f * pack : (f + 1) * pack]

    loads[1].wait()
    update = jnp.dot(mixed[:, :channels], attn_out[...], preferred_element_type=F32)
    stream[...] = (stream[...].astype(F32) + update).astype(BF16)
    normed = norm_rows(stream[...].astype(F32))
    loads[2].wait()
    for at in range(0, inner, WIDE):
        value = jnp.dot(normed, geglu_in[:, at : at + WIDE], preferred_element_type=F32)
        gate = jnp.dot(normed, geglu_in[:, inner + at : inner + at + WIDE], preferred_element_type=F32)
        act = value * (0.5 * gate) * (1.0 + lax.erf(gate * math.sqrt(0.5)))
        active[:, at : at + WIDE] = act.astype(BF16)
    loads[3].wait()
    update = lax.dot_general(
        active[...], geglu_out[...], (((1,), (1,)), ((), ())), preferred_element_type=F32
    )
    update = (stream[...].astype(F32) + update).astype(BF16)
    for f in range(frames):
        outs[f][...] = update[f * pixels : (f + 1) * pixels, :]


def temporal(parts, weights):
    frames = len(parts)
    pixels, channels = parts[0].shape
    lanes = round_up(channels, LANES)
    tokens = frames * pixels
    inner = weights[3].shape[1]
    vmem = pl.BlockSpec(memory_space=pltpu.VMEM)
    hbm = pl.BlockSpec(memory_space=pltpu.HBM)
    flops = 2 * tokens * channels * (3 * lanes + channels + 3 * inner)
    return pl.pallas_call(
        functools.partial(temporal_kernel, frames),
        out_shape=[jax.ShapeDtypeStruct((pixels, channels), BF16)] * frames,
        in_specs=[vmem] * frames + [hbm] * 4,
        out_specs=[vmem] * frames,
        scratch_shapes=[
            pltpu.VMEM((tokens, channels), BF16),
            pltpu.VMEM((tokens, 3 * lanes), BF16),
            pltpu.VMEM((tokens, lanes), BF16),
            pltpu.VMEM((tokens, inner), BF16),
            *[pltpu.VMEM(w.shape, BF16) for w in weights],
            pltpu.SemaphoreType.DMA((4,)),
        ],
        compiler_params=pltpu.CompilerParams(vmem_limit_bytes=40 * 1024 * 1024),
        cost_estimate=pl.CostEstimate(
            flops=flops, bytes_accessed=4000000, transcendentals=tokens * inner
        ),
        name="temporal",
    )(*parts, *weights)


def send(block, hops):
    axes = tuple(axis for axis, _ in hops)
    sizes = [lax.axis_size(axis) for axis in axes]
    route = []
    for source in range(math.prod(sizes)):
        rest, target, stride = source, 0, 1
        for size, (_, distance) in zip(reversed(sizes), reversed(hops)):
            target += (rest % size + distance) % size * stride
            rest, stride = rest // size, stride * size
        route.append((source, target))
    if all(a == b for a, b in route):
        return block
    return lax.ppermute(block, axes if len(axes) > 1 else axes[0], route)


def embed_time(stamps, time_weight):
    half_width = time_weight.shape[0] // 2
    frequency = jnp.exp(-math.log(10000.0) * jnp.arange(half_width, dtype=F32) / half_width)
    angles = stamps.astype(F32)[:, None] * frequency[None, :]
    sinusoid = jnp.concatenate([jnp.cos(angles), jnp.sin(angles)], axis=1)
    out = jnp.dot(jax.nn.silu(sinusoid).astype(BF16), time_weight, preferred_element_type=F32)
    return jnp.pad(out, ((0, 0), (0, round_up(out.shape[1], LANES) - out.shape[1])))


def per_device(
    features,
    timesteps,
    conv_first,
    conv_second,
    time_weight,
    qkv_weight,
    attn_out,
    geglu_in,
    geglu_out,
):
    _, _, own_rows, columns, channels = features.shape
    half = lax.axis_size("halo")
    rows = own_rows * half
    shards = lax.axis_size("shard")
    spot = lax.axis_index("shard")
    part = own_rows * columns // shards

    moved = send(features.reshape(own_rows * columns, channels), (("section", 1),))
    embeds = embed_time(timesteps[0], time_weight[0])
    spatial_weights, padded = prepare(conv_first[0], conv_second[0], qkv_weight[0])

    moved, spatial_weights, padded = lax.optimization_barrier((moved, spatial_weights, padded))
    temporal_weights = (padded, attn_out[0], geglu_in[0], geglu_out[0].T)
    own, other = [moved], [send(moved, (("halo", 1),))]
    for denoise_step in range(STEPS):
        parts = spatial(
            own, other, spatial_weights, embeds, denoise_step, rows, columns, half, shards
        )
        parts = [send(parts[d], (("shard", d),)) for d in range(shards)]
        parts = temporal(parts, temporal_weights)
        if denoise_step < STEPS - 1:
            own = [send(parts[d], (("shard", -d), ("section", 1))) for d in range(shards)]
            other = [send(block, (("halo", 1),)) for block in own]
        else:
            own = [send(parts[d], (("shard", -d),)) for d in range(shards)]
    result = jnp.zeros((own_rows * columns, channels), BF16)
    for d in range(shards):
        result = lax.dynamic_update_slice_in_dim(
            result, own[d], lax.rem(spot + d, shards) * part, axis=0
        )
    return result.reshape(features.shape)


def solution(mesh):
    return jax.shard_map(
        per_device,
        mesh=mesh,
        in_specs=(
            P(("groups", "section"), "shard", "halo", None, None),
            P(("groups", "section"), None),
            P("section", None, None, None, None),
            P("section", None, None, None, None),
            P("section", None, None),
            P("section", None, None),
            P("section", None, None),
            P("section", None, None),
            P("section", None, None),
        ),
        out_specs=P(("groups", "section"), "shard", "halo", None, None),
        check_vma=False,
    )
```

```python
import functools
import math

import jax
import jax.numpy as jnp
from jax import lax
from jax.experimental import pallas as pl
from jax.experimental.pallas import tpu as pltpu
from jax.sharding import PartitionSpec as P

HEAD_DIM = 64
GROUPS = 32
STEPS = 2
LANES = 128
WIDE = 256
F32 = jnp.float32
BF16 = jnp.bfloat16


def partner(spot, distance, count):
    if count & (count - 1):
        return (spot + distance) % count
    return spot ^ distance


def distances(count):
    order, low = [], count
    while low > 1:
        low = (low + 1) // 2
        order += [d for d in range(low, count) if d not in order]
    return order + [0]


def round_up(value, unit):
    return -(-value // unit) * unit


def dense_rows(pixels, channels):
    return pixels * channels // LANES


def pack_part(values, target, at, channels):
    pixels, full = values.shape[0], channels // LANES
    for i in range(full):
        block = values[:, i * LANES : (i + 1) * LANES].astype(BF16)
        target[at + i * pixels : at + (i + 1) * pixels, :] = block
    if channels % LANES:
        rest = values[:, full * LANES :]
        first, second = rest[: pixels // 2], rest[pixels // 2 :]
        lane = lax.broadcasted_iota(jnp.int32, (1, LANES), 1)
        both = jnp.where(lane < LANES // 2, first, pltpu.roll(second, LANES // 2, 1))
        target[at + full * pixels : at + full * pixels + pixels // 2, :] = both.astype(BF16)


def unpack_part(source, at, pixels, channels):
    full = channels // LANES
    blocks = [
        (i, 0, source[at + i * pixels : at + (i + 1) * pixels, :].astype(F32)) for i in range(full)
    ]
    if channels % LANES:
        both = source[at + full * pixels : at + full * pixels + pixels // 2, :].astype(F32)
        low = lax.broadcasted_iota(jnp.int32, (1, LANES), 1) < LANES // 2
        blocks.append((full, 0, jnp.where(low, both, 0.0)))
        blocks.append((full, pixels // 2, jnp.where(low, pltpu.roll(both, LANES // 2, 1), 0.0)))
    return blocks


def window_sum(values, width, direction):
    lanes = values.shape[1]
    done, result, power, size = 0, None, values, 1
    while True:
        if width & size:
            moved = power
            if done:
                moved = pltpu.roll(power, done if direction > 0 else lanes - done, 1)
            result = moved if result is None else result + moved
            done += size
        if done == width:
            return result
        power = power + pltpu.roll(power, size if direction > 0 else lanes - size, 1)
        size *= 2


def group_scale(total, square, entries, group_width, channels):
    lanes = total.shape[1]
    lane = lax.broadcasted_iota(jnp.int32, (1, lanes), 1)
    last = (lane % group_width == group_width - 1) & (lane < channels)

    def mean(sums):
        sums = window_sum(jnp.broadcast_to(jnp.sum(sums, axis=0, keepdims=True), (8, lanes)), group_width, 1)
        return window_sum(jnp.where(last, sums, 0.0), group_width, -1)[0:1] / entries

    average = mean(total)
    scale = lax.rsqrt(mean(square) - average * average + 1e-05)
    scale = jnp.where(lane < channels, 0.5 * scale, 0.0)
    return scale, -average * scale


def spatial_kernel(rows, half, columns, channels, group_width, step, ways, shards, *refs):
    own, other = refs[:ways], refs[ways : 2 * ways]
    kernels, embeds = refs[2 * ways : 2 * ways + 2]
    outs = refs[2 * ways + 2 : 2 * ways + 2 + shards]
    field, hidden, middle, edge, pair = refs[2 * ways + 2 + shards :]
    embed = embeds[step : step + 1, :]
    lanes = field.shape[1]
    own_rows = rows // half
    part = own_rows * columns // shards
    here = lax.axis_index("halo")
    spot = lax.axis_index("shard")
    own_base = here * (own_rows * columns)
    other_base = (1 - here) * (own_rows * columns)
    zero = jnp.zeros((8, lanes), F32)

    height = dense_rows(part, channels)
    for base, arrived in ((own_base, own), (other_base, other)):
        if ways == 1:
            place = pl.ds(pl.multiple_of(base, columns), own_rows * columns)
            field[place, lanes - LANES :] = jnp.zeros((own_rows * columns, LANES), F32)
            field[place, :channels] = arrived[0][...].astype(F32)
            continue
        held = [(block, at) for block in arrived for at in range(0, block.shape[0], height)]
        for (block, at), d in zip(held, distances(shards)):
            here_part = base + partner(spot, d, shards) * part
            for i, first, values in unpack_part(block, at, part, channels):
                place = pl.multiple_of(here_part + first, 8)
                field[pl.ds(place, values.shape[0]), i * LANES : (i + 1) * LANES] = values

    def sum_row(i, carry):
        total, square = carry
        chunk = field[pl.ds(pl.multiple_of(i * columns, columns), columns), :]
        chunk = chunk.reshape(columns // 8, 8, lanes)
        return total + jnp.sum(chunk, axis=0), square + jnp.sum(chunk * chunk, axis=0)

    field_sums = lax.fori_loop(0, rows, sum_row, (zero, zero), unroll=4)

    def activate(source, scale, shift, first, start, stop):
        def body(i, before):
            row = first - 1 + i
            inside = ((row >= 0) & (row < rows)).astype(F32)
            at = pl.multiple_of(jnp.clip(row, 0, rows - 1) * columns, columns)
            u = source[pl.ds(at, columns), :] * (scale * inside) + shift * inside
            g = u + u * jnp.tanh(u)
            to = pl.ds(pl.multiple_of(i * columns, columns), columns)
            rest = g[:, WIDE:]
            middle[to, :] = g[:, :WIDE].astype(BF16)
            edge[to, :] = rest.astype(BF16)
            pair[to, :] = (before + pltpu.roll(rest, LANES // 2, 1)).astype(BF16)
            return rest

        lax.fori_loop(start, stop, body, jnp.zeros((columns, LANES), F32), unroll=4)

    step_rows = min(WIDE, own_rows * columns)
    column = lax.broadcasted_iota(jnp.int32, (step_rows, 1), 0) % columns
    low = lax.broadcasted_iota(jnp.int32, (1, LANES), 1) < channels - WIDE

    def convolve(kernel, start):
        top, mid, bottom = [slice(start + r * columns, start + r * columns + step_rows) for r in range(3)]
        window = jnp.concatenate(
            [middle[top, :], middle[mid, :], middle[bottom, :], pair[mid, :], edge[bottom, :]], axis=1
        )
        y = jnp.dot(window, kernel[...], preferred_element_type=F32)

        def from_left(values):
            return jnp.where(column == 0, 0.0, pltpu.roll(values, 1, 0))

        def from_right(values):
            return jnp.where(column == columns - 1, 0.0, pltpu.roll(values, step_rows - 1, 0))

        wide = y[:, WIDE : 2 * WIDE] + from_left(y[:, :WIDE]) + from_right(y[:, 2 * WIDE : 3 * WIDE])
        tail = y[:, 3 * WIDE : 3 * WIDE + LANES]
        narrow = from_left(tail) + pltpu.roll(tail, LANES // 2, 1) + from_right(y[:, 3 * WIDE + LANES :])
        return wide, narrow

    entries = float(rows * columns * group_width)
    for pad in (0, (rows + 1) * columns):
        middle[pad : pad + columns, :] = jnp.zeros((columns, WIDE), BF16)
        edge[pad : pad + columns, :] = jnp.zeros((columns, LANES), BF16)
    activate(field, *group_scale(*field_sums, entries, group_width, channels), 0, 1, rows + 1)
    total, square = zero, zero
    for start in range(0, rows * columns, step_rows):
        wide, narrow = convolve(kernels.at[0], start)
        chunk = jnp.concatenate(
            [wide + embed[:, :WIDE], jnp.where(low, narrow + embed[:, WIDE:], 0.0)], axis=1
        )
        hidden[start : start + step_rows, :] = chunk
        chunk = chunk.reshape(step_rows // 8, 8, lanes)
        total = total + jnp.sum(chunk, axis=0)
        square = square + jnp.sum(chunk * chunk, axis=0)
    activate(
        hidden,
        *group_scale(total, square, entries, group_width, channels),
        here * own_rows,
        0,
        own_rows + 2,
    )
    for start in range(0, own_rows * columns, step_rows):
        wide, narrow = convolve(kernels.at[1], start)
        mine = pl.ds(pl.multiple_of(own_base + start, step_rows), step_rows)
        hidden[mine, :WIDE] = wide + field[mine, :WIDE]
        hidden[mine, WIDE:] = narrow + field[mine, WIDE:]
    for i, d in enumerate(distances(shards)):
        place = pl.multiple_of(own_base + partner(spot, d, shards) * part, part)
        pack_part(hidden[pl.ds(place, part), :], outs[i], 0, channels)


def spatial(own, other, weights, embeds, step, rows, columns, half, shards):
    tokens = rows * columns
    part = tokens // half // shards
    channels = sum(block.size for block in own) // (tokens // half)
    ways = len(own)
    lanes = round_up(channels, LANES)
    padded = tokens + 2 * columns
    depth = weights.shape[1]
    kernel = functools.partial(
        spatial_kernel,
        rows,
        half,
        columns,
        channels,
        channels // GROUPS,
        step,
        ways,
        shards,
    )
    vmem = pl.BlockSpec(memory_space=pltpu.VMEM)
    return pl.pallas_call(
        kernel,
        out_shape=[jax.ShapeDtypeStruct((dense_rows(part, channels), LANES), BF16)] * shards,
        in_specs=[vmem] * (2 * ways + 2),
        out_specs=[vmem] * shards,
        scratch_shapes=[
            pltpu.VMEM((tokens, lanes), F32),
            pltpu.VMEM((tokens, lanes), F32),
            pltpu.VMEM((padded, WIDE), BF16),
            pltpu.VMEM((padded, LANES), BF16),
            pltpu.VMEM((padded, LANES), BF16),
        ],
        compiler_params=pltpu.CompilerParams(vmem_limit_bytes=14 * 1024 * 1024),
        cost_estimate=pl.CostEstimate(
            flops=3 * tokens * depth * depth,
            bytes_accessed=6000000,
            transcendentals=tokens * lanes,
        ),
        name="spatial",
    )(*own, *other, weights, embeds)


def prepare_kernel(channels, kernel1, kernel2, qkv, kernels, padded):
    spare = channels - WIDE
    for kernel, packed in ((kernel1, kernels.at[0]), (kernel2, kernels.at[1])):
        depth = packed.shape[0]
        packed[3 * channels :, :] = jnp.zeros((depth - 3 * channels, depth), BF16)
        for r in range(3):
            for source, target in (
                (slice(0, WIDE), slice(r * WIDE, (r + 1) * WIDE)),
                (slice(WIDE, channels), slice(3 * WIDE + r * spare, 3 * WIDE + (r + 1) * spare)),
            ):
                for s in range(3):
                    packed[target, s * WIDE : (s + 1) * WIDE] = kernel[r, s, source, :WIDE]
                first, second, third = [kernel[r, s, source, WIDE:] for s in range(3)]
                packed[target, 3 * WIDE : 3 * WIDE + LANES] = jnp.concatenate([first, second], axis=1)
                packed[target, 3 * WIDE + LANES :] = jnp.concatenate(
                    [third, jnp.zeros_like(third)], axis=1
                )
    lanes = padded.shape[1] // 3
    padded[...] = jnp.zeros(padded.shape, BF16)
    for i in range(3):
        padded[:, i * lanes : i * lanes + channels] = qkv[:, i * channels : (i + 1) * channels]


def prepare(conv_first, conv_second, qkv):
    channels = qkv.shape[0]
    depth = round_up(3 * channels, WIDE)
    lanes = round_up(channels, LANES)
    vmem = pl.BlockSpec(memory_space=pltpu.VMEM)
    return pl.pallas_call(
        functools.partial(prepare_kernel, channels),
        out_shape=[
            jax.ShapeDtypeStruct((2, depth, depth), BF16),
            jax.ShapeDtypeStruct((channels, 3 * lanes), BF16),
        ],
        in_specs=[vmem] * 3,
        out_specs=[vmem] * 2,
        compiler_params=pltpu.CompilerParams(vmem_limit_bytes=14 * 1024 * 1024),
        cost_estimate=pl.CostEstimate(flops=0, bytes_accessed=10000000, transcendentals=0),
        name="prepare",
    )(conv_first, conv_second, qkv)


def norm_rows(values):
    average = jnp.mean(values, axis=-1, keepdims=True)
    centred = values - average
    spread = jnp.mean(centred * centred, axis=-1, keepdims=True)
    return (centred * lax.rsqrt(spread + 1e-05)).astype(BF16)


def feed_forward(stream, geglu_in, geglu_out, active):
    inner = geglu_out.shape[1]
    normed = norm_rows(stream.astype(F32))
    for at in range(0, inner, WIDE):
        value = jnp.dot(normed, geglu_in[:, at : at + WIDE], preferred_element_type=F32)
        gate = jnp.dot(normed, geglu_in[:, inner + at : inner + at + WIDE], preferred_element_type=F32)
        act = value * (0.5 * gate) * (1.0 + lax.erf(gate * math.sqrt(0.5)))
        active[:, at : at + WIDE] = act.astype(BF16)
    update = lax.dot_general(
        active[...], geglu_out[...], (((1,), (1,)), ((), ())), preferred_element_type=F32
    )
    return stream.astype(F32) + update


def leave(values, target):
    pixels, channels = values.shape
    if target.shape == values.shape:
        target[...] = values.astype(BF16)
        return
    spare = round_up(channels, LANES) - channels
    values = jnp.concatenate([values, jnp.zeros((pixels, spare), F32)], axis=1)
    pack_part(values, target, 0, channels)


def feed_kernel(count, *refs):
    rest, geglu_in, geglu_out = refs[:3]
    outs = refs[3 : 3 + count]
    (active,) = refs[3 + count :]
    done = feed_forward(rest[...], geglu_in, geglu_out, active)
    pixels = done.shape[0] // count
    for i in range(count):
        leave(done[i * pixels : (i + 1) * pixels, :], outs[i])


def temporal_kernel(frames, sooner, *refs):
    parts = refs[:frames]
    qkv, attn_out, geglu_in, geglu_out = refs[frames : frames + 4]
    outs = refs[frames + 4 : frames + 4 + sooner]
    rest = refs[frames + 4 + sooner]
    stream, projected, mixed, active = refs[frames + 5 + sooner :]
    channels = stream.shape[1]
    pixels = stream.shape[0] // frames
    lanes = projected.shape[1] // 3

    for f in range(frames):
        for i, first, values in unpack_part(parts[f], 0, pixels, channels):
            rows = slice(f * pixels + first, f * pixels + first + values.shape[0])
            width = min(LANES, channels - i * LANES)
            stream[rows, i * LANES : i * LANES + width] = values[:, :width].astype(BF16)
    normed = norm_rows(stream[...].astype(F32))
    projected[...] = jnp.dot(normed, qkv[...], preferred_element_type=F32).astype(BF16)

    pack = min(pixels, WIDE // frames)
    tile = frames * pack
    same = (
        lax.broadcasted_iota(jnp.int32, (tile, tile), 0) % pack
        == lax.broadcasted_iota(jnp.int32, (tile, tile), 1) % pack
    )
    lane = lax.broadcasted_iota(jnp.int32, (1, LANES), 1)
    sharing = LANES // HEAD_DIM
    for first in range(0, pixels, pack):
        places = [slice(f * pixels + first, f * pixels + first + pack) for f in range(frames)]
        for at in range(0, channels, LANES):
            query, key, value = [
                jnp.concatenate([projected[p, i * lanes + at : i * lanes + at + LANES] for p in places])
                for i in range(3)
            ]
            mix = None
            for j in range(min(sharing, (channels - at) // HEAD_DIM)):
                chosen = (lane >= j * HEAD_DIM) & (lane < (j + 1) * HEAD_DIM)
                scores = lax.dot_general(
                    query * chosen.astype(BF16),
                    key,
                    (((1,), (1,)), ((), ())),
                    preferred_element_type=F32,
                )
                scores = jnp.where(same, scores, float(jnp.finfo(F32).min))
                top = jnp.max(scores, axis=1, keepdims=True)
                powers = jnp.exp((scores - top) * HEAD_DIM ** (-0.5))
                total = jnp.sum(powers, axis=1, keepdims=True)
                weights = (powers * (1.0 / total)).astype(BF16)
                head = jnp.dot(weights, value, preferred_element_type=F32)
                mix = head if mix is None else jnp.where(chosen, head, mix)
            mix = mix.astype(BF16)
            for f, p in enumerate(places):
                mixed[p, at : at + LANES] = mix[f * pack : (f + 1) * pack]

    update = jnp.dot(mixed[:, :channels], attn_out[...], preferred_element_type=F32)
    after = (stream[...].astype(F32) + update).astype(BF16)
    rest[...] = after[sooner * pixels :, :]
    done = feed_forward(after[: sooner * pixels, :], geglu_in, geglu_out, active)
    for f in range(sooner):
        leave(done[f * pixels : (f + 1) * pixels, :], outs[f])


def temporal(parts, weights, dense):
    frames = len(parts)
    sooner = frames // 2
    later = frames - sooner
    channels = weights[0].shape[0]
    pixels = parts[0].size // channels
    lanes = round_up(channels, LANES)
    tokens = frames * pixels
    inner = weights[3].shape[1]
    vmem = pl.BlockSpec(memory_space=pltpu.VMEM)
    piece = jax.ShapeDtypeStruct(parts[0].shape if dense else (pixels, channels), BF16)
    feed_flops = 6 * pixels * channels * inner
    params = pltpu.CompilerParams(vmem_limit_bytes=14 * 1024 * 1024)
    *first, rest = pl.pallas_call(
        functools.partial(temporal_kernel, frames, sooner),
        out_shape=[piece] * sooner + [jax.ShapeDtypeStruct((later * pixels, channels), BF16)],
        in_specs=[vmem] * (frames + 4),
        out_specs=[vmem] * (sooner + 1),
        scratch_shapes=[
            pltpu.VMEM((tokens, channels), BF16),
            pltpu.VMEM((tokens, 3 * lanes), BF16),
            pltpu.VMEM((tokens, lanes), BF16),
            pltpu.VMEM((sooner * pixels, inner), BF16),
        ],
        compiler_params=params,
        cost_estimate=pl.CostEstimate(
            flops=8 * tokens * channels * lanes + sooner * feed_flops,
            bytes_accessed=4000000,
            transcendentals=sooner * pixels * inner,
        ),
        name="temporal",
    )(*parts, *weights)
    second = pl.pallas_call(
        functools.partial(feed_kernel, later),
        out_shape=[piece] * later,
        in_specs=[vmem] * 3,
        out_specs=[vmem] * later,
        scratch_shapes=[pltpu.VMEM((later * pixels, inner), BF16)],
        compiler_params=params,
        cost_estimate=pl.CostEstimate(
            flops=later * feed_flops,
            bytes_accessed=3000000,
            transcendentals=later * pixels * inner,
        ),
        name="feed",
    )(rest, weights[2], weights[3])
    return [*first, *second]


def send(block, axis, distance):
    count = lax.axis_size(axis)
    return lax.ppermute(block, axis, [(i, (i + distance) % count) for i in range(count)])


def exchange(parts, back=False, across=0):
    shards, sections = lax.axis_size("shard"), lax.axis_size("section")
    arrived = []
    for part, d in zip(parts, distances(shards)):
        target = [partner(z, d, shards) for z in range(shards)]
        if back:
            target = [target.index(z) for z in range(shards)]
        if across:
            route = [
                (z * sections + s, target[z] * sections + (s + across) % sections)
                for z in range(shards)
                for s in range(sections)
            ]
            part = lax.ppermute(part, ("shard", "section"), route)
        elif d:
            part = lax.ppermute(part, "shard", list(enumerate(target)))
        arrived.append(part)
    return arrived


def join_kernel(*refs):
    *parts, whole = refs
    height = parts[0].shape[0]
    for i, part in enumerate(parts):
        whole[i * height : (i + 1) * height, :] = part[...]


def join(parts):
    vmem = pl.BlockSpec(memory_space=pltpu.VMEM)
    height, lanes = parts[0].shape
    return pl.pallas_call(
        join_kernel,
        out_shape=jax.ShapeDtypeStruct((len(parts) * height, lanes), parts[0].dtype),
        in_specs=[vmem] * len(parts),
        out_specs=vmem,
        compiler_params=pltpu.CompilerParams(vmem_limit_bytes=4 * 1024 * 1024),
        name="join",
    )(*parts)


def assemble(parts):
    size, channels = parts[0].shape
    spot = lax.axis_index("shard")
    whole = jnp.zeros((len(parts) * size, channels), parts[0].dtype)
    for part, d in zip(parts, distances(len(parts))):
        place = partner(spot, d, len(parts)) * size
        whole = lax.dynamic_update_slice_in_dim(whole, part, place, axis=0)
    return whole


def embed_time(stamps, time_weight):
    half_width = time_weight.shape[0] // 2
    frequency = jnp.exp(-math.log(10000.0) * jnp.arange(half_width, dtype=F32) / half_width)
    angles = stamps.astype(F32)[:, None] * frequency[None, :]
    sinusoid = jnp.concatenate([jnp.cos(angles), jnp.sin(angles)], axis=1)
    out = jnp.dot(jax.nn.silu(sinusoid).astype(BF16), time_weight, preferred_element_type=F32)
    return jnp.pad(out, ((0, 0), (0, round_up(out.shape[1], LANES) - out.shape[1])))


def per_device(
    features,
    timesteps,
    conv_first,
    conv_second,
    time_weight,
    qkv_weight,
    attn_out,
    geglu_in,
    geglu_out,
):
    _, _, own_rows, columns, channels = features.shape
    half = lax.axis_size("halo")
    rows = own_rows * half
    shards = lax.axis_size("shard")

    moved = send(features.reshape(own_rows * columns, channels), "section", 1)
    embeds = embed_time(timesteps[0], time_weight[0])
    spatial_weights, padded = prepare(conv_first[0], conv_second[0], qkv_weight[0])

    moved, spatial_weights, padded = lax.optimization_barrier((moved, spatial_weights, padded))
    own = [moved]
    temporal_weights = (padded, attn_out[0], geglu_in[0], geglu_out[0].T)
    for denoise_step in range(STEPS):
        last = denoise_step == STEPS - 1
        parts = spatial(
            own,
            [send(block, "halo", 1) for block in own],
            spatial_weights,
            embeds,
            denoise_step,
            rows,
            columns,
            half,
            shards,
        )
        parts = temporal(exchange(parts), temporal_weights, dense=not last)
        parts = exchange(parts, back=True, across=0 if last else 1)
        own = [join(parts[: shards // 2]), *parts[shards // 2 :]]
    return assemble(parts).reshape(features.shape)


def solution(mesh):
    return jax.shard_map(
        per_device,
        mesh=mesh,
        in_specs=(
            P(("groups", "section"), "shard", "halo", None, None),
            P(("groups", "section"), None),
            P("section", None, None, None, None),
            P("section", None, None, None, None),
            P("section", None, None),
            P("section", None, None),
            P("section", None, None),
            P("section", None, None),
            P("section", None, None),
        ),
        out_specs=P(("groups", "section"), "shard", "halo", None, None),
        check_vma=False,
    )
```

```python
import functools
import math

import jax
import jax.numpy as jnp
from jax import lax
from jax.experimental import pallas as pl
from jax.experimental.pallas import tpu as pltpu
from jax.sharding import PartitionSpec as P

HEAD_DIM = 64
GROUPS = 32
STEPS = 2
LANES = 128
WIDE = 256
F32 = jnp.float32
BF16 = jnp.bfloat16


def partner(spot, distance, count):
    if count & (count - 1):
        return (spot + distance) % count
    return spot ^ distance


def distances(count):
    order, low = [], count
    while low > 1:
        low = (low + 1) // 2
        order += [d for d in range(low, count) if d not in order]
    return order + [0]


def round_up(value, unit):
    return -(-value // unit) * unit


def dense_rows(pixels, channels):
    return pixels * channels // LANES


def pack_part(values, target, at, channels):
    pixels, full = values.shape[0], channels // LANES
    for i in range(full):
        block = values[:, i * LANES : (i + 1) * LANES].astype(BF16)
        target[at + i * pixels : at + (i + 1) * pixels, :] = block
    if channels % LANES:
        rest = values[:, full * LANES :]
        first, second = rest[: pixels // 2], rest[pixels // 2 :]
        lane = lax.broadcasted_iota(jnp.int32, (1, LANES), 1)
        both = jnp.where(lane < LANES // 2, first, pltpu.roll(second, LANES // 2, 1))
        target[at + full * pixels : at + full * pixels + pixels // 2, :] = both.astype(BF16)


def unpack_part(source, at, pixels, channels):
    full = channels // LANES
    blocks = [
        (i, 0, source[at + i * pixels : at + (i + 1) * pixels, :].astype(F32)) for i in range(full)
    ]
    if channels % LANES:
        both = source[at + full * pixels : at + full * pixels + pixels // 2, :].astype(F32)
        low = lax.broadcasted_iota(jnp.int32, (1, LANES), 1) < LANES // 2
        blocks.append((full, 0, jnp.where(low, both, 0.0)))
        blocks.append((full, pixels // 2, jnp.where(low, pltpu.roll(both, LANES // 2, 1), 0.0)))
    return blocks


def group_scale(total, square, entries, group_width, channels):
    lanes = total.shape[1]
    lane = lax.broadcasted_iota(jnp.int32, (1, lanes), 1)
    spot = lane % group_width
    row = lax.broadcasted_iota(jnp.int32, (8, 1), 0)
    both = jnp.where(
        row == 0, jnp.sum(total, axis=0, keepdims=True), jnp.sum(square, axis=0, keepdims=True)
    )
    group = both
    for k in range(1, group_width):
        group = group + jnp.where(spot + k < group_width, pltpu.roll(both, lanes - k, 1), 0.0)
        group = group + jnp.where(spot >= k, pltpu.roll(both, k, 1), 0.0)
    group = group / entries
    average = group[0:1]
    scale = lax.rsqrt(group[1:2] - average * average + 1e-05)
    scale = jnp.where(lane < channels, 0.5 * scale, 0.0)
    return scale, -average * scale


def activate(source, targets, scale, shift, rows, columns, first, start, stop):
    middle, edge, pair = targets

    def body(i, before):
        row = first - 1 + i
        inside = ((row >= 0) & (row < rows)).astype(F32)
        at = pl.multiple_of(jnp.clip(row, 0, rows - 1) * columns, columns)
        u = source[pl.ds(at, columns), :] * (scale * inside) + shift * inside
        g = u + u * jnp.tanh(u)
        to = pl.ds(pl.multiple_of(i * columns, columns), columns)
        rest = g[:, WIDE:]
        middle[to, :] = g[:, :WIDE].astype(BF16)
        edge[to, :] = rest.astype(BF16)
        pair[to, :] = (before + pltpu.roll(rest, LANES // 2, 1)).astype(BF16)
        return rest

    lax.fori_loop(start, stop, body, jnp.zeros((columns, LANES), F32), unroll=stop - start)


def convolve(targets, kernel, start, count, columns):
    middle, edge, pair = targets
    top, mid, bottom = [
        pl.ds(pl.multiple_of(start + r * columns, columns), count) for r in range(3)
    ]
    window = jnp.concatenate(
        [middle[top, :], middle[mid, :], middle[bottom, :], pair[mid, :], edge[bottom, :]], axis=1
    )
    y = jnp.dot(window, kernel[...], preferred_element_type=F32)
    column = lax.broadcasted_iota(jnp.int32, (count, 1), 0) % columns

    def from_left(values):
        return jnp.where(column == 0, 0.0, pltpu.roll(values, 1, 0))

    def from_right(values):
        return jnp.where(column == columns - 1, 0.0, pltpu.roll(values, count - 1, 0))

    wide = y[:, WIDE : 2 * WIDE] + from_left(y[:, :WIDE]) + from_right(y[:, 2 * WIDE : 3 * WIDE])
    tail = y[:, 3 * WIDE : 3 * WIDE + LANES]
    return wide, from_left(tail) + from_right(y[:, 3 * WIDE + LANES :]), tail


def convolve_part(targets, kernel, start, columns, base, target):
    pixels = base.shape[0]
    wide, narrow, tail = convolve(targets, kernel, start, pixels, columns)
    for i in range(WIDE // LANES):
        lanes = slice(i * LANES, (i + 1) * LANES)
        target[i * pixels : (i + 1) * pixels, :] = (wide[:, lanes] + base[:, lanes]).astype(BF16)
    narrow = narrow + base[:, WIDE:]
    low = lax.broadcasted_iota(jnp.int32, (1, LANES), 1) < LANES // 2
    first, second = slice(0, pixels // 2), slice(pixels // 2, pixels)
    both = jnp.where(
        low,
        narrow[first] + pltpu.roll(tail[first], LANES // 2, 1),
        pltpu.roll(narrow[second], LANES // 2, 1) + tail[second],
    )
    target[WIDE // LANES * pixels :, :] = both.astype(BF16)


def spatial_kernel(rows, half, columns, channels, group_width, step, ways, shards, sooner, *refs):
    own, other = refs[:ways], refs[ways : 2 * ways]
    kernels, embeds = refs[2 * ways : 2 * ways + 2]
    outs = refs[2 * ways + 2 : 2 * ways + 2 + sooner]
    keep, *targets = refs[2 * ways + 2 + sooner : 2 * ways + 6 + sooner]
    field, hidden, *firsts = refs[2 * ways + 6 + sooner :]
    embed = embeds[step : step + 1, :]
    lanes = field.shape[1]
    own_rows = rows // half
    part = own_rows * columns // shards
    here = lax.axis_index("halo")
    spot = lax.axis_index("shard")
    own_base = here * (own_rows * columns)
    other_base = (1 - here) * (own_rows * columns)
    zero = jnp.zeros((8, lanes), F32)

    height = dense_rows(part, channels)
    for base, arrived in ((own_base, own), (other_base, other)):
        if ways == 1:
            place = pl.ds(pl.multiple_of(base, columns), own_rows * columns)
            field[place, lanes - LANES :] = jnp.zeros((own_rows * columns, LANES), F32)
            field[place, :channels] = arrived[0][...].astype(F32)
            continue
        held = [(block, at) for block in arrived for at in range(0, block.shape[0], height)]
        for (block, at), d in zip(held, distances(shards)):
            here_part = base + partner(spot, d, shards) * part
            for i, first, values in unpack_part(block, at, part, channels):
                place = pl.multiple_of(here_part + first, 8)
                field[pl.ds(place, values.shape[0]), i * LANES : (i + 1) * LANES] = values

    def sum_row(i, carry):
        total, square = carry
        chunk = field[pl.ds(pl.multiple_of(i * columns, columns), columns), :]
        chunk = chunk.reshape(columns // 8, 8, lanes)
        return total + jnp.sum(chunk, axis=0), square + jnp.sum(chunk * chunk, axis=0)

    total, square = lax.fori_loop(0, rows, sum_row, (zero, zero), unroll=4)
    entries = float(rows * columns * group_width)
    middle, edge, _ = firsts
    for pad in (0, (rows + 1) * columns):
        middle[pad : pad + columns, :] = jnp.zeros((columns, WIDE), BF16)
        edge[pad : pad + columns, :] = jnp.zeros((columns, LANES), BF16)
    scale, shift = group_scale(total, square, entries, group_width, channels)
    activate(field, firsts, scale, shift, rows, columns, 0, 1, rows + 1)

    low = lax.broadcasted_iota(jnp.int32, (1, LANES), 1) < channels - WIDE
    total, square = zero, zero
    count = min(WIDE, own_rows * columns)
    for start in range(0, rows * columns, count):
        wide, narrow, tail = convolve(firsts, kernels.at[0], start, count, columns)
        narrow = narrow + pltpu.roll(tail, LANES // 2, 1) + embed[:, WIDE:]
        chunk = jnp.concatenate([wide + embed[:, :WIDE], jnp.where(low, narrow, 0.0)], axis=1)
        hidden[start : start + count, :] = chunk
        chunk = chunk.reshape(count // 8, 8, lanes)
        total = total + jnp.sum(chunk, axis=0)
        square = square + jnp.sum(chunk * chunk, axis=0)
    scale, shift = group_scale(total, square, entries, group_width, channels)
    first_row = here * own_rows
    activate(hidden, targets, scale, shift, rows, columns, first_row, 0, own_rows + 2)
    for i, d in enumerate(distances(shards)):
        start = partner(spot, d, shards) * part
        base = field[pl.ds(pl.multiple_of(own_base + start, 8), part), :]
        if i < sooner:
            convolve_part(targets, kernels.at[1], start, columns, base, outs[i])
        else:
            keep[(i - sooner) * part : (i - sooner + 1) * part, :] = base


def finish_kernel(columns, shards, sooner, keep, middle, edge, pair, kernels, *outs):
    part = keep.shape[0] // (shards - sooner)
    spot = lax.axis_index("shard")
    for i, d in enumerate(distances(shards)[sooner:]):
        start = partner(spot, d, shards) * part
        base = keep[i * part : (i + 1) * part, :]
        convolve_part((middle, edge, pair), kernels.at[1], start, columns, base, outs[i])


def spatial(own, other, weights, embeds, step, rows, columns, half, shards):
    tokens = rows * columns
    part = tokens // half // shards
    channels = sum(block.size for block in own) // (tokens // half)
    ways = len(own)
    sooner = shards // 2
    later = shards - sooner
    lanes = round_up(channels, LANES)
    depth = weights.shape[1]
    piece = jax.ShapeDtypeStruct((dense_rows(part, channels), LANES), BF16)
    vmem = pl.BlockSpec(memory_space=pltpu.VMEM)
    params = pltpu.CompilerParams(vmem_limit_bytes=14 * 1024 * 1024)

    def active(rows_there):
        return [((rows_there + 2) * columns, width) for width in (WIDE, LANES, LANES)]

    *first, keep, middle, edge, pair = pl.pallas_call(
        functools.partial(
            spatial_kernel,
            rows,
            half,
            columns,
            channels,
            channels // GROUPS,
            step,
            ways,
            shards,
            sooner,
        ),
        out_shape=[piece] * sooner
        + [jax.ShapeDtypeStruct((later * part, lanes), F32)]
        + [jax.ShapeDtypeStruct(shape, BF16) for shape in active(rows // half)],
        in_specs=[vmem] * (2 * ways + 2),
        out_specs=[vmem] * (sooner + 4),
        scratch_shapes=[
            pltpu.VMEM((tokens, lanes), F32),
            pltpu.VMEM((tokens, lanes), F32),
            *[pltpu.VMEM(shape, BF16) for shape in active(rows)],
        ],
        compiler_params=params,
        cost_estimate=pl.CostEstimate(
            flops=3 * tokens * depth * depth,
            bytes_accessed=6000000,
            transcendentals=tokens * lanes,
        ),
        name="spatial",
    )(*own, *other, weights, embeds)
    second = pl.pallas_call(
        functools.partial(finish_kernel, columns, shards, sooner),
        out_shape=[piece] * later,
        in_specs=[vmem] * 5,
        out_specs=[vmem] * later,
        compiler_params=params,
        cost_estimate=pl.CostEstimate(
            flops=2 * later * part * depth * depth, bytes_accessed=3000000, transcendentals=0
        ),
        name="finish",
    )(keep, middle, edge, pair, weights)
    return [*first, *second]


def prepare_kernel(channels, kernel1, kernel2, qkv, kernels, padded):
    spare = channels - WIDE
    for kernel, packed in ((kernel1, kernels.at[0]), (kernel2, kernels.at[1])):
        depth = packed.shape[0]
        packed[3 * channels :, :] = jnp.zeros((depth - 3 * channels, depth), BF16)
        for r in range(3):
            for source, target in (
                (slice(0, WIDE), slice(r * WIDE, (r + 1) * WIDE)),
                (slice(WIDE, channels), slice(3 * WIDE + r * spare, 3 * WIDE + (r + 1) * spare)),
            ):
                for s in range(3):
                    packed[target, s * WIDE : (s + 1) * WIDE] = kernel[r, s, source, :WIDE]
                first, second, third = [kernel[r, s, source, WIDE:] for s in range(3)]
                packed[target, 3 * WIDE : 3 * WIDE + LANES] = jnp.concatenate([first, second], axis=1)
                packed[target, 3 * WIDE + LANES :] = jnp.concatenate(
                    [third, jnp.zeros_like(third)], axis=1
                )
    lanes = padded.shape[1] // 3
    padded[...] = jnp.zeros(padded.shape, BF16)
    for i in range(3):
        padded[:, i * lanes : i * lanes + channels] = qkv[:, i * channels : (i + 1) * channels]


def prepare(conv_first, conv_second, qkv):
    channels = qkv.shape[0]
    depth = round_up(3 * channels, WIDE)
    lanes = round_up(channels, LANES)
    vmem = pl.BlockSpec(memory_space=pltpu.VMEM)
    return pl.pallas_call(
        functools.partial(prepare_kernel, channels),
        out_shape=[
            jax.ShapeDtypeStruct((2, depth, depth), BF16),
            jax.ShapeDtypeStruct((channels, 3 * lanes), BF16),
        ],
        in_specs=[vmem] * 3,
        out_specs=[vmem] * 2,
        compiler_params=pltpu.CompilerParams(vmem_limit_bytes=14 * 1024 * 1024),
        cost_estimate=pl.CostEstimate(flops=0, bytes_accessed=10000000, transcendentals=0),
        name="prepare",
    )(conv_first, conv_second, qkv)


def norm_rows(values):
    average = jnp.mean(values, axis=-1, keepdims=True)
    centred = values - average
    spread = jnp.mean(centred * centred, axis=-1, keepdims=True)
    return (centred * lax.rsqrt(spread + 1e-05)).astype(BF16)


def feed_forward(stream, geglu_in, geglu_out, active):
    inner = geglu_out.shape[1]
    normed = norm_rows(stream.astype(F32))
    for at in range(0, inner, WIDE):
        value = jnp.dot(normed, geglu_in[:, at : at + WIDE], preferred_element_type=F32)
        gate = jnp.dot(normed, geglu_in[:, inner + at : inner + at + WIDE], preferred_element_type=F32)
        act = value * (0.5 * gate) * (1.0 + lax.erf(gate * math.sqrt(0.5)))
        active[:, at : at + WIDE] = act.astype(BF16)
    update = lax.dot_general(
        active[...], geglu_out[...], (((1,), (1,)), ((), ())), preferred_element_type=F32
    )
    return stream.astype(F32) + update


def leave(values, target):
    pixels, channels = values.shape
    if target.shape == values.shape:
        target[...] = values.astype(BF16)
        return
    spare = round_up(channels, LANES) - channels
    values = jnp.concatenate([values, jnp.zeros((pixels, spare), F32)], axis=1)
    pack_part(values, target, 0, channels)


def feed_kernel(count, *refs):
    rest, geglu_in, geglu_out = refs[:3]
    outs = refs[3 : 3 + count]
    (active,) = refs[3 + count :]
    done = feed_forward(rest[...], geglu_in, geglu_out, active)
    pixels = done.shape[0] // count
    for i in range(count):
        leave(done[i * pixels : (i + 1) * pixels, :], outs[i])


def temporal_kernel(frames, ways, sooner, *refs):
    parts = refs[:ways]
    qkv, attn_out, geglu_in, geglu_out = refs[ways : ways + 4]
    outs = refs[ways + 4 : ways + 4 + sooner]
    rest = refs[ways + 4 + sooner]
    stream, projected, mixed, active = refs[ways + 5 + sooner :]
    channels = stream.shape[1]
    pixels = stream.shape[0] // frames
    lanes = projected.shape[1] // 3

    height = dense_rows(pixels, channels)
    held = [(block, at) for block in parts for at in range(0, block.shape[0], height)]
    for f, (block, at) in enumerate(held):
        for i, first, values in unpack_part(block, at, pixels, channels):
            rows = slice(f * pixels + first, f * pixels + first + values.shape[0])
            width = min(LANES, channels - i * LANES)
            stream[rows, i * LANES : i * LANES + width] = values[:, :width].astype(BF16)
    normed = norm_rows(stream[...].astype(F32))
    projected[...] = jnp.dot(normed, qkv[...], preferred_element_type=F32).astype(BF16)

    pack = min(pixels, WIDE // frames)
    tile = frames * pack
    same = (
        lax.broadcasted_iota(jnp.int32, (tile, tile), 0) % pack
        == lax.broadcasted_iota(jnp.int32, (tile, tile), 1) % pack
    )
    lane = lax.broadcasted_iota(jnp.int32, (1, LANES), 1)
    sharing = LANES // HEAD_DIM
    for first in range(0, pixels, pack):
        places = [slice(f * pixels + first, f * pixels + first + pack) for f in range(frames)]
        for at in range(0, channels, LANES):
            query, key, value = [
                jnp.concatenate([projected[p, i * lanes + at : i * lanes + at + LANES] for p in places])
                for i in range(3)
            ]
            mix = None
            for j in range(min(sharing, (channels - at) // HEAD_DIM)):
                chosen = (lane >= j * HEAD_DIM) & (lane < (j + 1) * HEAD_DIM)
                scores = lax.dot_general(
                    query * chosen.astype(BF16),
                    key,
                    (((1,), (1,)), ((), ())),
                    preferred_element_type=F32,
                )
                scores = jnp.where(same, scores, float(jnp.finfo(F32).min))
                top = jnp.max(scores, axis=1, keepdims=True)
                powers = jnp.exp((scores - top) * HEAD_DIM ** (-0.5))
                total = jnp.sum(powers, axis=1, keepdims=True)
                weights = (powers * (1.0 / total)).astype(BF16)
                head = jnp.dot(weights, value, preferred_element_type=F32)
                mix = head if mix is None else jnp.where(chosen, head, mix)
            mix = mix.astype(BF16)
            for f, p in enumerate(places):
                mixed[p, at : at + LANES] = mix[f * pack : (f + 1) * pack]

    update = jnp.dot(mixed[:, :channels], attn_out[...], preferred_element_type=F32)
    after = (stream[...].astype(F32) + update).astype(BF16)
    rest[...] = after[sooner * pixels :, :]
    done = feed_forward(after[: sooner * pixels, :], geglu_in, geglu_out, active)
    for f in range(sooner):
        leave(done[f * pixels : (f + 1) * pixels, :], outs[f])


def temporal(parts, weights, dense):
    ways = len(parts)
    frames = lax.axis_size("shard")
    sooner = frames // 2
    later = frames - sooner
    channels = weights[0].shape[0]
    pixels = sum(part.size for part in parts) // channels // frames
    lanes = round_up(channels, LANES)
    tokens = frames * pixels
    inner = weights[3].shape[1]
    vmem = pl.BlockSpec(memory_space=pltpu.VMEM)
    piece = jax.ShapeDtypeStruct(
        (dense_rows(pixels, channels), LANES) if dense else (pixels, channels), BF16
    )
    feed_flops = 6 * pixels * channels * inner
    params = pltpu.CompilerParams(vmem_limit_bytes=14 * 1024 * 1024)
    *first, rest = pl.pallas_call(
        functools.partial(temporal_kernel, frames, ways, sooner),
        out_shape=[piece] * sooner + [jax.ShapeDtypeStruct((later * pixels, channels), BF16)],
        in_specs=[vmem] * (ways + 4),
        out_specs=[vmem] * (sooner + 1),
        scratch_shapes=[
            pltpu.VMEM((tokens, channels), BF16),
            pltpu.VMEM((tokens, 3 * lanes), BF16),
            pltpu.VMEM((tokens, lanes), BF16),
            pltpu.VMEM((sooner * pixels, inner), BF16),
        ],
        compiler_params=params,
        cost_estimate=pl.CostEstimate(
            flops=8 * tokens * channels * lanes + sooner * feed_flops,
            bytes_accessed=4000000,
            transcendentals=sooner * pixels * inner,
        ),
        name="temporal",
    )(*parts, *weights)
    second = pl.pallas_call(
        functools.partial(feed_kernel, later),
        out_shape=[piece] * later,
        in_specs=[vmem] * 3,
        out_specs=[vmem] * later,
        scratch_shapes=[pltpu.VMEM((later * pixels, inner), BF16)],
        compiler_params=params,
        cost_estimate=pl.CostEstimate(
            flops=later * feed_flops,
            bytes_accessed=3000000,
            transcendentals=later * pixels * inner,
        ),
        name="feed",
    )(rest, weights[2], weights[3])
    return [*first, *second]


def send(block, axis, distance):
    count = lax.axis_size(axis)
    return lax.ppermute(block, axis, [(i, (i + distance) % count) for i in range(count)])


def exchange(parts, back=False, across=0):
    shards, sections = lax.axis_size("shard"), lax.axis_size("section")
    arrived = []
    for part, d in zip(parts, distances(shards)):
        target = [partner(z, d, shards) for z in range(shards)]
        if back:
            target = [target.index(z) for z in range(shards)]
        if across:
            route = [
                (z * sections + s, target[z] * sections + (s + across) % sections)
                for z in range(shards)
                for s in range(sections)
            ]
            part = lax.ppermute(part, ("shard", "section"), route)
        elif d:
            part = lax.ppermute(part, "shard", list(enumerate(target)))
        arrived.append(part)
    return arrived


def join_kernel(*refs):
    *parts, whole = refs
    height = parts[0].shape[0]
    for i, part in enumerate(parts):
        whole[i * height : (i + 1) * height, :] = part[...]


def join(parts):
    vmem = pl.BlockSpec(memory_space=pltpu.VMEM)
    height, lanes = parts[0].shape
    return pl.pallas_call(
        join_kernel,
        out_shape=jax.ShapeDtypeStruct((len(parts) * height, lanes), parts[0].dtype),
        in_specs=[vmem] * len(parts),
        out_specs=vmem,
        compiler_params=pltpu.CompilerParams(vmem_limit_bytes=4 * 1024 * 1024),
        name="join",
    )(*parts)


def assemble(parts):
    size, channels = parts[0].shape
    spot = lax.axis_index("shard")
    whole = jnp.zeros((len(parts) * size, channels), parts[0].dtype)
    for part, d in zip(parts, distances(len(parts))):
        place = partner(spot, d, len(parts)) * size
        whole = lax.dynamic_update_slice_in_dim(whole, part, place, axis=0)
    return whole


def embed_time(stamps, time_weight):
    half_width = time_weight.shape[0] // 2
    frequency = jnp.exp(-math.log(10000.0) * jnp.arange(half_width, dtype=F32) / half_width)
    angles = stamps.astype(F32)[:, None] * frequency[None, :]
    sinusoid = jnp.concatenate([jnp.cos(angles), jnp.sin(angles)], axis=1)
    out = jnp.dot(jax.nn.silu(sinusoid).astype(BF16), time_weight, preferred_element_type=F32)
    return jnp.pad(out, ((0, 0), (0, round_up(out.shape[1], LANES) - out.shape[1])))


def per_device(
    features,
    timesteps,
    conv_first,
    conv_second,
    time_weight,
    qkv_weight,
    attn_out,
    geglu_in,
    geglu_out,
):
    _, _, own_rows, columns, channels = features.shape
    half = lax.axis_size("halo")
    rows = own_rows * half
    shards = lax.axis_size("shard")

    moved = send(features.reshape(own_rows * columns, channels), "section", 1)
    embeds = embed_time(timesteps[0], time_weight[0])
    spatial_weights, padded = prepare(conv_first[0], conv_second[0], qkv_weight[0])

    moved, spatial_weights, padded = lax.optimization_barrier((moved, spatial_weights, padded))
    own = [moved]
    temporal_weights = (padded, attn_out[0], geglu_in[0], geglu_out[0].T)
    for denoise_step in range(STEPS):
        last = denoise_step == STEPS - 1
        parts = spatial(
            own,
            [send(block, "halo", 1) for block in own],
            spatial_weights,
            embeds,
            denoise_step,
            rows,
            columns,
            half,
            shards,
        )
        parts = exchange(parts)
        parts = [join(parts[: shards // 2]), *parts[shards // 2 :]]
        parts = temporal(parts, temporal_weights, dense=not last)
        parts = exchange(parts, back=True, across=0 if last else 1)
        own = [join(parts[: shards // 2]), *parts[shards // 2 :]]
    return assemble(parts).reshape(features.shape)


def solution(mesh):
    return jax.shard_map(
        per_device,
        mesh=mesh,
        in_specs=(
            P(("groups", "section"), "shard", "halo", None, None),
            P(("groups", "section"), None),
            P("section", None, None, None, None),
            P("section", None, None, None, None),
            P("section", None, None),
            P("section", None, None),
            P("section", None, None),
            P("section", None, None),
            P("section", None, None),
        ),
        out_specs=P(("groups", "section"), "shard", "halo", None, None),
        check_vma=False,
    )
```

```python
import functools
import math

import jax
import jax.numpy as jnp
from jax import lax
from jax.experimental import pallas as pl
from jax.experimental.pallas import tpu as pltpu
from jax.sharding import PartitionSpec as P

HEAD_DIM = 64
GROUPS = 32
STEPS = 2
LANES = 128
WIDE = 256
F32 = jnp.float32
BF16 = jnp.bfloat16


def orders(count):
    far, near, low = list(range(count // 2, count)), [], count // 2
    while low > 1:
        near += range(low // 2, low)
        low //= 2
    return far + near + [0], near + far + [0]


def partners(spot, core, count):
    even, odd = orders(count)
    return [spot ^ jnp.where(core % 2 == 0, a, b) for a, b in zip(even, odd)]


def round_up(value, unit):
    return -(-value // unit) * unit


def dense_rows(pixels, channels):
    return pixels * channels // LANES


def pack_part(values, target, at, channels):
    pixels, full = values.shape[0], channels // LANES
    for i in range(full):
        block = values[:, i * LANES : (i + 1) * LANES].astype(BF16)
        target[at + i * pixels : at + (i + 1) * pixels, :] = block
    if channels % LANES:
        rest = values[:, full * LANES :]
        first, second = rest[: pixels // 2], rest[pixels // 2 :]
        lane = lax.broadcasted_iota(jnp.int32, (1, LANES), 1)
        both = jnp.where(lane < LANES // 2, first, pltpu.roll(second, LANES // 2, 1))
        target[at + full * pixels : at + full * pixels + pixels // 2, :] = both.astype(BF16)


def unpack_part(source, at, pixels, channels):
    full = channels // LANES
    blocks = [
        (i, 0, source[at + i * pixels : at + (i + 1) * pixels, :].astype(F32)) for i in range(full)
    ]
    if channels % LANES:
        both = source[at + full * pixels : at + full * pixels + pixels // 2, :].astype(F32)
        low = lax.broadcasted_iota(jnp.int32, (1, LANES), 1) < LANES // 2
        blocks.append((full, 0, jnp.where(low, both, 0.0)))
        blocks.append((full, pixels // 2, jnp.where(low, pltpu.roll(both, LANES // 2, 1), 0.0)))
    return blocks


def group_scale(total, square, entries, group_width, channels):
    lanes = total.shape[1]
    lane = lax.broadcasted_iota(jnp.int32, (1, lanes), 1)
    spot = lane % group_width
    row = lax.broadcasted_iota(jnp.int32, (8, 1), 0)
    both = jnp.where(
        row == 0, jnp.sum(total, axis=0, keepdims=True), jnp.sum(square, axis=0, keepdims=True)
    )
    group = both
    for k in range(1, group_width):
        group = group + jnp.where(spot + k < group_width, pltpu.roll(both, lanes - k, 1), 0.0)
        group = group + jnp.where(spot >= k, pltpu.roll(both, k, 1), 0.0)
    group = group / entries
    average = group[0:1]
    scale = lax.rsqrt(group[1:2] - average * average + 1e-05)
    scale = jnp.where(lane < channels, 0.5 * scale, 0.0)
    return scale, -average * scale


def activate(source, targets, scale, shift, rows, columns, first, start, stop):
    middle, edge, pair = targets

    def body(i, before):
        row = first - 1 + i
        inside = ((row >= 0) & (row < rows)).astype(F32)
        at = pl.multiple_of(jnp.clip(row, 0, rows - 1) * columns, columns)
        u = source[pl.ds(at, columns), :] * (scale * inside) + shift * inside
        g = u + u * jnp.tanh(u)
        to = pl.ds(pl.multiple_of(i * columns, columns), columns)
        rest = g[:, WIDE:]
        middle[to, :] = g[:, :WIDE].astype(BF16)
        edge[to, :] = rest.astype(BF16)
        pair[to, :] = (before + pltpu.roll(rest, LANES // 2, 1)).astype(BF16)
        return rest

    lax.fori_loop(start, stop, body, jnp.zeros((columns, LANES), F32), unroll=stop - start)


def convolve(targets, kernel, start, count, columns):
    middle, edge, pair = targets
    top, mid, bottom = [
        pl.ds(pl.multiple_of(start + r * columns, columns), count) for r in range(3)
    ]
    window = jnp.concatenate(
        [middle[top, :], middle[mid, :], middle[bottom, :], pair[mid, :], edge[bottom, :]], axis=1
    )
    y = jnp.dot(window, kernel[...], preferred_element_type=F32)
    column = lax.broadcasted_iota(jnp.int32, (count, 1), 0) % columns

    def from_left(values):
        return jnp.where(column == 0, 0.0, pltpu.roll(values, 1, 0))

    def from_right(values):
        return jnp.where(column == columns - 1, 0.0, pltpu.roll(values, count - 1, 0))

    wide = y[:, WIDE : 2 * WIDE] + from_left(y[:, :WIDE]) + from_right(y[:, 2 * WIDE : 3 * WIDE])
    tail = y[:, 3 * WIDE : 3 * WIDE + LANES]
    return wide, from_left(tail) + from_right(y[:, 3 * WIDE + LANES :]), tail


def convolve_part(targets, kernel, start, columns, base, target):
    pixels = base.shape[0]
    wide, narrow, tail = convolve(targets, kernel, start, pixels, columns)
    for i in range(WIDE // LANES):
        lanes = slice(i * LANES, (i + 1) * LANES)
        target[i * pixels : (i + 1) * pixels, :] = (wide[:, lanes] + base[:, lanes]).astype(BF16)
    narrow = narrow + base[:, WIDE:]
    low = lax.broadcasted_iota(jnp.int32, (1, LANES), 1) < LANES // 2
    first, second = slice(0, pixels // 2), slice(pixels // 2, pixels)
    both = jnp.where(
        low,
        narrow[first] + pltpu.roll(tail[first], LANES // 2, 1),
        pltpu.roll(narrow[second], LANES // 2, 1) + tail[second],
    )
    target[WIDE // LANES * pixels :, :] = both.astype(BF16)


def spatial_kernel(rows, half, columns, channels, group_width, step, ways, shards, sooner, *refs):
    own, other = refs[:ways], refs[ways : 2 * ways]
    kernels, embeds = refs[2 * ways : 2 * ways + 2]
    outs = refs[2 * ways + 2 : 2 * ways + 2 + sooner]
    keep, *targets = refs[2 * ways + 2 + sooner : 2 * ways + 6 + sooner]
    field, hidden, *firsts = refs[2 * ways + 6 + sooner :]
    embed = embeds[step : step + 1, :]
    lanes = field.shape[1]
    own_rows = rows // half
    part = own_rows * columns // shards
    here = lax.axis_index("halo")
    spot = lax.axis_index("shard")
    own_base = here * (own_rows * columns)
    other_base = (1 - here) * (own_rows * columns)
    zero = jnp.zeros((8, lanes), F32)

    height = dense_rows(part, channels)
    for core, base, arrived in ((here, own_base, own), (1 - here, other_base, other)):
        if ways == 1:
            place = pl.ds(pl.multiple_of(base, columns), own_rows * columns)
            field[place, lanes - LANES :] = jnp.zeros((own_rows * columns, LANES), F32)
            field[place, :channels] = arrived[0][...].astype(F32)
            continue
        held = [(block, at) for block in arrived for at in range(0, block.shape[0], height)]
        for (block, at), q in zip(held, partners(spot, core, shards)):
            for i, first, values in unpack_part(block, at, part, channels):
                place = pl.multiple_of(base + q * part + first, 8)
                field[pl.ds(place, values.shape[0]), i * LANES : (i + 1) * LANES] = values

    def sum_row(i, carry):
        total, square = carry
        chunk = field[pl.ds(pl.multiple_of(i * columns, columns), columns), :]
        chunk = chunk.reshape(columns // 8, 8, lanes)
        return total + jnp.sum(chunk, axis=0), square + jnp.sum(chunk * chunk, axis=0)

    total, square = lax.fori_loop(0, rows, sum_row, (zero, zero), unroll=4)
    entries = float(rows * columns * group_width)
    middle, edge, _ = firsts
    for pad in (0, (rows + 1) * columns):
        middle[pad : pad + columns, :] = jnp.zeros((columns, WIDE), BF16)
        edge[pad : pad + columns, :] = jnp.zeros((columns, LANES), BF16)
    scale, shift = group_scale(total, square, entries, group_width, channels)
    activate(field, firsts, scale, shift, rows, columns, 0, 1, rows + 1)

    low = lax.broadcasted_iota(jnp.int32, (1, LANES), 1) < channels - WIDE
    total, square = zero, zero
    count = min(WIDE, own_rows * columns)
    for start in range(0, rows * columns, count):
        wide, narrow, tail = convolve(firsts, kernels.at[0], start, count, columns)
        narrow = narrow + pltpu.roll(tail, LANES // 2, 1) + embed[:, WIDE:]
        chunk = jnp.concatenate([wide + embed[:, :WIDE], jnp.where(low, narrow, 0.0)], axis=1)
        hidden[start : start + count, :] = chunk
        chunk = chunk.reshape(count // 8, 8, lanes)
        total = total + jnp.sum(chunk, axis=0)
        square = square + jnp.sum(chunk * chunk, axis=0)
    scale, shift = group_scale(total, square, entries, group_width, channels)
    first_row = here * own_rows
    activate(hidden, targets, scale, shift, rows, columns, first_row, 0, own_rows + 2)
    for i, q in enumerate(partners(spot, here, shards)):
        start = q * part
        base = field[pl.ds(pl.multiple_of(own_base + start, 8), part), :]
        if i < sooner:
            convolve_part(targets, kernels.at[1], start, columns, base, outs[i])
        else:
            keep[(i - sooner) * part : (i - sooner + 1) * part, :] = base


def finish_kernel(columns, shards, sooner, keep, middle, edge, pair, kernels, *outs):
    part = keep.shape[0] // (shards - sooner)
    spot = lax.axis_index("shard")
    for i, q in enumerate(partners(spot, lax.axis_index("halo"), shards)[sooner:]):
        start = q * part
        base = keep[i * part : (i + 1) * part, :]
        convolve_part((middle, edge, pair), kernels.at[1], start, columns, base, outs[i])


def spatial(own, other, weights, embeds, step, rows, columns, half, shards):
    tokens = rows * columns
    part = tokens // half // shards
    channels = sum(block.size for block in own) // (tokens // half)
    ways = len(own)
    sooner = shards // 2
    later = shards - sooner
    lanes = round_up(channels, LANES)
    depth = weights.shape[1]
    piece = jax.ShapeDtypeStruct((dense_rows(part, channels), LANES), BF16)
    vmem = pl.BlockSpec(memory_space=pltpu.VMEM)
    params = pltpu.CompilerParams(vmem_limit_bytes=14 * 1024 * 1024)

    def active(rows_there):
        return [((rows_there + 2) * columns, width) for width in (WIDE, LANES, LANES)]

    *first, keep, middle, edge, pair = pl.pallas_call(
        functools.partial(
            spatial_kernel,
            rows,
            half,
            columns,
            channels,
            channels // GROUPS,
            step,
            ways,
            shards,
            sooner,
        ),
        out_shape=[piece] * sooner
        + [jax.ShapeDtypeStruct((later * part, lanes), F32)]
        + [jax.ShapeDtypeStruct(shape, BF16) for shape in active(rows // half)],
        in_specs=[vmem] * (2 * ways + 2),
        out_specs=[vmem] * (sooner + 4),
        scratch_shapes=[
            pltpu.VMEM((tokens, lanes), F32),
            pltpu.VMEM((tokens, lanes), F32),
            *[pltpu.VMEM(shape, BF16) for shape in active(rows)],
        ],
        compiler_params=params,
        cost_estimate=pl.CostEstimate(
            flops=3 * tokens * depth * depth,
            bytes_accessed=6000000,
            transcendentals=tokens * lanes,
        ),
        name="spatial",
    )(*own, *other, weights, embeds)
    second = pl.pallas_call(
        functools.partial(finish_kernel, columns, shards, sooner),
        out_shape=[piece] * later,
        in_specs=[vmem] * 5,
        out_specs=[vmem] * later,
        compiler_params=params,
        cost_estimate=pl.CostEstimate(
            flops=2 * later * part * depth * depth, bytes_accessed=3000000, transcendentals=0
        ),
        name="finish",
    )(keep, middle, edge, pair, weights)
    return [*first, *second]


def prepare_kernel(channels, kernel1, kernel2, qkv, kernels, padded):
    spare = channels - WIDE
    for kernel, packed in ((kernel1, kernels.at[0]), (kernel2, kernels.at[1])):
        depth = packed.shape[0]
        packed[3 * channels :, :] = jnp.zeros((depth - 3 * channels, depth), BF16)
        for r in range(3):
            for source, target in (
                (slice(0, WIDE), slice(r * WIDE, (r + 1) * WIDE)),
                (slice(WIDE, channels), slice(3 * WIDE + r * spare, 3 * WIDE + (r + 1) * spare)),
            ):
                for s in range(3):
                    packed[target, s * WIDE : (s + 1) * WIDE] = kernel[r, s, source, :WIDE]
                first, second, third = [kernel[r, s, source, WIDE:] for s in range(3)]
                packed[target, 3 * WIDE : 3 * WIDE + LANES] = jnp.concatenate([first, second], axis=1)
                packed[target, 3 * WIDE + LANES :] = jnp.concatenate(
                    [third, jnp.zeros_like(third)], axis=1
                )
    lanes = padded.shape[1] // 3
    padded[...] = jnp.zeros(padded.shape, BF16)
    for i in range(3):
        padded[:, i * lanes : i * lanes + channels] = qkv[:, i * channels : (i + 1) * channels]


def prepare(conv_first, conv_second, qkv):
    channels = qkv.shape[0]
    depth = round_up(3 * channels, WIDE)
    lanes = round_up(channels, LANES)
    vmem = pl.BlockSpec(memory_space=pltpu.VMEM)
    return pl.pallas_call(
        functools.partial(prepare_kernel, channels),
        out_shape=[
            jax.ShapeDtypeStruct((2, depth, depth), BF16),
            jax.ShapeDtypeStruct((channels, 3 * lanes), BF16),
        ],
        in_specs=[vmem] * 3,
        out_specs=[vmem] * 2,
        compiler_params=pltpu.CompilerParams(vmem_limit_bytes=14 * 1024 * 1024),
        cost_estimate=pl.CostEstimate(flops=0, bytes_accessed=10000000, transcendentals=0),
        name="prepare",
    )(conv_first, conv_second, qkv)


def norm_rows(values):
    average = jnp.mean(values, axis=-1, keepdims=True)
    centred = values - average
    spread = jnp.mean(centred * centred, axis=-1, keepdims=True)
    return (centred * lax.rsqrt(spread + 1e-05)).astype(BF16)


def feed_forward(stream, geglu_in, geglu_out, active):
    inner = geglu_out.shape[1]
    normed = norm_rows(stream.astype(F32))
    for at in range(0, inner, WIDE):
        value = jnp.dot(normed, geglu_in[:, at : at + WIDE], preferred_element_type=F32)
        gate = jnp.dot(normed, geglu_in[:, inner + at : inner + at + WIDE], preferred_element_type=F32)
        act = value * (0.5 * gate) * (1.0 + lax.erf(gate * math.sqrt(0.5)))
        active[:, at : at + WIDE] = act.astype(BF16)
    update = lax.dot_general(
        active[...], geglu_out[...], (((1,), (1,)), ((), ())), preferred_element_type=F32
    )
    return stream.astype(F32) + update


def leave(values, target):
    pixels, channels = values.shape
    spare = round_up(channels, LANES) - channels
    values = jnp.concatenate([values, jnp.zeros((pixels, spare), F32)], axis=1)
    pack_part(values, target, 0, channels)


def feed_kernel(count, *refs):
    rest, geglu_in, geglu_out = refs[:3]
    outs = refs[3 : 3 + count]
    (active,) = refs[3 + count :]
    done = feed_forward(rest[...], geglu_in, geglu_out, active)
    pixels = done.shape[0] // count
    for i in range(count):
        leave(done[i * pixels : (i + 1) * pixels, :], outs[i])


def temporal_kernel(frames, ways, sooner, *refs):
    parts = refs[:ways]
    qkv, attn_out, geglu_in, geglu_out = refs[ways : ways + 4]
    outs = refs[ways + 4 : ways + 4 + sooner]
    rest = refs[ways + 4 + sooner]
    stream, projected, mixed, active = refs[ways + 5 + sooner :]
    channels = stream.shape[1]
    pixels = stream.shape[0] // frames
    lanes = projected.shape[1] // 3

    height = dense_rows(pixels, channels)
    held = [(block, at) for block in parts for at in range(0, block.shape[0], height)]
    for f, (block, at) in enumerate(held):
        for i, first, values in unpack_part(block, at, pixels, channels):
            rows = slice(f * pixels + first, f * pixels + first + values.shape[0])
            width = min(LANES, channels - i * LANES)
            stream[rows, i * LANES : i * LANES + width] = values[:, :width].astype(BF16)
    normed = norm_rows(stream[...].astype(F32))
    projected[...] = jnp.dot(normed, qkv[...], preferred_element_type=F32).astype(BF16)

    pack = min(pixels, WIDE // frames)
    tile = frames * pack
    same = (
        lax.broadcasted_iota(jnp.int32, (tile, tile), 0) % pack
        == lax.broadcasted_iota(jnp.int32, (tile, tile), 1) % pack
    )
    lane = lax.broadcasted_iota(jnp.int32, (1, LANES), 1)
    sharing = LANES // HEAD_DIM
    chosen = [(lane >= j * HEAD_DIM) & (lane < (j + 1) * HEAD_DIM) for j in range(sharing)]
    for first in range(0, pixels, pack):
        places = [slice(f * pixels + first, f * pixels + first + pack) for f in range(frames)]

        def gather(at):
            return jnp.concatenate([projected[p, at : at + LANES] for p in places])

        heads = [(h * HEAD_DIM // LANES * LANES, h % sharing) for h in range(channels // HEAD_DIM)]
        scores = [
            lax.dot_general(
                gather(at) * chosen[j].astype(BF16),
                gather(lanes + at),
                (((1,), (1,)), ((), ())),
                preferred_element_type=F32,
            )
            for at, j in heads
        ]
        scores = [jnp.where(same, score, float(jnp.finfo(F32).min)) for score in scores]
        tops = [jnp.max(score, axis=1, keepdims=True) for score in scores]
        powers = [
            jnp.exp((score - top) * HEAD_DIM ** (-0.5)) for score, top in zip(scores, tops)
        ]
        totals = [1.0 / jnp.sum(power, axis=1, keepdims=True) for power in powers]
        weights = [(power * total).astype(BF16) for power, total in zip(powers, totals)]
        results = [
            jnp.dot(weight, gather(2 * lanes + at), preferred_element_type=F32)
            for weight, (at, _) in zip(weights, heads)
        ]
        for at in range(0, channels, LANES):
            mix = None
            for result, (spot, j) in zip(results, heads):
                if spot == at:
                    mix = result if mix is None else jnp.where(chosen[j], result, mix)
            mix = mix.astype(BF16)
            for f, p in enumerate(places):
                mixed[p, at : at + LANES] = mix[f * pack : (f + 1) * pack]

    update = jnp.dot(mixed[:, :channels], attn_out[...], preferred_element_type=F32)
    after = (stream[...].astype(F32) + update).astype(BF16)
    rest[...] = after[sooner * pixels :, :]
    done = feed_forward(after[: sooner * pixels, :], geglu_in, geglu_out, active)
    for f in range(sooner):
        leave(done[f * pixels : (f + 1) * pixels, :], outs[f])


def temporal(parts, weights):
    ways = len(parts)
    frames = lax.axis_size("shard")
    sooner = frames // 2
    later = frames - sooner
    channels = weights[0].shape[0]
    pixels = sum(part.size for part in parts) // channels // frames
    lanes = round_up(channels, LANES)
    tokens = frames * pixels
    inner = weights[3].shape[1]
    vmem = pl.BlockSpec(memory_space=pltpu.VMEM)
    piece = jax.ShapeDtypeStruct((dense_rows(pixels, channels), LANES), BF16)
    feed_flops = 6 * pixels * channels * inner
    params = pltpu.CompilerParams(vmem_limit_bytes=14 * 1024 * 1024)
    *first, rest = pl.pallas_call(
        functools.partial(temporal_kernel, frames, ways, sooner),
        out_shape=[piece] * sooner + [jax.ShapeDtypeStruct((later * pixels, channels), BF16)],
        in_specs=[vmem] * (ways + 4),
        out_specs=[vmem] * (sooner + 1),
        scratch_shapes=[
            pltpu.VMEM((tokens, channels), BF16),
            pltpu.VMEM((tokens, 3 * lanes), BF16),
            pltpu.VMEM((tokens, lanes), BF16),
            pltpu.VMEM((sooner * pixels, inner), BF16),
        ],
        compiler_params=params,
        cost_estimate=pl.CostEstimate(
            flops=8 * tokens * channels * lanes + sooner * feed_flops,
            bytes_accessed=4000000,
            transcendentals=sooner * pixels * inner,
        ),
        name="temporal",
    )(*parts, *weights)
    second = pl.pallas_call(
        functools.partial(feed_kernel, later),
        out_shape=[piece] * later,
        in_specs=[vmem] * 3,
        out_specs=[vmem] * later,
        scratch_shapes=[pltpu.VMEM((later * pixels, inner), BF16)],
        compiler_params=params,
        cost_estimate=pl.CostEstimate(
            flops=later * feed_flops,
            bytes_accessed=3000000,
            transcendentals=later * pixels * inner,
        ),
        name="feed",
    )(rest, weights[2], weights[3])
    return [*first, *second]


def send(block, axis, distance):
    count = lax.axis_size(axis)
    return lax.ppermute(block, axis, [(i, (i + distance) % count) for i in range(count)])


def exchange(parts, across=0):
    sizes = [lax.axis_size(axis) for axis in ("shard", "section", "halo")]
    shards, sections, cores = sizes
    arrived = []
    for part, *distance in zip(parts, *orders(shards)):
        if across or any(distance):
            route = [
                (
                    (z * sections + s) * cores + h,
                    ((z ^ distance[h % 2]) * sections + (s + across) % sections) * cores + h,
                )
                for z in range(shards)
                for s in range(sections)
                for h in range(cores)
            ]
            part = lax.ppermute(part, ("shard", "section", "halo"), route)
        arrived.append(part)
    return arrived


def join_kernel(*refs):
    *parts, whole = refs
    height = parts[0].shape[0]
    for i, part in enumerate(parts):
        whole[i * height : (i + 1) * height, :] = part[...]


def join(parts):
    vmem = pl.BlockSpec(memory_space=pltpu.VMEM)
    height, lanes = parts[0].shape
    return pl.pallas_call(
        join_kernel,
        out_shape=jax.ShapeDtypeStruct((len(parts) * height, lanes), parts[0].dtype),
        in_specs=[vmem] * len(parts),
        out_specs=vmem,
        compiler_params=pltpu.CompilerParams(vmem_limit_bytes=4 * 1024 * 1024),
        name="join",
    )(*parts)


def unpack_kernel(shards, *refs):
    parts, (whole,) = refs[:-1], refs[-1:]
    tokens, channels = whole.shape
    pixels = tokens // shards
    height = dense_rows(pixels, channels)
    held = [(block, at) for block in parts for at in range(0, block.shape[0], height)]
    places = partners(lax.axis_index("shard"), lax.axis_index("halo"), shards)
    for (block, at), q in zip(held, places):
        for i, first, values in unpack_part(block, at, pixels, channels):
            place = pl.multiple_of(q * pixels + first, 16)
            width = min(LANES, channels - i * LANES)
            lanes = slice(i * LANES, i * LANES + width)
            whole[pl.ds(place, values.shape[0]), lanes] = values[:, :width].astype(BF16)


def unpack(parts, shards, tokens, channels):
    vmem = pl.BlockSpec(memory_space=pltpu.VMEM)
    return pl.pallas_call(
        functools.partial(unpack_kernel, shards),
        out_shape=jax.ShapeDtypeStruct((tokens, channels), BF16),
        in_specs=[vmem] * len(parts),
        out_specs=vmem,
        compiler_params=pltpu.CompilerParams(vmem_limit_bytes=4 * 1024 * 1024),
        name="unpack",
    )(*parts)


def embed_time(stamps, time_weight):
    half_width = time_weight.shape[0] // 2
    frequency = jnp.exp(-math.log(10000.0) * jnp.arange(half_width, dtype=F32) / half_width)
    angles = stamps.astype(F32)[:, None] * frequency[None, :]
    sinusoid = jnp.concatenate([jnp.cos(angles), jnp.sin(angles)], axis=1)
    out = jnp.dot(jax.nn.silu(sinusoid).astype(BF16), time_weight, preferred_element_type=F32)
    return jnp.pad(out, ((0, 0), (0, round_up(out.shape[1], LANES) - out.shape[1])))


def per_device(
    features,
    timesteps,
    conv_first,
    conv_second,
    time_weight,
    qkv_weight,
    attn_out,
    geglu_in,
    geglu_out,
):
    _, _, own_rows, columns, channels = features.shape
    half = lax.axis_size("halo")
    rows = own_rows * half
    shards = lax.axis_size("shard")

    moved = send(features.reshape(own_rows * columns, channels), "section", 1)
    embeds = embed_time(timesteps[0], time_weight[0])
    spatial_weights, padded = prepare(conv_first[0], conv_second[0], qkv_weight[0])

    moved, spatial_weights, padded = lax.optimization_barrier((moved, spatial_weights, padded))
    own = [moved]
    temporal_weights = (padded, attn_out[0], geglu_in[0], geglu_out[0].T)
    for denoise_step in range(STEPS):
        last = denoise_step == STEPS - 1
        parts = spatial(
            own,
            [send(block, "halo", 1) for block in own],
            spatial_weights,
            embeds,
            denoise_step,
            rows,
            columns,
            half,
            shards,
        )
        parts = exchange(parts)
        parts = [join(parts[: shards // 2]), *parts[shards // 2 :]]
        parts = temporal(parts, temporal_weights)
        parts = exchange(parts, across=0 if last else 1)
        own = [join(parts[: shards // 2]), *parts[shards // 2 :]]
    return unpack(own, shards, own_rows * columns, channels).reshape(features.shape)


def solution(mesh):
    return jax.shard_map(
        per_device,
        mesh=mesh,
        in_specs=(
            P(("groups", "section"), "shard", "halo", None, None),
            P(("groups", "section"), None),
            P("section", None, None, None, None),
            P("section", None, None, None, None),
            P("section", None, None),
            P("section", None, None),
            P("section", None, None),
            P("section", None, None),
            P("section", None, None),
        ),
        out_specs=P(("groups", "section"), "shard", "halo", None, None),
        check_vma=False,
    )
```

```python
import functools
import math

import jax
import jax.numpy as jnp
from jax import lax
from jax.experimental import pallas as pl
from jax.experimental.pallas import tpu as pltpu
from jax.sharding import PartitionSpec as P

HEAD_DIM = 64
GROUPS = 32
STEPS = 2
LANES = 128
WIDE = 256
F32 = jnp.float32
BF16 = jnp.bfloat16


def order_out(count):
    return [d for d in reversed(range(count)) if d % 2] + [
        d for d in reversed(range(count)) if d % 2 == 0
    ]


def order_back(count):
    return order_out(count)


def round_up(value, unit):
    return -(-value // unit) * unit


def dense_rows(pixels, channels):
    return pixels * channels // LANES


def pack_part(values, target, at, channels):
    pixels, full = values.shape[0], channels // LANES
    for i in range(full):
        block = values[:, i * LANES : (i + 1) * LANES].astype(BF16)
        target[at + i * pixels : at + (i + 1) * pixels, :] = block
    if channels % LANES:
        rest = values[:, full * LANES :]
        first, second = rest[: pixels // 2], rest[pixels // 2 :]
        lane = lax.broadcasted_iota(jnp.int32, (1, LANES), 1)
        both = jnp.where(lane < LANES // 2, first, pltpu.roll(second, LANES // 2, 1))
        target[at + full * pixels : at + full * pixels + pixels // 2, :] = both.astype(BF16)


def unpack_part(source, at, pixels, channels):
    full = channels // LANES
    blocks = [
        (i, 0, source[at + i * pixels : at + (i + 1) * pixels, :].astype(F32)) for i in range(full)
    ]
    if channels % LANES:
        both = source[at + full * pixels : at + full * pixels + pixels // 2, :].astype(F32)
        low = lax.broadcasted_iota(jnp.int32, (1, LANES), 1) < LANES // 2
        blocks.append((full, 0, jnp.where(low, both, 0.0)))
        blocks.append((full, pixels // 2, jnp.where(low, pltpu.roll(both, LANES // 2, 1), 0.0)))
    return blocks


def group_scale(total, square, entries, group_width, channels):
    lanes = total.shape[1]
    lane = lax.broadcasted_iota(jnp.int32, (1, lanes), 1)
    spot = lane % group_width
    row = lax.broadcasted_iota(jnp.int32, (8, 1), 0)
    both = jnp.where(
        row == 0, jnp.sum(total, axis=0, keepdims=True), jnp.sum(square, axis=0, keepdims=True)
    )
    group = both
    for k in range(1, group_width):
        group = group + jnp.where(spot + k < group_width, pltpu.roll(both, lanes - k, 1), 0.0)
        group = group + jnp.where(spot >= k, pltpu.roll(both, k, 1), 0.0)
    group = group / entries
    average = group[0:1]
    scale = lax.rsqrt(group[1:2] - average * average + 1e-05)
    scale = jnp.where(lane < channels, 0.5 * scale, 0.0)
    return scale, -average * scale


def activate(source, targets, scale, shift, rows, columns, first, start, stop):
    middle, edge, pair = targets

    def body(i, before):
        row = first - 1 + i
        inside = ((row >= 0) & (row < rows)).astype(F32)
        at = pl.multiple_of(jnp.clip(row, 0, rows - 1) * columns, columns)
        u = source[pl.ds(at, columns), :] * (scale * inside) + shift * inside
        g = u + u * jnp.tanh(u)
        to = pl.ds(pl.multiple_of(i * columns, columns), columns)
        rest = g[:, WIDE:]
        middle[to, :] = g[:, :WIDE].astype(BF16)
        edge[to, :] = rest.astype(BF16)
        pair[to, :] = (before + pltpu.roll(rest, LANES // 2, 1)).astype(BF16)
        return rest

    lax.fori_loop(start, stop, body, jnp.zeros((columns, LANES), F32), unroll=stop - start)


def convolve(targets, kernel, start, count, columns):
    middle, edge, pair = targets
    top, mid, bottom = [
        pl.ds(pl.multiple_of(start + r * columns, columns), count) for r in range(3)
    ]
    window = jnp.concatenate(
        [middle[top, :], middle[mid, :], middle[bottom, :], pair[mid, :], edge[bottom, :]], axis=1
    )
    y = jnp.dot(window, kernel[...], preferred_element_type=F32)
    column = lax.broadcasted_iota(jnp.int32, (count, 1), 0) % columns

    def from_left(values):
        return jnp.where(column == 0, 0.0, pltpu.roll(values, 1, 0))

    def from_right(values):
        return jnp.where(column == columns - 1, 0.0, pltpu.roll(values, count - 1, 0))

    wide = y[:, WIDE : 2 * WIDE] + from_left(y[:, :WIDE]) + from_right(y[:, 2 * WIDE : 3 * WIDE])
    tail = y[:, 3 * WIDE : 3 * WIDE + LANES]
    return wide, from_left(tail) + from_right(y[:, 3 * WIDE + LANES :]), tail


def convolve_part(targets, kernel, start, columns, base, target):
    pixels = base.shape[0]
    wide, narrow, tail = convolve(targets, kernel, start, pixels, columns)
    for i in range(WIDE // LANES):
        lanes = slice(i * LANES, (i + 1) * LANES)
        target[i * pixels : (i + 1) * pixels, :] = (wide[:, lanes] + base[:, lanes]).astype(BF16)
    narrow = narrow + base[:, WIDE:]
    low = lax.broadcasted_iota(jnp.int32, (1, LANES), 1) < LANES // 2
    first, second = slice(0, pixels // 2), slice(pixels // 2, pixels)
    both = jnp.where(
        low,
        narrow[first] + pltpu.roll(tail[first], LANES // 2, 1),
        pltpu.roll(narrow[second], LANES // 2, 1) + tail[second],
    )
    target[WIDE // LANES * pixels :, :] = both.astype(BF16)


def spatial_kernel(rows, half, columns, channels, group_width, step, ways, shards, sooner, *refs):
    own, other = refs[:ways], refs[ways : 2 * ways]
    kernels, embeds = refs[2 * ways : 2 * ways + 2]
    outs = refs[2 * ways + 2 : 2 * ways + 2 + sooner]
    keep, *targets = refs[2 * ways + 2 + sooner : 2 * ways + 6 + sooner]
    field, hidden, *firsts = refs[2 * ways + 6 + sooner :]
    embed = embeds[step : step + 1, :]
    lanes = field.shape[1]
    own_rows = rows // half
    part = own_rows * columns // shards
    here = lax.axis_index("halo")
    spot = lax.axis_index("shard")
    own_base = here * (own_rows * columns)
    other_base = (1 - here) * (own_rows * columns)
    zero = jnp.zeros((8, lanes), F32)

    height = dense_rows(part, channels)
    for base, arrived in ((own_base, own), (other_base, other)):
        if ways == 1:
            place = pl.ds(pl.multiple_of(base, columns), own_rows * columns)
            field[place, lanes - LANES :] = jnp.zeros((own_rows * columns, LANES), F32)
            field[place, :channels] = arrived[0][...].astype(F32)
            continue
        held = [(block, at) for block in arrived for at in range(0, block.shape[0], height)]
        for (block, at), d in zip(held, order_back(shards)):
            for i, first, values in unpack_part(block, at, part, channels):
                place = pl.multiple_of(base + (spot ^ d) * part + first, 8)
                field[pl.ds(place, values.shape[0]), i * LANES : (i + 1) * LANES] = values

    def sum_row(i, carry):
        total, square = carry
        chunk = field[pl.ds(pl.multiple_of(i * columns, columns), columns), :]
        chunk = chunk.reshape(columns // 8, 8, lanes)
        return total + jnp.sum(chunk, axis=0), square + jnp.sum(chunk * chunk, axis=0)

    total, square = lax.fori_loop(0, rows, sum_row, (zero, zero), unroll=4)
    entries = float(rows * columns * group_width)
    middle, edge, _ = firsts
    for pad in (0, (rows + 1) * columns):
        middle[pad : pad + columns, :] = jnp.zeros((columns, WIDE), BF16)
        edge[pad : pad + columns, :] = jnp.zeros((columns, LANES), BF16)
    scale, shift = group_scale(total, square, entries, group_width, channels)
    activate(field, firsts, scale, shift, rows, columns, 0, 1, rows + 1)

    low = lax.broadcasted_iota(jnp.int32, (1, LANES), 1) < channels - WIDE
    total, square = zero, zero
    count = min(WIDE, own_rows * columns)
    for start in range(0, rows * columns, count):
        wide, narrow, tail = convolve(firsts, kernels.at[0], start, count, columns)
        narrow = narrow + pltpu.roll(tail, LANES // 2, 1) + embed[:, WIDE:]
        chunk = jnp.concatenate([wide + embed[:, :WIDE], jnp.where(low, narrow, 0.0)], axis=1)
        hidden[start : start + count, :] = chunk
        chunk = chunk.reshape(count // 8, 8, lanes)
        total = total + jnp.sum(chunk, axis=0)
        square = square + jnp.sum(chunk * chunk, axis=0)
    scale, shift = group_scale(total, square, entries, group_width, channels)
    first_row = here * own_rows
    activate(hidden, targets, scale, shift, rows, columns, first_row, 0, own_rows + 2)
    for i, d in enumerate(order_out(shards)):
        start = (spot ^ d) * part
        base = field[pl.ds(pl.multiple_of(own_base + start, 8), part), :]
        if i < sooner:
            convolve_part(targets, kernels.at[1], start, columns, base, outs[i])
        else:
            keep[(i - sooner) * part : (i - sooner + 1) * part, :] = base


def finish_kernel(columns, shards, sooner, keep, middle, edge, pair, kernels, *outs):
    part = keep.shape[0] // (shards - sooner)
    spot = lax.axis_index("shard")
    for i, d in enumerate(order_out(shards)[sooner:]):
        start = (spot ^ d) * part
        base = keep[i * part : (i + 1) * part, :]
        convolve_part((middle, edge, pair), kernels.at[1], start, columns, base, outs[i])


def spatial(own, other, weights, embeds, step, rows, columns, half, shards):
    tokens = rows * columns
    part = tokens // half // shards
    channels = sum(block.size for block in own) // (tokens // half)
    ways = len(own)
    sooner = shards // 2
    later = shards - sooner
    lanes = round_up(channels, LANES)
    depth = weights.shape[1]
    piece = jax.ShapeDtypeStruct((dense_rows(part, channels), LANES), BF16)
    vmem = pl.BlockSpec(memory_space=pltpu.VMEM)
    params = pltpu.CompilerParams(vmem_limit_bytes=14 * 1024 * 1024)

    def active(rows_there):
        return [((rows_there + 2) * columns, width) for width in (WIDE, LANES, LANES)]

    *first, keep, middle, edge, pair = pl.pallas_call(
        functools.partial(
            spatial_kernel,
            rows,
            half,
            columns,
            channels,
            channels // GROUPS,
            step,
            ways,
            shards,
            sooner,
        ),
        out_shape=[piece] * sooner
        + [jax.ShapeDtypeStruct((later * part, lanes), F32)]
        + [jax.ShapeDtypeStruct(shape, BF16) for shape in active(rows // half)],
        in_specs=[vmem] * (2 * ways + 2),
        out_specs=[vmem] * (sooner + 4),
        scratch_shapes=[
            pltpu.VMEM((tokens, lanes), F32),
            pltpu.VMEM((tokens, lanes), F32),
            *[pltpu.VMEM(shape, BF16) for shape in active(rows)],
        ],
        compiler_params=params,
        cost_estimate=pl.CostEstimate(
            flops=3 * tokens * depth * depth,
            bytes_accessed=6000000,
            transcendentals=tokens * lanes,
        ),
        name="spatial",
    )(*own, *other, weights, embeds)
    second = pl.pallas_call(
        functools.partial(finish_kernel, columns, shards, sooner),
        out_shape=[piece] * later,
        in_specs=[vmem] * 5,
        out_specs=[vmem] * later,
        compiler_params=params,
        cost_estimate=pl.CostEstimate(
            flops=2 * later * part * depth * depth, bytes_accessed=3000000, transcendentals=0
        ),
        name="finish",
    )(keep, middle, edge, pair, weights)
    return [*first, *second]


def prepare_kernel(channels, kernel1, kernel2, qkv, kernels, padded):
    spare = channels - WIDE
    for kernel, packed in ((kernel1, kernels.at[0]), (kernel2, kernels.at[1])):
        depth = packed.shape[0]
        packed[3 * channels :, :] = jnp.zeros((depth - 3 * channels, depth), BF16)
        for r in range(3):
            for source, target in (
                (slice(0, WIDE), slice(r * WIDE, (r + 1) * WIDE)),
                (slice(WIDE, channels), slice(3 * WIDE + r * spare, 3 * WIDE + (r + 1) * spare)),
            ):
                for s in range(3):
                    packed[target, s * WIDE : (s + 1) * WIDE] = kernel[r, s, source, :WIDE]
                first, second, third = [kernel[r, s, source, WIDE:] for s in range(3)]
                packed[target, 3 * WIDE : 3 * WIDE + LANES] = jnp.concatenate([first, second], axis=1)
                packed[target, 3 * WIDE + LANES :] = jnp.concatenate(
                    [third, jnp.zeros_like(third)], axis=1
                )
    lanes = padded.shape[1] // 3
    padded[...] = jnp.zeros(padded.shape, BF16)
    for i in range(3):
        padded[:, i * lanes : i * lanes + channels] = qkv[:, i * channels : (i + 1) * channels]


def prepare(conv_first, conv_second, qkv):
    channels = qkv.shape[0]
    depth = round_up(3 * channels, WIDE)
    lanes = round_up(channels, LANES)
    vmem = pl.BlockSpec(memory_space=pltpu.VMEM)
    return pl.pallas_call(
        functools.partial(prepare_kernel, channels),
        out_shape=[
            jax.ShapeDtypeStruct((2, depth, depth), BF16),
            jax.ShapeDtypeStruct((channels, 3 * lanes), BF16),
        ],
        in_specs=[vmem] * 3,
        out_specs=[vmem] * 2,
        compiler_params=pltpu.CompilerParams(vmem_limit_bytes=14 * 1024 * 1024),
        cost_estimate=pl.CostEstimate(flops=0, bytes_accessed=10000000, transcendentals=0),
        name="prepare",
    )(conv_first, conv_second, qkv)


def norm_rows(values):
    average = jnp.mean(values, axis=-1, keepdims=True)
    centred = values - average
    spread = jnp.mean(centred * centred, axis=-1, keepdims=True)
    return (centred * lax.rsqrt(spread + 1e-05)).astype(BF16)


def feed_forward(stream, geglu_in, geglu_out, active):
    inner = geglu_out.shape[1]
    normed = norm_rows(stream.astype(F32))
    for at in range(0, inner, WIDE):
        value = jnp.dot(normed, geglu_in[:, at : at + WIDE], preferred_element_type=F32)
        gate = jnp.dot(normed, geglu_in[:, inner + at : inner + at + WIDE], preferred_element_type=F32)
        act = value * (0.5 * gate) * (1.0 + lax.erf(gate * math.sqrt(0.5)))
        active[:, at : at + WIDE] = act.astype(BF16)
    update = lax.dot_general(
        active[...], geglu_out[...], (((1,), (1,)), ((), ())), preferred_element_type=F32
    )
    return stream.astype(F32) + update


def leave(values, target):
    pixels, channels = values.shape
    spare = round_up(channels, LANES) - channels
    values = jnp.concatenate([values, jnp.zeros((pixels, spare), F32)], axis=1)
    pack_part(values, target, 0, channels)


def feed_kernel(count, *refs):
    rest, geglu_in, geglu_out = refs[:3]
    outs = refs[3 : 3 + count]
    (active,) = refs[3 + count :]
    done = feed_forward(rest[...], geglu_in, geglu_out, active)
    pixels = done.shape[0] // count
    for i in range(count):
        leave(done[i * pixels : (i + 1) * pixels, :], outs[i])


def temporal_kernel(frames, ways, sooner, *refs):
    parts = refs[:ways]
    qkv, attn_out, geglu_in, geglu_out = refs[ways : ways + 4]
    outs = refs[ways + 4 : ways + 4 + sooner]
    rest = refs[ways + 4 + sooner]
    stream, projected, mixed, active = refs[ways + 5 + sooner :]
    channels = stream.shape[1]
    pixels = stream.shape[0] // frames
    lanes = projected.shape[1] // 3

    height = dense_rows(pixels, channels)
    held = [(block, at) for block in parts for at in range(0, block.shape[0], height)]
    for (block, at), d in zip(held, order_out(frames)):
        f = order_back(frames).index(d)
        for i, first, values in unpack_part(block, at, pixels, channels):
            rows = slice(f * pixels + first, f * pixels + first + values.shape[0])
            width = min(LANES, channels - i * LANES)
            stream[rows, i * LANES : i * LANES + width] = values[:, :width].astype(BF16)
    normed = norm_rows(stream[...].astype(F32))
    projected[...] = jnp.dot(normed, qkv[...], preferred_element_type=F32).astype(BF16)

    pack = min(pixels, WIDE // frames)
    tile = frames * pack
    same = (
        lax.broadcasted_iota(jnp.int32, (tile, tile), 0) % pack
        == lax.broadcasted_iota(jnp.int32, (tile, tile), 1) % pack
    )
    lane = lax.broadcasted_iota(jnp.int32, (1, LANES), 1)
    sharing = LANES // HEAD_DIM
    chosen = [(lane >= j * HEAD_DIM) & (lane < (j + 1) * HEAD_DIM) for j in range(sharing)]
    for first in range(0, pixels, pack):
        places = [slice(f * pixels + first, f * pixels + first + pack) for f in range(frames)]

        def gather(at):
            return jnp.concatenate([projected[p, at : at + LANES] for p in places])

        heads = [(h * HEAD_DIM // LANES * LANES, h % sharing) for h in range(channels // HEAD_DIM)]
        scores = [
            lax.dot_general(
                gather(at) * chosen[j].astype(BF16),
                gather(lanes + at),
                (((1,), (1,)), ((), ())),
                preferred_element_type=F32,
            )
            for at, j in heads
        ]
        scores = [jnp.where(same, score, float(jnp.finfo(F32).min)) for score in scores]
        tops = [jnp.max(score, axis=1, keepdims=True) for score in scores]
        powers = [
            jnp.exp((score - top) * HEAD_DIM ** (-0.5)) for score, top in zip(scores, tops)
        ]
        totals = [1.0 / jnp.sum(power, axis=1, keepdims=True) for power in powers]
        weights = [(power * total).astype(BF16) for power, total in zip(powers, totals)]
        results = [
            jnp.dot(weight, gather(2 * lanes + at), preferred_element_type=F32)
            for weight, (at, _) in zip(weights, heads)
        ]
        for at in range(0, channels, LANES):
            mix = None
            for result, (spot, j) in zip(results, heads):
                if spot == at:
                    mix = result if mix is None else jnp.where(chosen[j], result, mix)
            mix = mix.astype(BF16)
            for f, p in enumerate(places):
                mixed[p, at : at + LANES] = mix[f * pack : (f + 1) * pack]

    update = jnp.dot(mixed[:, :channels], attn_out[...], preferred_element_type=F32)
    after = (stream[...].astype(F32) + update).astype(BF16)
    rest[...] = after[sooner * pixels :, :]
    done = feed_forward(after[: sooner * pixels, :], geglu_in, geglu_out, active)
    for f in range(sooner):
        leave(done[f * pixels : (f + 1) * pixels, :], outs[f])


def temporal(parts, weights):
    ways = len(parts)
    frames = lax.axis_size("shard")
    sooner = frames // 2
    later = frames - sooner
    channels = weights[0].shape[0]
    pixels = sum(part.size for part in parts) // channels // frames
    lanes = round_up(channels, LANES)
    tokens = frames * pixels
    inner = weights[3].shape[1]
    vmem = pl.BlockSpec(memory_space=pltpu.VMEM)
    piece = jax.ShapeDtypeStruct((dense_rows(pixels, channels), LANES), BF16)
    feed_flops = 6 * pixels * channels * inner
    params = pltpu.CompilerParams(vmem_limit_bytes=14 * 1024 * 1024)
    *first, rest = pl.pallas_call(
        functools.partial(temporal_kernel, frames, ways, sooner),
        out_shape=[piece] * sooner + [jax.ShapeDtypeStruct((later * pixels, channels), BF16)],
        in_specs=[vmem] * (ways + 4),
        out_specs=[vmem] * (sooner + 1),
        scratch_shapes=[
            pltpu.VMEM((tokens, channels), BF16),
            pltpu.VMEM((tokens, 3 * lanes), BF16),
            pltpu.VMEM((tokens, lanes), BF16),
            pltpu.VMEM((sooner * pixels, inner), BF16),
        ],
        compiler_params=params,
        cost_estimate=pl.CostEstimate(
            flops=8 * tokens * channels * lanes + sooner * feed_flops,
            bytes_accessed=4000000,
            transcendentals=sooner * pixels * inner,
        ),
        name="temporal",
    )(*parts, *weights)
    second = pl.pallas_call(
        functools.partial(feed_kernel, later),
        out_shape=[piece] * later,
        in_specs=[vmem] * 3,
        out_specs=[vmem] * later,
        scratch_shapes=[pltpu.VMEM((later * pixels, inner), BF16)],
        compiler_params=params,
        cost_estimate=pl.CostEstimate(
            flops=later * feed_flops,
            bytes_accessed=3000000,
            transcendentals=later * pixels * inner,
        ),
        name="feed",
    )(rest, weights[2], weights[3])
    return [*first, *second]


def send(block, axis, distance):
    count = lax.axis_size(axis)
    return lax.ppermute(block, axis, [(i, (i + distance) % count) for i in range(count)])


def exchange(parts, order, across=0):
    shards, sections = lax.axis_size("shard"), lax.axis_size("section")
    arrived = []
    for part, d in zip(parts, order):
        if across:
            route = [
                (z * sections + s, (z ^ d) * sections + (s + across) % sections)
                for z in range(shards)
                for s in range(sections)
            ]
            part = lax.ppermute(part, ("shard", "section"), route)
        elif d:
            part = lax.ppermute(part, "shard", [(z, z ^ d) for z in range(shards)])
        arrived.append(part)
    return arrived


def join_kernel(*refs):
    *parts, whole = refs
    height = parts[0].shape[0]
    for i, part in enumerate(parts):
        whole[i * height : (i + 1) * height, :] = part[...]


def join(parts):
    vmem = pl.BlockSpec(memory_space=pltpu.VMEM)
    height, lanes = parts[0].shape
    return pl.pallas_call(
        join_kernel,
        out_shape=jax.ShapeDtypeStruct((len(parts) * height, lanes), parts[0].dtype),
        in_specs=[vmem] * len(parts),
        out_specs=vmem,
        compiler_params=pltpu.CompilerParams(vmem_limit_bytes=4 * 1024 * 1024),
        name="join",
    )(*parts)


def unpack_kernel(shards, *refs):
    parts, (whole,) = refs[:-1], refs[-1:]
    tokens, channels = whole.shape
    pixels = tokens // shards
    height = dense_rows(pixels, channels)
    held = [(block, at) for block in parts for at in range(0, block.shape[0], height)]
    spot = lax.axis_index("shard")
    for (block, at), d in zip(held, order_back(shards)):
        for i, first, values in unpack_part(block, at, pixels, channels):
            place = pl.multiple_of((spot ^ d) * pixels + first, 16)
            width = min(LANES, channels - i * LANES)
            lanes = slice(i * LANES, i * LANES + width)
            whole[pl.ds(place, values.shape[0]), lanes] = values[:, :width].astype(BF16)


def unpack(parts, shards, tokens, channels):
    vmem = pl.BlockSpec(memory_space=pltpu.VMEM)
    return pl.pallas_call(
        functools.partial(unpack_kernel, shards),
        out_shape=jax.ShapeDtypeStruct((tokens, channels), BF16),
        in_specs=[vmem] * len(parts),
        out_specs=vmem,
        compiler_params=pltpu.CompilerParams(vmem_limit_bytes=4 * 1024 * 1024),
        name="unpack",
    )(*parts)


def embed_time(stamps, time_weight):
    half_width = time_weight.shape[0] // 2
    frequency = jnp.exp(-math.log(10000.0) * jnp.arange(half_width, dtype=F32) / half_width)
    angles = stamps.astype(F32)[:, None] * frequency[None, :]
    sinusoid = jnp.concatenate([jnp.cos(angles), jnp.sin(angles)], axis=1)
    out = jnp.dot(jax.nn.silu(sinusoid).astype(BF16), time_weight, preferred_element_type=F32)
    return jnp.pad(out, ((0, 0), (0, round_up(out.shape[1], LANES) - out.shape[1])))


def per_device(
    features,
    timesteps,
    conv_first,
    conv_second,
    time_weight,
    qkv_weight,
    attn_out,
    geglu_in,
    geglu_out,
):
    _, _, own_rows, columns, channels = features.shape
    half = lax.axis_size("halo")
    rows = own_rows * half
    shards = lax.axis_size("shard")

    moved = send(features.reshape(own_rows * columns, channels), "section", 1)
    embeds = embed_time(timesteps[0], time_weight[0])
    spatial_weights, padded = prepare(conv_first[0], conv_second[0], qkv_weight[0])

    moved, spatial_weights, padded = lax.optimization_barrier((moved, spatial_weights, padded))
    own = [moved]
    temporal_weights = (padded, attn_out[0], geglu_in[0], geglu_out[0].T)
    for denoise_step in range(STEPS):
        last = denoise_step == STEPS - 1
        parts = spatial(
            own,
            [send(block, "halo", 1) for block in own],
            spatial_weights,
            embeds,
            denoise_step,
            rows,
            columns,
            half,
            shards,
        )
        parts = exchange(parts, order_out(shards))
        parts = [join(parts[: shards // 2]), *parts[shards // 2 :]]
        parts = temporal(parts, temporal_weights)
        parts = exchange(parts, order_back(shards), across=0 if last else 1)
        own = [join(parts[: shards // 2]), *parts[shards // 2 :]]
    return unpack(own, shards, own_rows * columns, channels).reshape(features.shape)


def solution(mesh):
    return jax.shard_map(
        per_device,
        mesh=mesh,
        in_specs=(
            P(("groups", "section"), "shard", "halo", None, None),
            P(("groups", "section"), None),
            P("section", None, None, None, None),
            P("section", None, None, None, None),
            P("section", None, None),
            P("section", None, None),
            P("section", None, None),
            P("section", None, None),
            P("section", None, None),
        ),
        out_specs=P(("groups", "section"), "shard", "halo", None, None),
        check_vma=False,
    )
```

```python
import functools
import math

import jax
import jax.numpy as jnp
from jax import lax
from jax.experimental import pallas as pl
from jax.experimental.pallas import tpu as pltpu
from jax.sharding import PartitionSpec as P

HEAD_DIM = 64
GROUPS = 32
STEPS = 2
LANES = 128
WIDE = 256
F32 = jnp.float32
BF16 = jnp.bfloat16


def order_out(count):
    return [d for d in reversed(range(count)) if d % 2] + [
        d for d in reversed(range(count)) if d % 2 == 0
    ]


def order_back(count):
    return order_out(count)


def round_up(value, unit):
    return -(-value // unit) * unit


def dense_rows(pixels, channels):
    return pixels * channels // LANES


def pack_part(values, target, at, channels):
    pixels, full = values.shape[0], channels // LANES
    for i in range(full):
        block = values[:, i * LANES : (i + 1) * LANES].astype(BF16)
        target[at + i * pixels : at + (i + 1) * pixels, :] = block
    if channels % LANES:
        rest = values[:, full * LANES :]
        first, second = rest[: pixels // 2], rest[pixels // 2 :]
        lane = lax.broadcasted_iota(jnp.int32, (1, LANES), 1)
        both = jnp.where(lane < LANES // 2, first, pltpu.roll(second, LANES // 2, 1))
        target[at + full * pixels : at + full * pixels + pixels // 2, :] = both.astype(BF16)


def unpack_part(source, at, pixels, channels):
    full = channels // LANES
    blocks = [
        (i, 0, source[at + i * pixels : at + (i + 1) * pixels, :].astype(F32)) for i in range(full)
    ]
    if channels % LANES:
        both = source[at + full * pixels : at + full * pixels + pixels // 2, :].astype(F32)
        low = lax.broadcasted_iota(jnp.int32, (1, LANES), 1) < LANES // 2
        blocks.append((full, 0, jnp.where(low, both, 0.0)))
        blocks.append((full, pixels // 2, jnp.where(low, pltpu.roll(both, LANES // 2, 1), 0.0)))
    return blocks


def group_scale(total, square, entries, group_width, channels):
    lanes = total.shape[1]
    lane = lax.broadcasted_iota(jnp.int32, (1, lanes), 1)
    spot = lane % group_width
    row = lax.broadcasted_iota(jnp.int32, (8, 1), 0)
    both = jnp.where(
        row == 0, jnp.sum(total, axis=0, keepdims=True), jnp.sum(square, axis=0, keepdims=True)
    )
    group = both
    for k in range(1, group_width):
        group = group + jnp.where(spot + k < group_width, pltpu.roll(both, lanes - k, 1), 0.0)
        group = group + jnp.where(spot >= k, pltpu.roll(both, k, 1), 0.0)
    group = group / entries
    average = group[0:1]
    scale = lax.rsqrt(group[1:2] - average * average + 1e-05)
    scale = jnp.where(lane < channels, 0.5 * scale, 0.0)
    return scale, -average * scale


def activate(source, targets, scale, shift, rows, columns, first, start, stop):
    middle, edge, pair = targets

    def body(i, before):
        row = first - 1 + i
        inside = ((row >= 0) & (row < rows)).astype(F32)
        at = pl.multiple_of(jnp.clip(row, 0, rows - 1) * columns, columns)
        u = source[pl.ds(at, columns), :] * (scale * inside) + shift * inside
        g = u + u * jnp.tanh(u)
        to = pl.ds(pl.multiple_of(i * columns, columns), columns)
        rest = g[:, WIDE:]
        middle[to, :] = g[:, :WIDE].astype(BF16)
        edge[to, :] = rest.astype(BF16)
        pair[to, :] = (before + pltpu.roll(rest, LANES // 2, 1)).astype(BF16)
        return rest

    lax.fori_loop(start, stop, body, jnp.zeros((columns, LANES), F32), unroll=stop - start)


def convolve(targets, kernel, start, count, columns):
    middle, edge, pair = targets
    top, mid, bottom = [
        pl.ds(pl.multiple_of(start + r * columns, columns), count) for r in range(3)
    ]
    window = jnp.concatenate(
        [middle[top, :], middle[mid, :], middle[bottom, :], pair[mid, :], edge[bottom, :]], axis=1
    )
    y = jnp.dot(window, kernel[...], preferred_element_type=F32)
    column = lax.broadcasted_iota(jnp.int32, (count, 1), 0) % columns

    def from_left(values):
        return jnp.where(column == 0, 0.0, pltpu.roll(values, 1, 0))

    def from_right(values):
        return jnp.where(column == columns - 1, 0.0, pltpu.roll(values, count - 1, 0))

    wide = y[:, WIDE : 2 * WIDE] + from_left(y[:, :WIDE]) + from_right(y[:, 2 * WIDE : 3 * WIDE])
    tail = y[:, 3 * WIDE : 3 * WIDE + LANES]
    return wide, from_left(tail) + from_right(y[:, 3 * WIDE + LANES :]), tail


def convolve_part(targets, kernel, start, columns, base, target):
    pixels = base.shape[0]
    wide, narrow, tail = convolve(targets, kernel, start, pixels, columns)
    for i in range(WIDE // LANES):
        lanes = slice(i * LANES, (i + 1) * LANES)
        target[i * pixels : (i + 1) * pixels, :] = (wide[:, lanes] + base[:, lanes]).astype(BF16)
    narrow = narrow + base[:, WIDE:]
    low = lax.broadcasted_iota(jnp.int32, (1, LANES), 1) < LANES // 2
    first, second = slice(0, pixels // 2), slice(pixels // 2, pixels)
    both = jnp.where(
        low,
        narrow[first] + pltpu.roll(tail[first], LANES // 2, 1),
        pltpu.roll(narrow[second], LANES // 2, 1) + tail[second],
    )
    target[WIDE // LANES * pixels :, :] = both.astype(BF16)


def spatial_kernel(rows, half, columns, channels, group_width, step, ways, order, sooner, *refs):
    shards = len(order)
    own, other = refs[:ways], refs[ways : 2 * ways]
    kernels, embeds = refs[2 * ways : 2 * ways + 2]
    outs = refs[2 * ways + 2 : 2 * ways + 2 + sooner]
    keep, *targets = refs[2 * ways + 2 + sooner : 2 * ways + 6 + sooner]
    field, hidden, *firsts = refs[2 * ways + 6 + sooner :]
    embed = embeds[step : step + 1, :]
    lanes = field.shape[1]
    own_rows = rows // half
    part = own_rows * columns // shards
    here = lax.axis_index("halo")
    spot = lax.axis_index("shard")
    own_base = here * (own_rows * columns)
    other_base = (1 - here) * (own_rows * columns)
    zero = jnp.zeros((8, lanes), F32)

    height = dense_rows(part, channels)
    for base, arrived in ((own_base, own), (other_base, other)):
        held = [(block, at) for block in arrived for at in range(0, block.shape[0], height)]
        for (block, at), d in zip(held, order):
            for i, first, values in unpack_part(block, at, part, channels):
                place = pl.multiple_of(base + (d if step == 0 else spot ^ d) * part + first, 8)
                field[pl.ds(place, values.shape[0]), i * LANES : (i + 1) * LANES] = values

    def sum_row(i, carry):
        total, square = carry
        chunk = field[pl.ds(pl.multiple_of(i * columns, columns), columns), :]
        chunk = chunk.reshape(columns // 8, 8, lanes)
        return total + jnp.sum(chunk, axis=0), square + jnp.sum(chunk * chunk, axis=0)

    total, square = lax.fori_loop(0, rows, sum_row, (zero, zero), unroll=4)
    entries = float(rows * columns * group_width)
    middle, edge, _ = firsts
    for pad in (0, (rows + 1) * columns):
        middle[pad : pad + columns, :] = jnp.zeros((columns, WIDE), BF16)
        edge[pad : pad + columns, :] = jnp.zeros((columns, LANES), BF16)
    scale, shift = group_scale(total, square, entries, group_width, channels)
    activate(field, firsts, scale, shift, rows, columns, 0, 1, rows + 1)

    low = lax.broadcasted_iota(jnp.int32, (1, LANES), 1) < channels - WIDE
    total, square = zero, zero
    count = min(WIDE, own_rows * columns)
    for start in range(0, rows * columns, count):
        wide, narrow, tail = convolve(firsts, kernels.at[0], start, count, columns)
        narrow = narrow + pltpu.roll(tail, LANES // 2, 1) + embed[:, WIDE:]
        chunk = jnp.concatenate([wide + embed[:, :WIDE], jnp.where(low, narrow, 0.0)], axis=1)
        hidden[start : start + count, :] = chunk
        chunk = chunk.reshape(count // 8, 8, lanes)
        total = total + jnp.sum(chunk, axis=0)
        square = square + jnp.sum(chunk * chunk, axis=0)
    scale, shift = group_scale(total, square, entries, group_width, channels)
    first_row = here * own_rows
    activate(hidden, targets, scale, shift, rows, columns, first_row, 0, own_rows + 2)
    for i, d in enumerate(order_out(shards)):
        start = (spot ^ d) * part
        base = field[pl.ds(pl.multiple_of(own_base + start, 8), part), :]
        if i < sooner:
            convolve_part(targets, kernels.at[1], start, columns, base, outs[i])
        else:
            keep[(i - sooner) * part : (i - sooner + 1) * part, :] = base


def finish_kernel(columns, shards, sooner, keep, middle, edge, pair, kernels, *outs):
    part = keep.shape[0] // (shards - sooner)
    spot = lax.axis_index("shard")
    for i, d in enumerate(order_out(shards)[sooner:]):
        start = (spot ^ d) * part
        base = keep[i * part : (i + 1) * part, :]
        convolve_part((middle, edge, pair), kernels.at[1], start, columns, base, outs[i])


def spatial(own, other, weights, embeds, step, rows, columns, half, shards):
    tokens = rows * columns
    part = tokens // half // shards
    channels = sum(block.size for block in own) // (tokens // half)
    ways = len(own)
    sooner = shards // 2
    later = shards - sooner
    lanes = round_up(channels, LANES)
    depth = weights.shape[1]
    piece = jax.ShapeDtypeStruct((dense_rows(part, channels), LANES), BF16)
    vmem = pl.BlockSpec(memory_space=pltpu.VMEM)
    params = pltpu.CompilerParams(vmem_limit_bytes=14 * 1024 * 1024)

    def active(rows_there):
        return [((rows_there + 2) * columns, width) for width in (WIDE, LANES, LANES)]

    *first, keep, middle, edge, pair = pl.pallas_call(
        functools.partial(
            spatial_kernel,
            rows,
            half,
            columns,
            channels,
            channels // GROUPS,
            step,
            ways,
            order_back(shards) if step else list(range(shards)),
            sooner,
        ),
        out_shape=[piece] * sooner
        + [jax.ShapeDtypeStruct((later * part, lanes), F32)]
        + [jax.ShapeDtypeStruct(shape, BF16) for shape in active(rows // half)],
        in_specs=[vmem] * (2 * ways + 2),
        out_specs=[vmem] * (sooner + 4),
        scratch_shapes=[
            pltpu.VMEM((tokens, lanes), F32),
            pltpu.VMEM((tokens, lanes), F32),
            *[pltpu.VMEM(shape, BF16) for shape in active(rows)],
        ],
        compiler_params=params,
        cost_estimate=pl.CostEstimate(
            flops=3 * tokens * depth * depth,
            bytes_accessed=6000000,
            transcendentals=tokens * lanes,
        ),
        name="spatial",
    )(*own, *other, weights, embeds)
    second = pl.pallas_call(
        functools.partial(finish_kernel, columns, shards, sooner),
        out_shape=[piece] * later,
        in_specs=[vmem] * 5,
        out_specs=[vmem] * later,
        compiler_params=params,
        cost_estimate=pl.CostEstimate(
            flops=2 * later * part * depth * depth, bytes_accessed=3000000, transcendentals=0
        ),
        name="finish",
    )(keep, middle, edge, pair, weights)
    return [*first, *second]


def prepare_kernel(channels, kernel1, kernel2, qkv, kernels, padded):
    spare = channels - WIDE
    for kernel, packed in ((kernel1, kernels.at[0]), (kernel2, kernels.at[1])):
        depth = packed.shape[0]
        packed[3 * channels :, :] = jnp.zeros((depth - 3 * channels, depth), BF16)
        for r in range(3):
            for source, target in (
                (slice(0, WIDE), slice(r * WIDE, (r + 1) * WIDE)),
                (slice(WIDE, channels), slice(3 * WIDE + r * spare, 3 * WIDE + (r + 1) * spare)),
            ):
                for s in range(3):
                    packed[target, s * WIDE : (s + 1) * WIDE] = kernel[r, s, source, :WIDE]
                first, second, third = [kernel[r, s, source, WIDE:] for s in range(3)]
                packed[target, 3 * WIDE : 3 * WIDE + LANES] = jnp.concatenate([first, second], axis=1)
                packed[target, 3 * WIDE + LANES :] = jnp.concatenate(
                    [third, jnp.zeros_like(third)], axis=1
                )
    lanes = padded.shape[1] // 3
    padded[...] = jnp.zeros(padded.shape, BF16)
    for i in range(3):
        padded[:, i * lanes : i * lanes + channels] = qkv[:, i * channels : (i + 1) * channels]


def prepare(conv_first, conv_second, qkv):
    channels = qkv.shape[0]
    depth = round_up(3 * channels, WIDE)
    lanes = round_up(channels, LANES)
    vmem = pl.BlockSpec(memory_space=pltpu.VMEM)
    return pl.pallas_call(
        functools.partial(prepare_kernel, channels),
        out_shape=[
            jax.ShapeDtypeStruct((2, depth, depth), BF16),
            jax.ShapeDtypeStruct((channels, 3 * lanes), BF16),
        ],
        in_specs=[vmem] * 3,
        out_specs=[vmem] * 2,
        compiler_params=pltpu.CompilerParams(vmem_limit_bytes=14 * 1024 * 1024),
        cost_estimate=pl.CostEstimate(flops=0, bytes_accessed=10000000, transcendentals=0),
        name="prepare",
    )(conv_first, conv_second, qkv)


def norm_rows(values):
    average = jnp.mean(values, axis=-1, keepdims=True)
    centred = values - average
    spread = jnp.mean(centred * centred, axis=-1, keepdims=True)
    return (centred * lax.rsqrt(spread + 1e-05)).astype(BF16)


def feed_forward(stream, geglu_in, geglu_out, active):
    inner = geglu_out.shape[1]
    normed = norm_rows(stream.astype(F32))
    for at in range(0, inner, WIDE):
        value = jnp.dot(normed, geglu_in[:, at : at + WIDE], preferred_element_type=F32)
        gate = jnp.dot(normed, geglu_in[:, inner + at : inner + at + WIDE], preferred_element_type=F32)
        act = value * (0.5 * gate) * (1.0 + lax.erf(gate * math.sqrt(0.5)))
        active[:, at : at + WIDE] = act.astype(BF16)
    update = lax.dot_general(
        active[...], geglu_out[...], (((1,), (1,)), ((), ())), preferred_element_type=F32
    )
    return stream.astype(F32) + update


def leave(values, target):
    pixels, channels = values.shape
    spare = round_up(channels, LANES) - channels
    values = jnp.concatenate([values, jnp.zeros((pixels, spare), F32)], axis=1)
    pack_part(values, target, 0, channels)


def feed_kernel(count, *refs):
    rest, geglu_in, geglu_out = refs[:3]
    outs = refs[3 : 3 + count]
    (active,) = refs[3 + count :]
    done = feed_forward(rest[...], geglu_in, geglu_out, active)
    pixels = done.shape[0] // count
    for i in range(count):
        leave(done[i * pixels : (i + 1) * pixels, :], outs[i])


def temporal_kernel(frames, ways, sooner, *refs):
    parts = refs[:ways]
    qkv, attn_out, geglu_in, geglu_out = refs[ways : ways + 4]
    outs = refs[ways + 4 : ways + 4 + sooner]
    rest = refs[ways + 4 + sooner]
    stream, projected, mixed, active = refs[ways + 5 + sooner :]
    channels = stream.shape[1]
    pixels = stream.shape[0] // frames
    lanes = projected.shape[1] // 3

    height = dense_rows(pixels, channels)
    held = [(block, at) for block in parts for at in range(0, block.shape[0], height)]
    for (block, at), d in zip(held, order_out(frames)):
        f = order_back(frames).index(d)
        for i, first, values in unpack_part(block, at, pixels, channels):
            rows = slice(f * pixels + first, f * pixels + first + values.shape[0])
            width = min(LANES, channels - i * LANES)
            stream[rows, i * LANES : i * LANES + width] = values[:, :width].astype(BF16)
    normed = norm_rows(stream[...].astype(F32))
    projected[...] = jnp.dot(normed, qkv[...], preferred_element_type=F32).astype(BF16)

    pack = min(pixels, WIDE // frames)
    tile = frames * pack
    same = (
        lax.broadcasted_iota(jnp.int32, (tile, tile), 0) % pack
        == lax.broadcasted_iota(jnp.int32, (tile, tile), 1) % pack
    )
    lane = lax.broadcasted_iota(jnp.int32, (1, LANES), 1)
    sharing = LANES // HEAD_DIM
    chosen = [(lane >= j * HEAD_DIM) & (lane < (j + 1) * HEAD_DIM) for j in range(sharing)]
    for first in range(0, pixels, pack):
        places = [slice(f * pixels + first, f * pixels + first + pack) for f in range(frames)]

        def gather(at):
            return jnp.concatenate([projected[p, at : at + LANES] for p in places])

        heads = [(h * HEAD_DIM // LANES * LANES, h % sharing) for h in range(channels // HEAD_DIM)]
        scores = [
            lax.dot_general(
                gather(at) * chosen[j].astype(BF16),
                gather(lanes + at),
                (((1,), (1,)), ((), ())),
                preferred_element_type=F32,
            )
            for at, j in heads
        ]
        scores = [jnp.where(same, score, float(jnp.finfo(F32).min)) for score in scores]
        tops = [jnp.max(score, axis=1, keepdims=True) for score in scores]
        powers = [
            jnp.exp((score - top) * HEAD_DIM ** (-0.5)) for score, top in zip(scores, tops)
        ]
        totals = [1.0 / jnp.sum(power, axis=1, keepdims=True) for power in powers]
        weights = [(power * total).astype(BF16) for power, total in zip(powers, totals)]
        results = [
            jnp.dot(weight, gather(2 * lanes + at), preferred_element_type=F32)
            for weight, (at, _) in zip(weights, heads)
        ]
        for at in range(0, channels, LANES):
            mix = None
            for result, (spot, j) in zip(results, heads):
                if spot == at:
                    mix = result if mix is None else jnp.where(chosen[j], result, mix)
            mix = mix.astype(BF16)
            for f, p in enumerate(places):
                mixed[p, at : at + LANES] = mix[f * pack : (f + 1) * pack]

    update = jnp.dot(mixed[:, :channels], attn_out[...], preferred_element_type=F32)
    after = (stream[...].astype(F32) + update).astype(BF16)
    rest[...] = after[sooner * pixels :, :]
    done = feed_forward(after[: sooner * pixels, :], geglu_in, geglu_out, active)
    for f in range(sooner):
        leave(done[f * pixels : (f + 1) * pixels, :], outs[f])


def temporal(parts, weights):
    ways = len(parts)
    frames = lax.axis_size("shard")
    sooner = frames // 2
    later = frames - sooner
    channels = weights[0].shape[0]
    pixels = sum(part.size for part in parts) // channels // frames
    lanes = round_up(channels, LANES)
    tokens = frames * pixels
    inner = weights[3].shape[1]
    vmem = pl.BlockSpec(memory_space=pltpu.VMEM)
    piece = jax.ShapeDtypeStruct((dense_rows(pixels, channels), LANES), BF16)
    feed_flops = 6 * pixels * channels * inner
    params = pltpu.CompilerParams(vmem_limit_bytes=14 * 1024 * 1024)
    *first, rest = pl.pallas_call(
        functools.partial(temporal_kernel, frames, ways, sooner),
        out_shape=[piece] * sooner + [jax.ShapeDtypeStruct((later * pixels, channels), BF16)],
        in_specs=[vmem] * (ways + 4),
        out_specs=[vmem] * (sooner + 1),
        scratch_shapes=[
            pltpu.VMEM((tokens, channels), BF16),
            pltpu.VMEM((tokens, 3 * lanes), BF16),
            pltpu.VMEM((tokens, lanes), BF16),
            pltpu.VMEM((sooner * pixels, inner), BF16),
        ],
        compiler_params=params,
        cost_estimate=pl.CostEstimate(
            flops=8 * tokens * channels * lanes + sooner * feed_flops,
            bytes_accessed=4000000,
            transcendentals=sooner * pixels * inner,
        ),
        name="temporal",
    )(*parts, *weights)
    second = pl.pallas_call(
        functools.partial(feed_kernel, later),
        out_shape=[piece] * later,
        in_specs=[vmem] * 3,
        out_specs=[vmem] * later,
        scratch_shapes=[pltpu.VMEM((later * pixels, inner), BF16)],
        compiler_params=params,
        cost_estimate=pl.CostEstimate(
            flops=later * feed_flops,
            bytes_accessed=3000000,
            transcendentals=later * pixels * inner,
        ),
        name="feed",
    )(rest, weights[2], weights[3])
    return [*first, *second]


def send(block, axis, distance):
    count = lax.axis_size(axis)
    return lax.ppermute(block, axis, [(i, (i + distance) % count) for i in range(count)])


def exchange(parts, order, across=0):
    shards, sections = lax.axis_size("shard"), lax.axis_size("section")
    arrived = []
    for part, d in zip(parts, order):
        if across:
            route = [
                (z * sections + s, (z ^ d) * sections + (s + across) % sections)
                for z in range(shards)
                for s in range(sections)
            ]
            part = lax.ppermute(part, ("shard", "section"), route)
        elif d:
            part = lax.ppermute(part, "shard", [(z, z ^ d) for z in range(shards)])
        arrived.append(part)
    return arrived


def join_kernel(*refs):
    *parts, whole = refs
    height = parts[0].shape[0]
    for i, part in enumerate(parts):
        whole[i * height : (i + 1) * height, :] = part[...]


def join(parts):
    vmem = pl.BlockSpec(memory_space=pltpu.VMEM)
    height, lanes = parts[0].shape
    return pl.pallas_call(
        join_kernel,
        out_shape=jax.ShapeDtypeStruct((len(parts) * height, lanes), parts[0].dtype),
        in_specs=[vmem] * len(parts),
        out_specs=vmem,
        compiler_params=pltpu.CompilerParams(vmem_limit_bytes=4 * 1024 * 1024),
        name="join",
    )(*parts)


def pack_kernel(shards, field, *outs):
    tokens, channels = field.shape
    pixels, full = tokens // shards, channels // LANES
    height = dense_rows(pixels, channels)
    for q in range(shards):
        out = outs[q * len(outs) // shards]
        at = q * height % out.shape[0]
        for i in range(full):
            block = field[q * pixels : (q + 1) * pixels, i * LANES : (i + 1) * LANES]
            out[at + i * pixels : at + (i + 1) * pixels, :] = block
        if channels % LANES:
            halves = [
                field[q * pixels + j : q * pixels + j + pixels // 2, full * LANES :]
                for j in (0, pixels // 2)
            ]
            out[at + full * pixels : at + height, :] = jnp.concatenate(halves, axis=1)


def pack(field, shards, ways):
    rows = dense_rows(*field.shape) // ways
    vmem = pl.BlockSpec(memory_space=pltpu.VMEM)
    return pl.pallas_call(
        functools.partial(pack_kernel, shards),
        out_shape=[jax.ShapeDtypeStruct((rows, LANES), BF16)] * ways,
        in_specs=[vmem],
        out_specs=[vmem] * ways,
        compiler_params=pltpu.CompilerParams(vmem_limit_bytes=4 * 1024 * 1024),
        name="pack",
    )(field)


def unpack_kernel(shards, *refs):
    parts, (whole,) = refs[:-1], refs[-1:]
    tokens, channels = whole.shape
    pixels = tokens // shards
    height = dense_rows(pixels, channels)
    held = [(block, at) for block in parts for at in range(0, block.shape[0], height)]
    spot = lax.axis_index("shard")
    for (block, at), d in zip(held, order_back(shards)):
        for i, first, values in unpack_part(block, at, pixels, channels):
            place = pl.multiple_of((spot ^ d) * pixels + first, 16)
            width = min(LANES, channels - i * LANES)
            lanes = slice(i * LANES, i * LANES + width)
            whole[pl.ds(place, values.shape[0]), lanes] = values[:, :width].astype(BF16)


def unpack(parts, shards, tokens, channels):
    vmem = pl.BlockSpec(memory_space=pltpu.VMEM)
    return pl.pallas_call(
        functools.partial(unpack_kernel, shards),
        out_shape=jax.ShapeDtypeStruct((tokens, channels), BF16),
        in_specs=[vmem] * len(parts),
        out_specs=vmem,
        compiler_params=pltpu.CompilerParams(vmem_limit_bytes=4 * 1024 * 1024),
        name="unpack",
    )(*parts)


def embed_time(stamps, time_weight):
    half_width = time_weight.shape[0] // 2
    frequency = jnp.exp(-math.log(10000.0) * jnp.arange(half_width, dtype=F32) / half_width)
    angles = stamps.astype(F32)[:, None] * frequency[None, :]
    sinusoid = jnp.concatenate([jnp.cos(angles), jnp.sin(angles)], axis=1)
    out = jnp.dot(jax.nn.silu(sinusoid).astype(BF16), time_weight, preferred_element_type=F32)
    return jnp.pad(out, ((0, 0), (0, round_up(out.shape[1], LANES) - out.shape[1])))


def per_device(
    features,
    timesteps,
    conv_first,
    conv_second,
    time_weight,
    qkv_weight,
    attn_out,
    geglu_in,
    geglu_out,
):
    _, _, own_rows, columns, channels = features.shape
    half = lax.axis_size("halo")
    rows = own_rows * half
    shards = lax.axis_size("shard")

    start = pack(features.reshape(own_rows * columns, channels), shards, 2)
    *early, moved = [send(block, "section", 1) for block in start]
    embeds = embed_time(timesteps[0], time_weight[0])
    spatial_weights, padded = prepare(conv_first[0], conv_second[0], qkv_weight[0])

    moved, spatial_weights, padded = lax.optimization_barrier((moved, spatial_weights, padded))
    own = [*early, moved]
    temporal_weights = (padded, attn_out[0], geglu_in[0], geglu_out[0].T)
    for denoise_step in range(STEPS):
        last = denoise_step == STEPS - 1
        parts = spatial(
            own,
            [send(block, "halo", 1) for block in own],
            spatial_weights,
            embeds,
            denoise_step,
            rows,
            columns,
            half,
            shards,
        )
        parts = exchange(parts, order_out(shards))
        parts = [join(parts[: shards // 2]), *parts[shards // 2 :]]
        parts = temporal(parts, temporal_weights)
        parts = exchange(parts, order_back(shards), across=0 if last else 1)
        own = [join(parts[: shards // 2]), *parts[shards // 2 :]]
    return unpack(own, shards, own_rows * columns, channels).reshape(features.shape)


def solution(mesh):
    return jax.shard_map(
        per_device,
        mesh=mesh,
        in_specs=(
            P(("groups", "section"), "shard", "halo", None, None),
            P(("groups", "section"), None),
            P("section", None, None, None, None),
            P("section", None, None, None, None),
            P("section", None, None),
            P("section", None, None),
            P("section", None, None),
            P("section", None, None),
            P("section", None, None),
        ),
        out_specs=P(("groups", "section"), "shard", "halo", None, None),
        check_vma=False,
    )
```

```python
import functools
import math

import jax
import jax.numpy as jnp
from jax import lax
from jax.experimental import pallas as pl
from jax.experimental.pallas import tpu as pltpu
from jax.sharding import PartitionSpec as P

HEAD_DIM = 64
GROUPS = 32
STEPS = 2
LANES = 128
WIDE = 256
F32 = jnp.float32
BF16 = jnp.bfloat16


def order_out(count, step):
    falling = list(reversed(range(count)))
    if step == 0:
        return falling
    return [d for d in falling if d % 2] + [d for d in falling if d % 2 == 0]


def order_back(count):
    return order_out(count, 1)


def round_up(value, unit):
    return -(-value // unit) * unit


def dense_rows(pixels, channels):
    return pixels * channels // LANES


def pack_part(values, target, at, channels):
    pixels, full = values.shape[0], channels // LANES
    for i in range(full):
        block = values[:, i * LANES : (i + 1) * LANES].astype(BF16)
        target[at + i * pixels : at + (i + 1) * pixels, :] = block
    if channels % LANES:
        rest = values[:, full * LANES :]
        first, second = rest[: pixels // 2], rest[pixels // 2 :]
        lane = lax.broadcasted_iota(jnp.int32, (1, LANES), 1)
        both = jnp.where(lane < LANES // 2, first, pltpu.roll(second, LANES // 2, 1))
        target[at + full * pixels : at + full * pixels + pixels // 2, :] = both.astype(BF16)


def unpack_part(source, at, pixels, channels):
    full = channels // LANES
    blocks = [
        (i, 0, source[at + i * pixels : at + (i + 1) * pixels, :].astype(F32)) for i in range(full)
    ]
    if channels % LANES:
        both = source[at + full * pixels : at + full * pixels + pixels // 2, :].astype(F32)
        low = lax.broadcasted_iota(jnp.int32, (1, LANES), 1) < LANES // 2
        blocks.append((full, 0, jnp.where(low, both, 0.0)))
        blocks.append((full, pixels // 2, jnp.where(low, pltpu.roll(both, LANES // 2, 1), 0.0)))
    return blocks


def group_scale(total, square, entries, group_width, channels):
    lanes = total.shape[1]
    lane = lax.broadcasted_iota(jnp.int32, (1, lanes), 1)
    spot = lane % group_width
    row = lax.broadcasted_iota(jnp.int32, (8, 1), 0)
    both = jnp.where(
        row == 0, jnp.sum(total, axis=0, keepdims=True), jnp.sum(square, axis=0, keepdims=True)
    )
    group = both
    for k in range(1, group_width):
        group = group + jnp.where(spot + k < group_width, pltpu.roll(both, lanes - k, 1), 0.0)
        group = group + jnp.where(spot >= k, pltpu.roll(both, k, 1), 0.0)
    group = group / entries
    average = group[0:1]
    scale = lax.rsqrt(group[1:2] - average * average + 1e-05)
    scale = jnp.where(lane < channels, 0.5 * scale, 0.0)
    return scale, -average * scale


def activate(source, targets, scale, shift, rows, columns, first, start, stop):
    middle, edge, pair = targets

    def body(i, before):
        row = first - 1 + i
        inside = ((row >= 0) & (row < rows)).astype(F32)
        at = pl.multiple_of(jnp.clip(row, 0, rows - 1) * columns, columns)
        u = source[pl.ds(at, columns), :] * (scale * inside) + shift * inside
        g = u + u * jnp.tanh(u)
        to = pl.ds(pl.multiple_of(i * columns, columns), columns)
        rest = g[:, WIDE:]
        middle[to, :] = g[:, :WIDE].astype(BF16)
        edge[to, :] = rest.astype(BF16)
        pair[to, :] = (before + pltpu.roll(rest, LANES // 2, 1)).astype(BF16)
        return rest

    lax.fori_loop(start, stop, body, jnp.zeros((columns, LANES), F32), unroll=stop - start)


def convolve(targets, kernel, start, count, columns):
    middle, edge, pair = targets
    top, mid, bottom = [
        pl.ds(pl.multiple_of(start + r * columns, columns), count) for r in range(3)
    ]
    window = jnp.concatenate(
        [middle[top, :], middle[mid, :], middle[bottom, :], pair[mid, :], edge[bottom, :]], axis=1
    )
    y = jnp.dot(window, kernel[...], preferred_element_type=F32)
    column = lax.broadcasted_iota(jnp.int32, (count, 1), 0) % columns

    def from_left(values):
        return jnp.where(column == 0, 0.0, pltpu.roll(values, 1, 0))

    def from_right(values):
        return jnp.where(column == columns - 1, 0.0, pltpu.roll(values, count - 1, 0))

    wide = y[:, WIDE : 2 * WIDE] + from_left(y[:, :WIDE]) + from_right(y[:, 2 * WIDE : 3 * WIDE])
    tail = y[:, 3 * WIDE : 3 * WIDE + LANES]
    return wide, from_left(tail) + from_right(y[:, 3 * WIDE + LANES :]), tail


def convolve_part(targets, kernel, start, columns, base, target):
    pixels = base.shape[0]
    wide, narrow, tail = convolve(targets, kernel, start, pixels, columns)
    for i in range(WIDE // LANES):
        lanes = slice(i * LANES, (i + 1) * LANES)
        target[i * pixels : (i + 1) * pixels, :] = (wide[:, lanes] + base[:, lanes]).astype(BF16)
    narrow = narrow + base[:, WIDE:]
    low = lax.broadcasted_iota(jnp.int32, (1, LANES), 1) < LANES // 2
    first, second = slice(0, pixels // 2), slice(pixels // 2, pixels)
    both = jnp.where(
        low,
        narrow[first] + pltpu.roll(tail[first], LANES // 2, 1),
        pltpu.roll(narrow[second], LANES // 2, 1) + tail[second],
    )
    target[WIDE // LANES * pixels :, :] = both.astype(BF16)


def spatial_kernel(rows, half, columns, channels, group_width, step, ways, order, sooner, *refs):
    shards = len(order)
    own, other = refs[:ways], refs[ways : 2 * ways]
    kernels, embeds = refs[2 * ways : 2 * ways + 2]
    outs = refs[2 * ways + 2 : 2 * ways + 2 + sooner]
    keep, *targets = refs[2 * ways + 2 + sooner : 2 * ways + 6 + sooner]
    field, hidden, *firsts = refs[2 * ways + 6 + sooner :]
    embed = embeds[step : step + 1, :]
    lanes = field.shape[1]
    own_rows = rows // half
    part = own_rows * columns // shards
    here = lax.axis_index("halo")
    spot = lax.axis_index("shard")
    own_base = here * (own_rows * columns)
    other_base = (1 - here) * (own_rows * columns)
    zero = jnp.zeros((8, lanes), F32)

    height = dense_rows(part, channels)
    for base, arrived in ((own_base, own), (other_base, other)):
        held = [(block, at) for block in arrived for at in range(0, block.shape[0], height)]
        for (block, at), d in zip(held, order):
            for i, first, values in unpack_part(block, at, part, channels):
                place = pl.multiple_of(base + (d if step == 0 else spot ^ d) * part + first, 8)
                field[pl.ds(place, values.shape[0]), i * LANES : (i + 1) * LANES] = values

    def sum_row(i, carry):
        total, square = carry
        chunk = field[pl.ds(pl.multiple_of(i * columns, columns), columns), :]
        chunk = chunk.reshape(columns // 8, 8, lanes)
        return total + jnp.sum(chunk, axis=0), square + jnp.sum(chunk * chunk, axis=0)

    total, square = lax.fori_loop(0, rows, sum_row, (zero, zero), unroll=4)
    entries = float(rows * columns * group_width)
    middle, edge, _ = firsts
    for pad in (0, (rows + 1) * columns):
        middle[pad : pad + columns, :] = jnp.zeros((columns, WIDE), BF16)
        edge[pad : pad + columns, :] = jnp.zeros((columns, LANES), BF16)
    scale, shift = group_scale(total, square, entries, group_width, channels)
    activate(field, firsts, scale, shift, rows, columns, 0, 1, rows + 1)

    low = lax.broadcasted_iota(jnp.int32, (1, LANES), 1) < channels - WIDE
    total, square = zero, zero
    count = min(WIDE, own_rows * columns)
    for start in range(0, rows * columns, count):
        wide, narrow, tail = convolve(firsts, kernels.at[0], start, count, columns)
        narrow = narrow + pltpu.roll(tail, LANES // 2, 1) + embed[:, WIDE:]
        chunk = jnp.concatenate([wide + embed[:, :WIDE], jnp.where(low, narrow, 0.0)], axis=1)
        hidden[start : start + count, :] = chunk
        chunk = chunk.reshape(count // 8, 8, lanes)
        total = total + jnp.sum(chunk, axis=0)
        square = square + jnp.sum(chunk * chunk, axis=0)
    scale, shift = group_scale(total, square, entries, group_width, channels)
    first_row = here * own_rows
    activate(hidden, targets, scale, shift, rows, columns, first_row, 0, own_rows + 2)
    for i, d in enumerate(order_out(shards, step)):
        start = (spot ^ d) * part
        base = field[pl.ds(pl.multiple_of(own_base + start, 8), part), :]
        if i < sooner:
            convolve_part(targets, kernels.at[1], start, columns, base, outs[i])
        else:
            keep[(i - sooner) * part : (i - sooner + 1) * part, :] = base


def finish_kernel(columns, shards, sooner, step, keep, middle, edge, pair, kernels, *outs):
    part = keep.shape[0] // (shards - sooner)
    spot = lax.axis_index("shard")
    for i, d in enumerate(order_out(shards, step)[sooner:]):
        start = (spot ^ d) * part
        base = keep[i * part : (i + 1) * part, :]
        convolve_part((middle, edge, pair), kernels.at[1], start, columns, base, outs[i])


def spatial(own, other, weights, embeds, step, rows, columns, half, shards):
    tokens = rows * columns
    part = tokens // half // shards
    channels = sum(block.size for block in own) // (tokens // half)
    ways = len(own)
    sooner = shards // 2
    later = shards - sooner
    lanes = round_up(channels, LANES)
    depth = weights.shape[1]
    piece = jax.ShapeDtypeStruct((dense_rows(part, channels), LANES), BF16)
    vmem = pl.BlockSpec(memory_space=pltpu.VMEM)
    params = pltpu.CompilerParams(vmem_limit_bytes=14 * 1024 * 1024)

    def active(rows_there):
        return [((rows_there + 2) * columns, width) for width in (WIDE, LANES, LANES)]

    *first, keep, middle, edge, pair = pl.pallas_call(
        functools.partial(
            spatial_kernel,
            rows,
            half,
            columns,
            channels,
            channels // GROUPS,
            step,
            ways,
            order_back(shards) if step else list(range(shards)),
            sooner,
        ),
        out_shape=[piece] * sooner
        + [jax.ShapeDtypeStruct((later * part, lanes), F32)]
        + [jax.ShapeDtypeStruct(shape, BF16) for shape in active(rows // half)],
        in_specs=[vmem] * (2 * ways + 2),
        out_specs=[vmem] * (sooner + 4),
        scratch_shapes=[
            pltpu.VMEM((tokens, lanes), F32),
            pltpu.VMEM((tokens, lanes), F32),
            *[pltpu.VMEM(shape, BF16) for shape in active(rows)],
        ],
        compiler_params=params,
        cost_estimate=pl.CostEstimate(
            flops=3 * tokens * depth * depth,
            bytes_accessed=6000000,
            transcendentals=tokens * lanes,
        ),
        name="spatial",
    )(*own, *other, weights, embeds)
    second = pl.pallas_call(
        functools.partial(finish_kernel, columns, shards, sooner, step),
        out_shape=[piece] * later,
        in_specs=[vmem] * 5,
        out_specs=[vmem] * later,
        compiler_params=params,
        cost_estimate=pl.CostEstimate(
            flops=2 * later * part * depth * depth, bytes_accessed=3000000, transcendentals=0
        ),
        name="finish",
    )(keep, middle, edge, pair, weights)
    return [*first, *second]


def prepare_kernel(channels, kernel1, kernel2, qkv, kernels, padded):
    spare = channels - WIDE
    for kernel, packed in ((kernel1, kernels.at[0]), (kernel2, kernels.at[1])):
        depth = packed.shape[0]
        packed[3 * channels :, :] = jnp.zeros((depth - 3 * channels, depth), BF16)
        for r in range(3):
            for source, target in (
                (slice(0, WIDE), slice(r * WIDE, (r + 1) * WIDE)),
                (slice(WIDE, channels), slice(3 * WIDE + r * spare, 3 * WIDE + (r + 1) * spare)),
            ):
                for s in range(3):
                    packed[target, s * WIDE : (s + 1) * WIDE] = kernel[r, s, source, :WIDE]
                first, second, third = [kernel[r, s, source, WIDE:] for s in range(3)]
                packed[target, 3 * WIDE : 3 * WIDE + LANES] = jnp.concatenate([first, second], axis=1)
                packed[target, 3 * WIDE + LANES :] = jnp.concatenate(
                    [third, jnp.zeros_like(third)], axis=1
                )
    lanes = padded.shape[1] // 3
    padded[...] = jnp.zeros(padded.shape, BF16)
    for i in range(3):
        padded[:, i * lanes : i * lanes + channels] = qkv[:, i * channels : (i + 1) * channels]


def prepare(conv_first, conv_second, qkv):
    channels = qkv.shape[0]
    depth = round_up(3 * channels, WIDE)
    lanes = round_up(channels, LANES)
    vmem = pl.BlockSpec(memory_space=pltpu.VMEM)
    return pl.pallas_call(
        functools.partial(prepare_kernel, channels),
        out_shape=[
            jax.ShapeDtypeStruct((2, depth, depth), BF16),
            jax.ShapeDtypeStruct((channels, 3 * lanes), BF16),
        ],
        in_specs=[vmem] * 3,
        out_specs=[vmem] * 2,
        compiler_params=pltpu.CompilerParams(vmem_limit_bytes=14 * 1024 * 1024),
        cost_estimate=pl.CostEstimate(flops=0, bytes_accessed=10000000, transcendentals=0),
        name="prepare",
    )(conv_first, conv_second, qkv)


def norm_rows(values):
    average = jnp.mean(values, axis=-1, keepdims=True)
    centred = values - average
    spread = jnp.mean(centred * centred, axis=-1, keepdims=True)
    return (centred * lax.rsqrt(spread + 1e-05)).astype(BF16)


def feed_forward(stream, geglu_in, geglu_out, active):
    inner = geglu_out.shape[1]
    normed = norm_rows(stream.astype(F32))
    for at in range(0, inner, WIDE):
        value = jnp.dot(normed, geglu_in[:, at : at + WIDE], preferred_element_type=F32)
        gate = jnp.dot(normed, geglu_in[:, inner + at : inner + at + WIDE], preferred_element_type=F32)
        act = value * (0.5 * gate) * (1.0 + lax.erf(gate * math.sqrt(0.5)))
        active[:, at : at + WIDE] = act.astype(BF16)
    update = lax.dot_general(
        active[...], geglu_out[...], (((1,), (1,)), ((), ())), preferred_element_type=F32
    )
    return stream.astype(F32) + update


def leave(values, target):
    pixels, channels = values.shape
    spare = round_up(channels, LANES) - channels
    values = jnp.concatenate([values, jnp.zeros((pixels, spare), F32)], axis=1)
    pack_part(values, target, 0, channels)


def feed_kernel(count, *refs):
    rest, geglu_in, geglu_out = refs[:3]
    outs = refs[3 : 3 + count]
    (active,) = refs[3 + count :]
    done = feed_forward(rest[...], geglu_in, geglu_out, active)
    pixels = done.shape[0] // count
    for i in range(count):
        leave(done[i * pixels : (i + 1) * pixels, :], outs[i])


def temporal_kernel(frames, ways, sooner, step, *refs):
    parts = refs[:ways]
    qkv, attn_out, geglu_in, geglu_out = refs[ways : ways + 4]
    outs = refs[ways + 4 : ways + 4 + sooner]
    rest = refs[ways + 4 + sooner]
    stream, projected, mixed, active = refs[ways + 5 + sooner :]
    channels = stream.shape[1]
    pixels = stream.shape[0] // frames
    lanes = projected.shape[1] // 3

    height = dense_rows(pixels, channels)
    held = [(block, at) for block in parts for at in range(0, block.shape[0], height)]
    for (block, at), d in zip(held, order_out(frames, step)):
        f = order_back(frames).index(d)
        for i, first, values in unpack_part(block, at, pixels, channels):
            rows = slice(f * pixels + first, f * pixels + first + values.shape[0])
            width = min(LANES, channels - i * LANES)
            stream[rows, i * LANES : i * LANES + width] = values[:, :width].astype(BF16)
    normed = norm_rows(stream[...].astype(F32))
    projected[...] = jnp.dot(normed, qkv[...], preferred_element_type=F32).astype(BF16)

    pack = min(pixels, WIDE // frames)
    tile = frames * pack
    same = (
        lax.broadcasted_iota(jnp.int32, (tile, tile), 0) % pack
        == lax.broadcasted_iota(jnp.int32, (tile, tile), 1) % pack
    )
    lane = lax.broadcasted_iota(jnp.int32, (1, LANES), 1)
    sharing = LANES // HEAD_DIM
    chosen = [(lane >= j * HEAD_DIM) & (lane < (j + 1) * HEAD_DIM) for j in range(sharing)]
    for first in range(0, pixels, pack):
        places = [slice(f * pixels + first, f * pixels + first + pack) for f in range(frames)]

        def gather(at):
            return jnp.concatenate([projected[p, at : at + LANES] for p in places])

        heads = [(h * HEAD_DIM // LANES * LANES, h % sharing) for h in range(channels // HEAD_DIM)]
        scores = [
            lax.dot_general(
                gather(at) * chosen[j].astype(BF16),
                gather(lanes + at),
                (((1,), (1,)), ((), ())),
                preferred_element_type=F32,
            )
            for at, j in heads
        ]
        scores = [jnp.where(same, score, float(jnp.finfo(F32).min)) for score in scores]
        tops = [jnp.max(score, axis=1, keepdims=True) for score in scores]
        powers = [
            jnp.exp((score - top) * HEAD_DIM ** (-0.5)) for score, top in zip(scores, tops)
        ]
        totals = [1.0 / jnp.sum(power, axis=1, keepdims=True) for power in powers]
        weights = [power.astype(BF16) for power in powers]
        results = [
            jnp.dot(weight, gather(2 * lanes + at), preferred_element_type=F32) * total
            for weight, total, (at, _) in zip(weights, totals, heads)
        ]
        for at in range(0, channels, LANES):
            mix = None
            for result, (spot, j) in zip(results, heads):
                if spot == at:
                    mix = result if mix is None else jnp.where(chosen[j], result, mix)
            mix = mix.astype(BF16)
            for f, p in enumerate(places):
                mixed[p, at : at + LANES] = mix[f * pack : (f + 1) * pack]

    update = jnp.dot(mixed[:, :channels], attn_out[...], preferred_element_type=F32)
    after = (stream[...].astype(F32) + update).astype(BF16)
    rest[...] = after[sooner * pixels :, :]
    done = feed_forward(after[: sooner * pixels, :], geglu_in, geglu_out, active)
    for f in range(sooner):
        leave(done[f * pixels : (f + 1) * pixels, :], outs[f])


def temporal(parts, weights, step):
    ways = len(parts)
    frames = lax.axis_size("shard")
    sooner = frames // 2
    later = frames - sooner
    channels = weights[0].shape[0]
    pixels = sum(part.size for part in parts) // channels // frames
    lanes = round_up(channels, LANES)
    tokens = frames * pixels
    inner = weights[3].shape[1]
    vmem = pl.BlockSpec(memory_space=pltpu.VMEM)
    piece = jax.ShapeDtypeStruct((dense_rows(pixels, channels), LANES), BF16)
    feed_flops = 6 * pixels * channels * inner
    params = pltpu.CompilerParams(vmem_limit_bytes=14 * 1024 * 1024)
    *first, rest = pl.pallas_call(
        functools.partial(temporal_kernel, frames, ways, sooner, step),
        out_shape=[piece] * sooner + [jax.ShapeDtypeStruct((later * pixels, channels), BF16)],
        in_specs=[vmem] * (ways + 4),
        out_specs=[vmem] * (sooner + 1),
        scratch_shapes=[
            pltpu.VMEM((tokens, channels), BF16),
            pltpu.VMEM((tokens, 3 * lanes), BF16),
            pltpu.VMEM((tokens, lanes), BF16),
            pltpu.VMEM((sooner * pixels, inner), BF16),
        ],
        compiler_params=params,
        cost_estimate=pl.CostEstimate(
            flops=8 * tokens * channels * lanes + sooner * feed_flops,
            bytes_accessed=4000000,
            transcendentals=sooner * pixels * inner,
        ),
        name="temporal",
    )(*parts, *weights)
    second = pl.pallas_call(
        functools.partial(feed_kernel, later),
        out_shape=[piece] * later,
        in_specs=[vmem] * 3,
        out_specs=[vmem] * later,
        scratch_shapes=[pltpu.VMEM((later * pixels, inner), BF16)],
        compiler_params=params,
        cost_estimate=pl.CostEstimate(
            flops=later * feed_flops,
            bytes_accessed=3000000,
            transcendentals=later * pixels * inner,
        ),
        name="feed",
    )(rest, weights[2], weights[3])
    return [*first, *second]


def send(block, axis, distance):
    count = lax.axis_size(axis)
    return lax.ppermute(block, axis, [(i, (i + distance) % count) for i in range(count)])


def exchange(parts, order, across=0):
    shards, sections = lax.axis_size("shard"), lax.axis_size("section")
    arrived = []
    for part, d in zip(parts, order):
        if across:
            route = [
                (z * sections + s, (z ^ d) * sections + (s + across) % sections)
                for z in range(shards)
                for s in range(sections)
            ]
            part = lax.ppermute(part, ("shard", "section"), route)
        elif d:
            part = lax.ppermute(part, "shard", [(z, z ^ d) for z in range(shards)])
        arrived.append(part)
    return arrived


def join_kernel(*refs):
    *parts, whole = refs
    height = parts[0].shape[0]
    for i, part in enumerate(parts):
        whole[i * height : (i + 1) * height, :] = part[...]


def join(parts):
    vmem = pl.BlockSpec(memory_space=pltpu.VMEM)
    height, lanes = parts[0].shape
    return pl.pallas_call(
        join_kernel,
        out_shape=jax.ShapeDtypeStruct((len(parts) * height, lanes), parts[0].dtype),
        in_specs=[vmem] * len(parts),
        out_specs=vmem,
        compiler_params=pltpu.CompilerParams(vmem_limit_bytes=4 * 1024 * 1024),
        name="join",
    )(*parts)


def pack_kernel(shards, field, *outs):
    tokens, channels = field.shape
    pixels, full = tokens // shards, channels // LANES
    height = dense_rows(pixels, channels)
    for q in range(shards):
        out = outs[q * len(outs) // shards]
        at = q * height % out.shape[0]
        for i in range(full):
            block = field[q * pixels : (q + 1) * pixels, i * LANES : (i + 1) * LANES]
            out[at + i * pixels : at + (i + 1) * pixels, :] = block
        if channels % LANES:
            halves = [
                field[q * pixels + j : q * pixels + j + pixels // 2, full * LANES :]
                for j in (0, pixels // 2)
            ]
            out[at + full * pixels : at + height, :] = jnp.concatenate(halves, axis=1)


def pack(field, shards, ways):
    rows = dense_rows(*field.shape) // ways
    vmem = pl.BlockSpec(memory_space=pltpu.VMEM)
    return pl.pallas_call(
        functools.partial(pack_kernel, shards),
        out_shape=[jax.ShapeDtypeStruct((rows, LANES), BF16)] * ways,
        in_specs=[vmem],
        out_specs=[vmem] * ways,
        compiler_params=pltpu.CompilerParams(vmem_limit_bytes=4 * 1024 * 1024),
        name="pack",
    )(field)


def unpack_kernel(shards, *refs):
    parts, (whole,) = refs[:-1], refs[-1:]
    tokens, channels = whole.shape
    pixels = tokens // shards
    height = dense_rows(pixels, channels)
    held = [(block, at) for block in parts for at in range(0, block.shape[0], height)]
    spot = lax.axis_index("shard")
    for (block, at), d in zip(held, order_back(shards)):
        for i, first, values in unpack_part(block, at, pixels, channels):
            place = pl.multiple_of((spot ^ d) * pixels + first, 16)
            width = min(LANES, channels - i * LANES)
            lanes = slice(i * LANES, i * LANES + width)
            whole[pl.ds(place, values.shape[0]), lanes] = values[:, :width].astype(BF16)


def unpack(parts, shards, tokens, channels):
    vmem = pl.BlockSpec(memory_space=pltpu.VMEM)
    return pl.pallas_call(
        functools.partial(unpack_kernel, shards),
        out_shape=jax.ShapeDtypeStruct((tokens, channels), BF16),
        in_specs=[vmem] * len(parts),
        out_specs=vmem,
        compiler_params=pltpu.CompilerParams(vmem_limit_bytes=4 * 1024 * 1024),
        name="unpack",
    )(*parts)


def embed_time(stamps, time_weight):
    half_width = time_weight.shape[0] // 2
    frequency = jnp.exp(-math.log(10000.0) * jnp.arange(half_width, dtype=F32) / half_width)
    angles = stamps.astype(F32)[:, None] * frequency[None, :]
    sinusoid = jnp.concatenate([jnp.cos(angles), jnp.sin(angles)], axis=1)
    out = jnp.dot(jax.nn.silu(sinusoid).astype(BF16), time_weight, preferred_element_type=F32)
    return jnp.pad(out, ((0, 0), (0, round_up(out.shape[1], LANES) - out.shape[1])))


def per_device(
    features,
    timesteps,
    conv_first,
    conv_second,
    time_weight,
    qkv_weight,
    attn_out,
    geglu_in,
    geglu_out,
):
    _, _, own_rows, columns, channels = features.shape
    half = lax.axis_size("halo")
    rows = own_rows * half
    shards = lax.axis_size("shard")

    start = pack(features.reshape(own_rows * columns, channels), shards, 2)
    *early, moved = [send(block, "section", 1) for block in start]
    embeds = embed_time(timesteps[0], time_weight[0])
    spatial_weights, padded = prepare(conv_first[0], conv_second[0], qkv_weight[0])

    moved, spatial_weights, padded = lax.optimization_barrier((moved, spatial_weights, padded))
    own = [*early, moved]
    temporal_weights = (padded, attn_out[0], geglu_in[0], geglu_out[0].T)
    for denoise_step in range(STEPS):
        last = denoise_step == STEPS - 1
        parts = spatial(
            own,
            [send(block, "halo", 1) for block in own],
            spatial_weights,
            embeds,
            denoise_step,
            rows,
            columns,
            half,
            shards,
        )
        parts = exchange(parts, order_out(shards, denoise_step))
        parts = [join(parts[: shards // 2]), *parts[shards // 2 :]]
        parts = temporal(parts, temporal_weights, denoise_step)
        parts = exchange(parts, order_back(shards), across=0 if last else 1)
        own = [join(parts[: shards // 2]), *parts[shards // 2 :]]
    return unpack(own, shards, own_rows * columns, channels).reshape(features.shape)


def solution(mesh):
    return jax.shard_map(
        per_device,
        mesh=mesh,
        in_specs=(
            P(("groups", "section"), "shard", "halo", None, None),
            P(("groups", "section"), None),
            P("section", None, None, None, None),
            P("section", None, None, None, None),
            P("section", None, None),
            P("section", None, None),
            P("section", None, None),
            P("section", None, None),
            P("section", None, None),
        ),
        out_specs=P(("groups", "section"), "shard", "halo", None, None),
        check_vma=False,
    )
```

```python
import functools
import math

import jax
import jax.numpy as jnp
from jax import lax
from jax.experimental import pallas as pl
from jax.experimental.pallas import tpu as pltpu
from jax.sharding import PartitionSpec as P

HEAD_DIM = 64
GROUPS = 32
STEPS = 2
LANES = 128
WIDE = 256
F32 = jnp.float32
BF16 = jnp.bfloat16


def order_out(count, step):
    falling = list(reversed(range(count)))
    if step == 0:
        return falling
    return [d for d in falling if d % 2] + [d for d in falling if d % 2 == 0]


def order_back(count):
    return order_out(count, 1)


def round_up(value, unit):
    return -(-value // unit) * unit


def dense_rows(pixels, channels):
    return pixels * channels // LANES


def pack_part(values, target, at, channels):
    pixels, full = values.shape[0], channels // LANES
    for i in range(full):
        block = values[:, i * LANES : (i + 1) * LANES].astype(BF16)
        target[at + i * pixels : at + (i + 1) * pixels, :] = block
    if channels % LANES:
        rest = values[:, full * LANES :]
        first, second = rest[: pixels // 2], rest[pixels // 2 :]
        lane = lax.broadcasted_iota(jnp.int32, (1, LANES), 1)
        both = jnp.where(lane < LANES // 2, first, pltpu.roll(second, LANES // 2, 1))
        target[at + full * pixels : at + full * pixels + pixels // 2, :] = both.astype(BF16)


def unpack_part(source, at, pixels, channels):
    full = channels // LANES
    blocks = [
        (i, 0, source[at + i * pixels : at + (i + 1) * pixels, :].astype(F32)) for i in range(full)
    ]
    if channels % LANES:
        both = source[at + full * pixels : at + full * pixels + pixels // 2, :].astype(F32)
        low = lax.broadcasted_iota(jnp.int32, (1, LANES), 1) < LANES // 2
        blocks.append((full, 0, jnp.where(low, both, 0.0)))
        blocks.append((full, pixels // 2, jnp.where(low, pltpu.roll(both, LANES // 2, 1), 0.0)))
    return blocks


def group_scale(total, square, entries, group_width, channels):
    lanes = total.shape[1]
    lane = lax.broadcasted_iota(jnp.int32, (1, lanes), 1)
    spot = lane % group_width
    row = lax.broadcasted_iota(jnp.int32, (8, 1), 0)
    both = jnp.where(
        row == 0, jnp.sum(total, axis=0, keepdims=True), jnp.sum(square, axis=0, keepdims=True)
    )
    group = both
    for k in range(1, group_width):
        group = group + jnp.where(spot + k < group_width, pltpu.roll(both, lanes - k, 1), 0.0)
        group = group + jnp.where(spot >= k, pltpu.roll(both, k, 1), 0.0)
    group = group / entries
    average = group[0:1]
    scale = lax.rsqrt(group[1:2] - average * average + 1e-05)
    scale = jnp.where(lane < channels, 0.5 * scale, 0.0)
    return scale, -average * scale


def activate(source, targets, scale, shift, rows, columns, first, start, stop):
    middle, edge, pair = targets

    def body(i, before):
        row = first - 1 + i
        inside = ((row >= 0) & (row < rows)).astype(F32)
        at = pl.multiple_of(jnp.clip(row, 0, rows - 1) * columns, columns)
        u = source[pl.ds(at, columns), :] * (scale * inside) + shift * inside
        g = u + u * jnp.tanh(u)
        to = pl.ds(pl.multiple_of(i * columns, columns), columns)
        rest = g[:, WIDE:]
        middle[to, :] = g[:, :WIDE].astype(BF16)
        edge[to, :] = rest.astype(BF16)
        pair[to, :] = (before + pltpu.roll(rest, LANES // 2, 1)).astype(BF16)
        return rest

    lax.fori_loop(start, stop, body, jnp.zeros((columns, LANES), F32), unroll=stop - start)


def convolve(targets, kernel, start, count, columns):
    middle, edge, pair = targets
    top, mid, bottom = [
        pl.ds(pl.multiple_of(start + r * columns, columns), count) for r in range(3)
    ]
    window = jnp.concatenate(
        [middle[top, :], middle[mid, :], middle[bottom, :], pair[mid, :], edge[bottom, :]], axis=1
    )
    y = jnp.dot(window, kernel[...], preferred_element_type=F32)
    column = lax.broadcasted_iota(jnp.int32, (count, 1), 0) % columns

    def from_left(values):
        return jnp.where(column == 0, 0.0, pltpu.roll(values, 1, 0))

    def from_right(values):
        return jnp.where(column == columns - 1, 0.0, pltpu.roll(values, count - 1, 0))

    wide = y[:, WIDE : 2 * WIDE] + from_left(y[:, :WIDE]) + from_right(y[:, 2 * WIDE : 3 * WIDE])
    tail = y[:, 3 * WIDE : 3 * WIDE + LANES]
    return wide, from_left(tail) + from_right(y[:, 3 * WIDE + LANES :]), tail


def convolve_part(targets, kernel, start, columns, base, target):
    pixels = base.shape[0]
    wide, narrow, tail = convolve(targets, kernel, start, pixels, columns)
    for i in range(WIDE // LANES):
        lanes = slice(i * LANES, (i + 1) * LANES)
        target[i * pixels : (i + 1) * pixels, :] = (wide[:, lanes] + base[:, lanes]).astype(BF16)
    narrow = narrow + base[:, WIDE:]
    low = lax.broadcasted_iota(jnp.int32, (1, LANES), 1) < LANES // 2
    first, second = slice(0, pixels // 2), slice(pixels // 2, pixels)
    both = jnp.where(
        low,
        narrow[first] + pltpu.roll(tail[first], LANES // 2, 1),
        pltpu.roll(narrow[second], LANES // 2, 1) + tail[second],
    )
    target[WIDE // LANES * pixels :, :] = both.astype(BF16)


def spatial_kernel(rows, half, columns, channels, group_width, step, ways, order, sooner, *refs):
    shards = len(order)
    own, other = refs[:ways], refs[ways : 2 * ways]
    kernels, embeds = refs[2 * ways : 2 * ways + 2]
    outs = refs[2 * ways + 2 : 2 * ways + 2 + sooner]
    keep, *targets = refs[2 * ways + 2 + sooner : 2 * ways + 6 + sooner]
    field, hidden, *firsts = refs[2 * ways + 6 + sooner :]
    embed = embeds[step : step + 1, :]
    lanes = field.shape[1]
    own_rows = rows // half
    part = own_rows * columns // shards
    here = lax.axis_index("halo")
    spot = lax.axis_index("shard")
    own_base = here * (own_rows * columns)
    other_base = (1 - here) * (own_rows * columns)
    zero = jnp.zeros((8, lanes), F32)

    height = dense_rows(part, channels)
    for base, arrived in ((own_base, own), (other_base, other)):
        held = [(block, at) for block in arrived for at in range(0, block.shape[0], height)]
        for (block, at), d in zip(held, order):
            for i, first, values in unpack_part(block, at, part, channels):
                place = pl.multiple_of(base + (d if step == 0 else spot ^ d) * part + first, 8)
                field[pl.ds(place, values.shape[0]), i * LANES : (i + 1) * LANES] = values

    def sum_row(i, carry):
        total, square = carry
        chunk = field[pl.ds(pl.multiple_of(i * columns, columns), columns), :]
        chunk = chunk.reshape(columns // 8, 8, lanes)
        return total + jnp.sum(chunk, axis=0), square + jnp.sum(chunk * chunk, axis=0)

    total, square = lax.fori_loop(0, rows, sum_row, (zero, zero), unroll=4)
    entries = float(rows * columns * group_width)
    middle, edge, _ = firsts
    for pad in (0, (rows + 1) * columns):
        middle[pad : pad + columns, :] = jnp.zeros((columns, WIDE), BF16)
        edge[pad : pad + columns, :] = jnp.zeros((columns, LANES), BF16)
    scale, shift = group_scale(total, square, entries, group_width, channels)
    activate(field, firsts, scale, shift, rows, columns, 0, 1, rows + 1)

    low = lax.broadcasted_iota(jnp.int32, (1, LANES), 1) < channels - WIDE
    total, square = zero, zero
    count = min(WIDE, own_rows * columns)
    for start in range(0, rows * columns, count):
        wide, narrow, tail = convolve(firsts, kernels.at[0], start, count, columns)
        narrow = narrow + pltpu.roll(tail, LANES // 2, 1) + embed[:, WIDE:]
        chunk = jnp.concatenate([wide + embed[:, :WIDE], jnp.where(low, narrow, 0.0)], axis=1)
        hidden[start : start + count, :] = chunk
        chunk = chunk.reshape(count // 8, 8, lanes)
        total = total + jnp.sum(chunk, axis=0)
        square = square + jnp.sum(chunk * chunk, axis=0)
    scale, shift = group_scale(total, square, entries, group_width, channels)
    first_row = here * own_rows
    activate(hidden, targets, scale, shift, rows, columns, first_row, 0, own_rows + 2)
    for i, d in enumerate(order_out(shards, step)):
        start = (spot ^ d) * part
        base = field[pl.ds(pl.multiple_of(own_base + start, 8), part), :]
        if i < sooner:
            convolve_part(targets, kernels.at[1], start, columns, base, outs[i])
        else:
            keep[(i - sooner) * part : (i - sooner + 1) * part, :] = base


def finish_kernel(columns, shards, sooner, step, keep, middle, edge, pair, kernels, *outs):
    part = keep.shape[0] // (shards - sooner)
    spot = lax.axis_index("shard")
    for i, d in enumerate(order_out(shards, step)[sooner:]):
        start = (spot ^ d) * part
        base = keep[i * part : (i + 1) * part, :]
        convolve_part((middle, edge, pair), kernels.at[1], start, columns, base, outs[i])


def spatial(own, other, weights, embeds, step, rows, columns, half, shards):
    tokens = rows * columns
    part = tokens // half // shards
    channels = sum(block.size for block in own) // (tokens // half)
    ways = len(own)
    sooner = shards // 2
    later = shards - sooner
    lanes = round_up(channels, LANES)
    depth = weights.shape[1]
    piece = jax.ShapeDtypeStruct((dense_rows(part, channels), LANES), BF16)
    vmem = pl.BlockSpec(memory_space=pltpu.VMEM)
    params = pltpu.CompilerParams(vmem_limit_bytes=14 * 1024 * 1024)

    def active(rows_there):
        return [((rows_there + 2) * columns, width) for width in (WIDE, LANES, LANES)]

    *first, keep, middle, edge, pair = pl.pallas_call(
        functools.partial(
            spatial_kernel,
            rows,
            half,
            columns,
            channels,
            channels // GROUPS,
            step,
            ways,
            order_back(shards) if step else list(range(shards)),
            sooner,
        ),
        out_shape=[piece] * sooner
        + [jax.ShapeDtypeStruct((later * part, lanes), F32)]
        + [jax.ShapeDtypeStruct(shape, BF16) for shape in active(rows // half)],
        in_specs=[vmem] * (2 * ways + 2),
        out_specs=[vmem] * (sooner + 4),
        scratch_shapes=[
            pltpu.VMEM((tokens, lanes), F32),
            pltpu.VMEM((tokens, lanes), F32),
            *[pltpu.VMEM(shape, BF16) for shape in active(rows)],
        ],
        compiler_params=params,
        cost_estimate=pl.CostEstimate(
            flops=3 * tokens * depth * depth,
            bytes_accessed=6000000,
            transcendentals=tokens * lanes,
        ),
        name="spatial",
    )(*own, *other, weights, embeds)
    second = pl.pallas_call(
        functools.partial(finish_kernel, columns, shards, sooner, step),
        out_shape=[piece] * later,
        in_specs=[vmem] * 5,
        out_specs=[vmem] * later,
        compiler_params=params,
        cost_estimate=pl.CostEstimate(
            flops=2 * later * part * depth * depth, bytes_accessed=3000000, transcendentals=0
        ),
        name="finish",
    )(keep, middle, edge, pair, weights)
    return [*first, *second]


def prepare_kernel(channels, kernel1, kernel2, qkv, kernels, padded):
    spare = channels - WIDE
    for kernel, packed in ((kernel1, kernels.at[0]), (kernel2, kernels.at[1])):
        depth = packed.shape[0]
        packed[3 * channels :, :] = jnp.zeros((depth - 3 * channels, depth), BF16)
        for r in range(3):
            for source, target in (
                (slice(0, WIDE), slice(r * WIDE, (r + 1) * WIDE)),
                (slice(WIDE, channels), slice(3 * WIDE + r * spare, 3 * WIDE + (r + 1) * spare)),
            ):
                for s in range(3):
                    packed[target, s * WIDE : (s + 1) * WIDE] = kernel[r, s, source, :WIDE]
                first, second, third = [kernel[r, s, source, WIDE:] for s in range(3)]
                packed[target, 3 * WIDE : 3 * WIDE + LANES] = jnp.concatenate([first, second], axis=1)
                packed[target, 3 * WIDE + LANES :] = jnp.concatenate(
                    [third, jnp.zeros_like(third)], axis=1
                )
    lanes = padded.shape[1] // 3
    padded[...] = jnp.zeros(padded.shape, BF16)
    for i in range(3):
        padded[:, i * lanes : i * lanes + channels] = qkv[:, i * channels : (i + 1) * channels]


def prepare(conv_first, conv_second, qkv):
    channels = qkv.shape[0]
    depth = round_up(3 * channels, WIDE)
    lanes = round_up(channels, LANES)
    vmem = pl.BlockSpec(memory_space=pltpu.VMEM)
    return pl.pallas_call(
        functools.partial(prepare_kernel, channels),
        out_shape=[
            jax.ShapeDtypeStruct((2, depth, depth), BF16),
            jax.ShapeDtypeStruct((channels, 3 * lanes), BF16),
        ],
        in_specs=[vmem] * 3,
        out_specs=[vmem] * 2,
        compiler_params=pltpu.CompilerParams(vmem_limit_bytes=14 * 1024 * 1024),
        cost_estimate=pl.CostEstimate(flops=0, bytes_accessed=10000000, transcendentals=0),
        name="prepare",
    )(conv_first, conv_second, qkv)


def norm_rows(values):
    average = jnp.mean(values, axis=-1, keepdims=True)
    centred = values - average
    spread = jnp.mean(centred * centred, axis=-1, keepdims=True)
    return (centred * lax.rsqrt(spread + 1e-05)).astype(BF16)


def feed_forward(stream, geglu_in, geglu_out, active):
    inner = geglu_out.shape[1]
    normed = norm_rows(stream.astype(F32))
    for at in range(0, inner, WIDE):
        value = jnp.dot(normed, geglu_in[:, at : at + WIDE], preferred_element_type=F32)
        gate = jnp.dot(normed, geglu_in[:, inner + at : inner + at + WIDE], preferred_element_type=F32)
        act = value * (0.5 * gate) * (1.0 + lax.erf(gate * math.sqrt(0.5)))
        active[:, at : at + WIDE] = act.astype(BF16)
    update = lax.dot_general(
        active[...], geglu_out[...], (((1,), (1,)), ((), ())), preferred_element_type=F32
    )
    return stream.astype(F32) + update


def leave(values, target):
    pixels, channels = values.shape
    spare = round_up(channels, LANES) - channels
    values = jnp.concatenate([values, jnp.zeros((pixels, spare), F32)], axis=1)
    pack_part(values, target, 0, channels)


def feed_kernel(count, *refs):
    rest, geglu_in, geglu_out = refs[:3]
    outs = refs[3 : 3 + count]
    (active,) = refs[3 + count :]
    done = feed_forward(rest[...], geglu_in, geglu_out, active)
    pixels = done.shape[0] // count
    for i in range(count):
        leave(done[i * pixels : (i + 1) * pixels, :], outs[i])


def temporal_kernel(frames, ways, sooner, step, *refs):
    parts = refs[:ways]
    qkv, attn_out, geglu_in, geglu_out = refs[ways : ways + 4]
    outs = refs[ways + 4 : ways + 4 + sooner]
    rest = refs[ways + 4 + sooner]
    stream, projected, mixed, active = refs[ways + 5 + sooner :]
    channels = stream.shape[1]
    pixels = stream.shape[0] // frames
    lanes = projected.shape[1] // 3

    height = dense_rows(pixels, channels)
    held = [(block, at) for block in parts for at in range(0, block.shape[0], height)]
    for (block, at), d in zip(held, order_out(frames, step)):
        f = order_back(frames).index(d)
        for i, first, values in unpack_part(block, at, pixels, channels):
            rows = slice(f * pixels + first, f * pixels + first + values.shape[0])
            width = min(LANES, channels - i * LANES)
            stream[rows, i * LANES : i * LANES + width] = values[:, :width].astype(BF16)
    normed = norm_rows(stream[...].astype(F32))
    projected[...] = jnp.dot(normed, qkv[...], preferred_element_type=F32).astype(BF16)

    pack = min(pixels, WIDE // frames)
    tile = frames * pack
    same = (
        lax.broadcasted_iota(jnp.int32, (tile, tile), 0) % pack
        == lax.broadcasted_iota(jnp.int32, (tile, tile), 1) % pack
    )
    lane = lax.broadcasted_iota(jnp.int32, (1, LANES), 1)
    sharing = LANES // HEAD_DIM
    chosen = [(lane >= j * HEAD_DIM) & (lane < (j + 1) * HEAD_DIM) for j in range(sharing)]
    for first in range(0, pixels, pack):
        places = [slice(f * pixels + first, f * pixels + first + pack) for f in range(frames)]

        def gather(at):
            return jnp.concatenate([projected[p, at : at + LANES] for p in places])

        heads = [(h * HEAD_DIM // LANES * LANES, h % sharing) for h in range(channels // HEAD_DIM)]
        scores = [
            lax.dot_general(
                gather(at) * chosen[j].astype(BF16),
                gather(lanes + at),
                (((1,), (1,)), ((), ())),
                preferred_element_type=F32,
            )
            for at, j in heads
        ]
        scores = [jnp.where(same, score, float(jnp.finfo(F32).min)) for score in scores]
        tops = [jnp.max(score, axis=1, keepdims=True) for score in scores]
        powers = [
            jnp.exp2((score - top) * (HEAD_DIM ** (-0.5) / math.log(2.0))) for score, top in zip(scores, tops)
        ]
        totals = [1.0 / jnp.sum(power, axis=1, keepdims=True) for power in powers]
        weights = [power.astype(BF16) for power in powers]
        results = [
            jnp.dot(weight, gather(2 * lanes + at), preferred_element_type=F32) * total
            for weight, total, (at, _) in zip(weights, totals, heads)
        ]
        for at in range(0, channels, LANES):
            mix = None
            for result, (spot, j) in zip(results, heads):
                if spot == at:
                    mix = result if mix is None else jnp.where(chosen[j], result, mix)
            mix = mix.astype(BF16)
            for f, p in enumerate(places):
                mixed[p, at : at + LANES] = mix[f * pack : (f + 1) * pack]

    update = jnp.dot(mixed[:, :channels], attn_out[...], preferred_element_type=F32)
    after = (stream[...].astype(F32) + update).astype(BF16)
    rest[...] = after[sooner * pixels :, :]
    done = feed_forward(after[: sooner * pixels, :], geglu_in, geglu_out, active)
    for f in range(sooner):
        leave(done[f * pixels : (f + 1) * pixels, :], outs[f])


def temporal(parts, weights, step):
    ways = len(parts)
    frames = lax.axis_size("shard")
    sooner = frames // 2
    later = frames - sooner
    channels = weights[0].shape[0]
    pixels = sum(part.size for part in parts) // channels // frames
    lanes = round_up(channels, LANES)
    tokens = frames * pixels
    inner = weights[3].shape[1]
    vmem = pl.BlockSpec(memory_space=pltpu.VMEM)
    piece = jax.ShapeDtypeStruct((dense_rows(pixels, channels), LANES), BF16)
    feed_flops = 6 * pixels * channels * inner
    params = pltpu.CompilerParams(vmem_limit_bytes=14 * 1024 * 1024)
    *first, rest = pl.pallas_call(
        functools.partial(temporal_kernel, frames, ways, sooner, step),
        out_shape=[piece] * sooner + [jax.ShapeDtypeStruct((later * pixels, channels), BF16)],
        in_specs=[vmem] * (ways + 4),
        out_specs=[vmem] * (sooner + 1),
        scratch_shapes=[
            pltpu.VMEM((tokens, channels), BF16),
            pltpu.VMEM((tokens, 3 * lanes), BF16),
            pltpu.VMEM((tokens, lanes), BF16),
            pltpu.VMEM((sooner * pixels, inner), BF16),
        ],
        compiler_params=params,
        cost_estimate=pl.CostEstimate(
            flops=8 * tokens * channels * lanes + sooner * feed_flops,
            bytes_accessed=4000000,
            transcendentals=sooner * pixels * inner,
        ),
        name="temporal",
    )(*parts, *weights)
    second = pl.pallas_call(
        functools.partial(feed_kernel, later),
        out_shape=[piece] * later,
        in_specs=[vmem] * 3,
        out_specs=[vmem] * later,
        scratch_shapes=[pltpu.VMEM((later * pixels, inner), BF16)],
        compiler_params=params,
        cost_estimate=pl.CostEstimate(
            flops=later * feed_flops,
            bytes_accessed=3000000,
            transcendentals=later * pixels * inner,
        ),
        name="feed",
    )(rest, weights[2], weights[3])
    return [*first, *second]


def send(block, axis, distance):
    count = lax.axis_size(axis)
    return lax.ppermute(block, axis, [(i, (i + distance) % count) for i in range(count)])


def exchange(parts, order, across=0):
    shards, sections = lax.axis_size("shard"), lax.axis_size("section")
    arrived = []
    for part, d in zip(parts, order):
        if across:
            route = [
                (z * sections + s, (z ^ d) * sections + (s + across) % sections)
                for z in range(shards)
                for s in range(sections)
            ]
            part = lax.ppermute(part, ("shard", "section"), route)
        elif d:
            part = lax.ppermute(part, "shard", [(z, z ^ d) for z in range(shards)])
        arrived.append(part)
    return arrived


def join_kernel(*refs):
    *parts, whole = refs
    height = parts[0].shape[0]
    for i, part in enumerate(parts):
        whole[i * height : (i + 1) * height, :] = part[...]


def join(parts):
    vmem = pl.BlockSpec(memory_space=pltpu.VMEM)
    height, lanes = parts[0].shape
    return pl.pallas_call(
        join_kernel,
        out_shape=jax.ShapeDtypeStruct((len(parts) * height, lanes), parts[0].dtype),
        in_specs=[vmem] * len(parts),
        out_specs=vmem,
        compiler_params=pltpu.CompilerParams(vmem_limit_bytes=4 * 1024 * 1024),
        name="join",
    )(*parts)


def pack_kernel(shards, field, *outs):
    tokens, channels = field.shape
    pixels, full = tokens // shards, channels // LANES
    height = dense_rows(pixels, channels)
    for q in range(shards):
        out = outs[q * len(outs) // shards]
        at = q * height % out.shape[0]
        for i in range(full):
            block = field[q * pixels : (q + 1) * pixels, i * LANES : (i + 1) * LANES]
            out[at + i * pixels : at + (i + 1) * pixels, :] = block
        if channels % LANES:
            halves = [
                field[q * pixels + j : q * pixels + j + pixels // 2, full * LANES :]
                for j in (0, pixels // 2)
            ]
            out[at + full * pixels : at + height, :] = jnp.concatenate(halves, axis=1)


def pack(field, shards, ways):
    rows = dense_rows(*field.shape) // ways
    vmem = pl.BlockSpec(memory_space=pltpu.VMEM)
    return pl.pallas_call(
        functools.partial(pack_kernel, shards),
        out_shape=[jax.ShapeDtypeStruct((rows, LANES), BF16)] * ways,
        in_specs=[vmem],
        out_specs=[vmem] * ways,
        compiler_params=pltpu.CompilerParams(vmem_limit_bytes=4 * 1024 * 1024),
        name="pack",
    )(field)


def unpack_kernel(shards, *refs):
    parts, (whole,) = refs[:-1], refs[-1:]
    tokens, channels = whole.shape
    pixels = tokens // shards
    height = dense_rows(pixels, channels)
    held = [(block, at) for block in parts for at in range(0, block.shape[0], height)]
    spot = lax.axis_index("shard")
    for (block, at), d in zip(held, order_back(shards)):
        for i, first, values in unpack_part(block, at, pixels, channels):
            place = pl.multiple_of((spot ^ d) * pixels + first, 16)
            width = min(LANES, channels - i * LANES)
            lanes = slice(i * LANES, i * LANES + width)
            whole[pl.ds(place, values.shape[0]), lanes] = values[:, :width].astype(BF16)


def unpack(parts, shards, tokens, channels):
    vmem = pl.BlockSpec(memory_space=pltpu.VMEM)
    return pl.pallas_call(
        functools.partial(unpack_kernel, shards),
        out_shape=jax.ShapeDtypeStruct((tokens, channels), BF16),
        in_specs=[vmem] * len(parts),
        out_specs=vmem,
        compiler_params=pltpu.CompilerParams(vmem_limit_bytes=4 * 1024 * 1024),
        name="unpack",
    )(*parts)


def embed_time(stamps, time_weight):
    half_width = time_weight.shape[0] // 2
    frequency = jnp.exp(-math.log(10000.0) * jnp.arange(half_width, dtype=F32) / half_width)
    angles = stamps.astype(F32)[:, None] * frequency[None, :]
    sinusoid = jnp.concatenate([jnp.cos(angles), jnp.sin(angles)], axis=1)
    out = jnp.dot(jax.nn.silu(sinusoid).astype(BF16), time_weight, preferred_element_type=F32)
    return jnp.pad(out, ((0, 0), (0, round_up(out.shape[1], LANES) - out.shape[1])))


def per_device(
    features,
    timesteps,
    conv_first,
    conv_second,
    time_weight,
    qkv_weight,
    attn_out,
    geglu_in,
    geglu_out,
):
    _, _, own_rows, columns, channels = features.shape
    half = lax.axis_size("halo")
    rows = own_rows * half
    shards = lax.axis_size("shard")

    start = pack(features.reshape(own_rows * columns, channels), shards, 2)
    *early, moved = [send(block, "section", 1) for block in start]
    embeds = embed_time(timesteps[0], time_weight[0])
    spatial_weights, padded = prepare(conv_first[0], conv_second[0], qkv_weight[0])

    moved, spatial_weights, padded = lax.optimization_barrier((moved, spatial_weights, padded))
    own = [*early, moved]
    temporal_weights = (padded, attn_out[0], geglu_in[0], geglu_out[0].T)
    for denoise_step in range(STEPS):
        last = denoise_step == STEPS - 1
        parts = spatial(
            own,
            [send(block, "halo", 1) for block in own],
            spatial_weights,
            embeds,
            denoise_step,
            rows,
            columns,
            half,
            shards,
        )
        parts = exchange(parts, order_out(shards, denoise_step))
        parts = [join(parts[: shards // 2]), *parts[shards // 2 :]]
        parts = temporal(parts, temporal_weights, denoise_step)
        parts = exchange(parts, order_back(shards), across=0 if last else 1)
        own = [join(parts[: shards // 2]), *parts[shards // 2 :]]
    return unpack(own, shards, own_rows * columns, channels).reshape(features.shape)


def solution(mesh):
    return jax.shard_map(
        per_device,
        mesh=mesh,
        in_specs=(
            P(("groups", "section"), "shard", "halo", None, None),
            P(("groups", "section"), None),
            P("section", None, None, None, None),
            P("section", None, None, None, None),
            P("section", None, None),
            P("section", None, None),
            P("section", None, None),
            P("section", None, None),
            P("section", None, None),
        ),
        out_specs=P(("groups", "section"), "shard", "halo", None, None),
        check_vma=False,
    )
```
